32 devices in a mesh: fibre: 2 (over y), chan: 4 (over z), win: 2 (over x), freq: 2 (over core).
Axes of the slice: x: 2, y: 2, z: 4, core: 2. Of those that a mesh axis runs over, the one named last changes fastest.
Arguments:
- spectra: bfloat16 [16, 2, 64, 2048], P('win', None, ('fibre', 'chan'), 'freq'), parts along dimension 2, may hold values from -50 to 50
- keep: int32 [32], P(('fibre', 'win')), parts along dimension 0, may hold values 0 or 1
- pair_mask: int32 [64, 4], P(('fibre', 'chan')), parts along dimension 0, may hold values 0 or 1
Outputs:
- correlations: float32 [64, 4, 8, 1024], P(('fibre', 'chan'), None, None, ('win', 'freq')), parts along dimension 0
The draws below stay inside these ranges and needn't reach their ends.
There are 2 independent parts, one for each index of `fibre`. The reference program is written for one: setup_inputs(seed, part) draws one part's arguments, and reference() takes and returns one part's arrays. A program takes and returns all parts, laid end to end along the dimension named above; each array names one. Nothing has to cross between parts.
All inputs are finite; a program needn't handle non-finite values. No bound on the sum of `keep` or of `pair_mask` on one device may be relied on, other than what follows from the above.
Results may differ from the reference program's by a relative error of at most 0.0014.
Values may be sent and summed in bfloat16 or wider, within the bound.
No kernel may reach another device: no remote copies, remote signals or barrier semaphores. Data moves between devices by JAX's collectives and lax.ppermute only.
A program may use at most 128 MiB of HBM per device.

```python
import math
import jax
import jax.numpy as jnp
from jax import lax

F = 2048
LAGS = 1024
F_LO = 60
NSAMP = 15000
CH_DEV = 8
CH = 32
W = 16
CYCLE = 3


def draw_spectra(key, part):
    base_key, scale_key = jax.random.split(jax.random.fold_in(key, 17))
    quarter = jnp.arange(F) * 4 // F
    base = jnp.clip(jax.random.normal(base_key, (W, 2, CH, F), jnp.float32), -5.0, 5.0)
    levels = jnp.exp(jax.random.uniform(scale_key, (W, 1, CH, 4), jnp.float32) * math.log(10.0))
    scales = levels[:, :, :, quarter]
    return (base * scales).astype(jnp.bfloat16)


def set_ends(array, rng, least, high):
    place = [jax.random.randint(jax.random.fold_in(rng, axis), (), 0, length) for axis, length in enumerate(array.shape)]
    longest = array.shape.index(max(array.shape))
    next_to = place[:longest] + [(place[longest] + 1) % array.shape[longest]] + place[longest + 1:]
    return array.at[tuple(place)].set(least).at[tuple(next_to)].set(high)


def setup_inputs(seed: int = 0, part: int = 0) -> dict:
    keys = jax.random.split(jax.random.key(seed), 4)
    part_splits = jax.random.split(jax.random.fold_in(keys[3], part), 4)
    return {
        "spectra": draw_spectra(jax.random.fold_in(jax.random.fold_in(keys[3], part), 71), part),
        "keep": set_ends((jax.random.randint(part_splits[1], (W,), 0, 4) < 3).astype(jnp.int32), jax.random.fold_in(part_splits[1], 1), 0, 1),
        "pair_mask": set_ends((jax.random.randint(part_splits[2], (CH, CYCLE + 1), 0, 5) < 4).astype(jnp.int32), jax.random.fold_in(part_splits[2], 1), 0, 1),
    }


EPS = 1e-06

def lag_table(start, count):
    bins = F_LO + start + jnp.arange(count, dtype=jnp.int32)
    offsets = jnp.arange(LAGS, dtype=jnp.int32) - LAGS // 2
    turns = jnp.remainder(bins[:, None] * offsets[None, :], NSAMP).astype(jnp.float32)
    angle = turns * (2.0 * math.pi / NSAMP)
    return jnp.concatenate([jnp.cos(angle), -jnp.sin(angle)], axis=0)

def reference(spectra, keep, pair_mask):
    spec = spectra.astype(jnp.float32)
    power = lax.optimization_barrier(jnp.sum(spec * spec, axis=(1, 3))) / F
    white = lax.optimization_barrier((spec * lax.rsqrt(power + EPS)[:, None, :, None]).astype(jnp.bfloat16))
    white = white.astype(jnp.float32)
    own = white * keep.astype(jnp.float32)[:, None, None, None]
    swapped = jnp.concatenate([own[:, 1:2], -own[:, 0:1]], axis=1)
    blocks = CH // CH_DEV
    padded = jnp.concatenate([white, jnp.zeros((W, 2, CYCLE * CH_DEV, F), jnp.float32)], axis=2)
    table = lag_table(0, F)
    own_blocks = own.reshape(W, 2, blocks, CH_DEV, F)
    swap_blocks = swapped.reshape(W, 2, blocks, CH_DEV, F)

    def one_offset(step):
        partner = lax.dynamic_slice_in_dim(padded, (step * CH_DEV).astype(jnp.int32), CH, 2)
        partner = partner.reshape(W, 2, blocks, CH_DEV, F)
        real_part = jnp.einsum('wcbif,wcbjf->bijf', own_blocks, partner)
        imag_part = jnp.einsum('wcbif,wcbjf->bijf', swap_blocks, partner)
        cross = jnp.concatenate([real_part, imag_part], axis=-1).reshape(CH * CH_DEV, 2 * F)
        lagsum = jnp.dot(cross, table, precision=lax.Precision.HIGHEST)
        return lagsum.reshape(CH, CH_DEV, LAGS)
    stacked = lax.map(one_offset, jnp.arange(CYCLE + 1, dtype=jnp.int32))
    lagsum = jnp.transpose(stacked, (1, 0, 2, 3))
    scale = 1.0 / math.sqrt(W * F)
    return lagsum * scale * pair_mask.astype(jnp.float32)[:, :, None, None]
```

```python
import functools
import math

import jax
import jax.numpy as jnp
import numpy as np
from jax import lax
from jax.experimental import pallas as pl
from jax.experimental.pallas import tpu as pltpu
from jax.sharding import PartitionSpec as P

LAGS = 1024
F_LO = 60
NSAMP = 15000
EPS = 1e-06
LANES = 128
FINE = 32
VMEM_LIMIT = 48 * 1024 * 1024


def from_behind(block, axis, distance):
    devices = range(lax.axis_size(axis))
    route = [(i - distance, i) for i in devices if i - distance in devices]
    return lax.ppermute(block, axis, route)


def phases(bins, lags):
    turns = np.remainder(np.asarray(bins, np.int64)[:, None] * np.asarray(lags, np.int64)[None, :], NSAMP)
    angle = turns * (2.0 * math.pi / NSAMP)
    return np.stack([np.cos(angle), np.sin(angle)]).astype(np.float32)


def split(value):
    high = value.astype(jnp.bfloat16)
    return high, (value - high.astype(jnp.float32)).astype(jnp.bfloat16)


def power_kernel(x_ref, out_ref):
    for w in range(x_ref.shape[0]):
        x = x_ref[w].astype(jnp.float32)
        x = x[0] * x[0] + x[1] * x[1]
        out_ref[w] = jnp.sum(x, axis=-1, keepdims=True)


def table_kernel(coarse_ref, fine_ref, high_ref, low_ref):
    f_dev = high_ref.shape[0] // 2
    fine_cos, fine_sin = fine_ref[0], fine_ref[1]

    def body(a, carry):
        cos_a = coarse_ref[0, pl.ds(a, 1), :]
        sin_a = coarse_ref[1, pl.ds(a, 1), :]
        rows = pl.multiple_of(a * FINE, FINE)
        high, low = split(cos_a * fine_cos - sin_a * fine_sin)
        high_ref[pl.ds(rows, FINE), :] = high
        low_ref[pl.ds(rows, FINE), :] = low
        high, low = split(-(cos_a * fine_sin + sin_a * fine_cos))
        high_ref[pl.ds(f_dev + rows, FINE), :] = high
        low_ref[pl.ds(f_dev + rows, FINE), :] = low
        return carry

    lax.fori_loop(0, f_dev // FINE, body, 0)


def whiten(x_ref, power_ref, n_bins, w, lanes):
    scale = lax.rsqrt(power_ref[w] / n_bins + EPS)
    parts = []
    for part in range(2):
        value = x_ref[w, part, :, lanes].astype(jnp.float32) * scale
        parts.append(value.astype(jnp.bfloat16).astype(jnp.float32))
    return parts


def correlate(own_ref, x_ref, power_ref, twiddle_ref, high_ref, low_ref, out_ref, rows_high, rows_low, n_bins):
    w_dev, _, ch, f_dev = own_ref.shape
    groups = twiddle_ref.shape[0] // 2

    def body(tile, carry):
        start = pl.multiple_of(tile * LANES, LANES)
        start_im = pl.multiple_of(f_dev + tile * LANES, LANES)
        lanes = pl.ds(start, LANES)
        lanes_im = pl.ds(start_im, LANES)
        real = [None] * ch
        imag = [None] * ch
        for w in range(w_dev):
            partner_re, partner_im = whiten(x_ref, power_ref, n_bins, w, lanes)
            for i in range(ch):
                own_re = own_ref[w, 0, pl.ds(i, 1), lanes]
                own_im = own_ref[w, 1, pl.ds(i, 1), lanes]
                re = own_re * partner_re + own_im * partner_im
                im = own_im * partner_re - own_re * partner_im
                real[i] = re if w == 0 else real[i] + re
                imag[i] = im if w == 0 else imag[i] + im
        for q in range(groups):
            cos_q = twiddle_ref[pl.ds(q, 1), lanes]
            sin_q = twiddle_ref[pl.ds(groups + q, 1), lanes]
            for i in range(0, ch, 2):
                rows = pl.ds((q * ch + i) * ch, 2 * ch)
                re = jnp.concatenate(real[i:i + 2], axis=0)
                im = jnp.concatenate(imag[i:i + 2], axis=0)
                high, low = split(re * cos_q - im * sin_q)
                rows_high[rows, lanes] = high
                rows_low[rows, lanes] = low
                high, low = split(re * sin_q + im * cos_q)
                rows_high[rows, lanes_im] = high
                rows_low[rows, lanes_im] = low
        return carry

    lax.fori_loop(0, f_dev // LANES, body, 0)
    dot = functools.partial(jnp.dot, preferred_element_type=jnp.float32)
    out_ref[...] = (dot(rows_high[...], high_ref[...])
                    + (dot(rows_low[...], high_ref[...]) + dot(rows_high[...], low_ref[...])))


def own_kernel(n_bins, keep_ref, x_ref, power_ref, twiddle_ref, high_ref, low_ref,
               own_ref, out_ref, rows_high, rows_low):
    for w in range(x_ref.shape[0]):
        parts = whiten(x_ref, power_ref, n_bins, w, slice(None))
        kept = keep_ref[w].astype(jnp.float32)
        for part in range(2):
            own_ref[w, part] = parts[part] * kept
    correlate(own_ref, x_ref, power_ref, twiddle_ref, high_ref, low_ref, out_ref, rows_high, rows_low, n_bins)


def partner_kernel(n_bins, own_ref, x_ref, power_ref, twiddle_ref, high_ref, low_ref, out_ref, rows_high, rows_low):
    correlate(own_ref, x_ref, power_ref, twiddle_ref, high_ref, low_ref, out_ref, rows_high, rows_low, n_bins)


def combine_kernel(scale, mask_ref, *refs):
    out_ref = refs[-1]
    ch, offsets = out_ref.shape[:2]
    start = 0
    for ref in refs[:-1]:
        for k in range(ref.shape[1]):
            total = ref[0, k]
            for p in range(1, ref.shape[0]):
                total = total + ref[p, k]
            for i in range(ch):
                factor = mask_ref[i, start + k].astype(jnp.float32) * scale
                out_ref[i, start + k] = total[i * ch:(i + 1) * ch] * factor
        start += ref.shape[1]


VMEM = pl.BlockSpec(memory_space=pltpu.VMEM)
SMEM = pl.BlockSpec(memory_space=pltpu.SMEM)


def local(spectra, keep, pair_mask):
    w_dev, _, ch, f_dev = spectra.shape
    reach = pair_mask.shape[1] - 1
    n_chan, n_win, n_freq = (lax.axis_size(a) for a in ("chan", "win", "freq"))
    groups = n_win * n_freq
    width = LAGS // groups
    n_bins = f_dev * n_freq
    params = pltpu.CompilerParams(vmem_limit_bytes=VMEM_LIMIT)
    chan = lax.axis_index("chan")
    freq = lax.axis_index("freq")

    blocks = [spectra]
    for step in range(reach):
        blocks.append(from_behind(blocks[-1], "chan", -1))

    power = pl.pallas_call(
        power_kernel,
        out_shape=jax.ShapeDtypeStruct((w_dev, ch, 1), jnp.float32),
        in_specs=[VMEM], out_specs=VMEM, compiler_params=params,
    )(spectra)
    slots = jnp.zeros((n_chan + reach, w_dev, ch), jnp.float32)
    slots = lax.dynamic_update_slice(slots, power.reshape(1, w_dev, ch), (chan, 0, 0))
    slots = lax.psum(slots, ("chan", "freq"))
    powers = lax.dynamic_slice(slots, (chan, 0, 0), (reach + 1, w_dev, ch))[..., None]

    coarse = phases(np.arange(0, n_bins, FINE), np.arange(width))
    coarse = coarse.reshape(2, n_freq, f_dev // FINE, width)
    coarse = lax.dynamic_index_in_dim(jnp.asarray(coarse), freq, 1, keepdims=False)
    fine = jnp.asarray(phases(F_LO + np.arange(FINE), np.arange(width)))
    high, low = pl.pallas_call(
        table_kernel,
        out_shape=[jax.ShapeDtypeStruct((2 * f_dev, width), jnp.bfloat16)] * 2,
        in_specs=[VMEM] * 2, out_specs=[VMEM] * 2, compiler_params=params,
    )(coarse, fine)
    twiddle = phases(F_LO + np.arange(n_bins), np.arange(groups) * width - LAGS // 2)
    twiddle = np.moveaxis(twiddle, 1, 2).reshape(2 * groups, n_freq, f_dev)
    twiddle = lax.dynamic_index_in_dim(jnp.asarray(twiddle), freq, 1, keepdims=False)

    rows = groups * ch * ch
    scratch = [pltpu.VMEM((rows, 2 * f_dev), jnp.bfloat16)] * 2
    sums = jax.ShapeDtypeStruct((rows, width), jnp.float32)
    cost = pl.CostEstimate(flops=6 * rows * 2 * f_dev * width, bytes_accessed=2 ** 22, transcendentals=0)
    own, first = pl.pallas_call(
        functools.partial(own_kernel, n_bins),
        out_shape=[jax.ShapeDtypeStruct(spectra.shape, jnp.float32), sums],
        in_specs=[SMEM] + [VMEM] * 5, out_specs=[VMEM] * 2,
        scratch_shapes=scratch, compiler_params=params, cost_estimate=cost,
    )(keep, spectra, powers[0], twiddle, high, low)
    parts = [first]
    for k in range(1, reach + 1):
        parts.append(pl.pallas_call(
            functools.partial(partner_kernel, n_bins),
            out_shape=sums,
            in_specs=[VMEM] * 6, out_specs=VMEM,
            scratch_shapes=scratch, compiler_params=params, cost_estimate=cost,
        )(own, blocks[k], powers[k], twiddle, high, low))

    received = []
    for part in parts:
        part = part.reshape(groups, 1, ch * ch, width)
        received.append(lax.all_to_all(part, ("win", "freq"), 0, 0, tiled=True))
    scale = 1.0 / math.sqrt(w_dev * n_win * n_bins)
    return pl.pallas_call(
        functools.partial(combine_kernel, scale),
        out_shape=jax.ShapeDtypeStruct((ch, reach + 1, ch, width), jnp.float32),
        in_specs=[SMEM] + [VMEM] * len(received), out_specs=VMEM, compiler_params=params,
    )(pair_mask, *received)


def solution(mesh):
    in_specs = (
        P("win", None, ("fibre", "chan"), "freq"),
        P(("fibre", "win")),
        P(("fibre", "chan"), None),
    )
    out_specs = P(("fibre", "chan"), None, None, ("win", "freq"))
    return jax.shard_map(local, mesh=mesh, in_specs=in_specs, out_specs=out_specs, check_vma=False)
```

```python
import functools
import math

import jax
import jax.numpy as jnp
import numpy as np
from jax import lax
from jax.experimental import pallas as pl
from jax.experimental.pallas import tpu as pltpu
from jax.sharding import PartitionSpec as P

LAGS = 1024
F_LO = 60
NSAMP = 15000
EPS = 1e-06
LANES = 128
FINE = 32
CHUNK = 512
VMEM_LIMIT = 48 * 1024 * 1024


def from_behind(block, axis, distance):
    devices = range(lax.axis_size(axis))
    route = [(i - distance, i) for i in devices if i - distance in devices]
    return lax.ppermute(block, axis, route)


def phases(bins, lags):
    turns = np.remainder(np.asarray(bins, np.int64)[:, None] * np.asarray(lags, np.int64)[None, :], NSAMP)
    angle = turns * (2.0 * math.pi / NSAMP)
    return np.stack([np.cos(angle), np.sin(angle)]).astype(np.float32)


def split(value):
    high = value.astype(jnp.bfloat16)
    return high, (value - high.astype(jnp.float32)).astype(jnp.bfloat16)


def power_kernel(x_ref, out_ref):
    for w in range(x_ref.shape[0]):
        x = x_ref[w].astype(jnp.float32)
        x = x[0] * x[0] + x[1] * x[1]
        out_ref[w] = jnp.sum(x, axis=-1, keepdims=True)


def table_kernel(coarse_ref, fine_ref, high_ref, low_ref):
    f_dev = high_ref.shape[0] // 2
    per_chunk = CHUNK // FINE
    fine_cos, fine_sin = fine_ref[0], fine_ref[1]

    def body(a, carry):
        cos_a = coarse_ref[0, pl.ds(a, 1), :]
        sin_a = coarse_ref[1, pl.ds(a, 1), :]
        rows = pl.multiple_of((a + a // per_chunk * per_chunk) * FINE, FINE)
        high, low = split(cos_a * fine_cos - sin_a * fine_sin)
        high_ref[pl.ds(rows, FINE), :] = high
        low_ref[pl.ds(rows, FINE), :] = low
        high, low = split(-(cos_a * fine_sin + sin_a * fine_cos))
        high_ref[pl.ds(CHUNK + rows, FINE), :] = high
        low_ref[pl.ds(CHUNK + rows, FINE), :] = low
        return carry

    lax.fori_loop(0, f_dev // FINE, body, 0)


def whiten_kernel(n_bins, x_ref, power_ref, out_ref):
    for w in range(x_ref.shape[0]):
        scale = lax.rsqrt(power_ref[w] / n_bins + EPS)
        for part in range(2):
            out_ref[w, part] = (x_ref[w, part].astype(jnp.float32) * scale).astype(jnp.bfloat16)


def cross_tile(own_ref, partner_ref, lanes):
    w_dev, _, ch, _ = own_ref.shape
    real = [None] * ch
    imag = [None] * ch
    for w in range(w_dev):
        partner_re = partner_ref[w, 0, :, lanes].astype(jnp.float32)
        partner_im = partner_ref[w, 1, :, lanes].astype(jnp.float32)
        for i in range(ch):
            own_re = own_ref[w, 0, i:i + 1, lanes]
            own_im = own_ref[w, 1, i:i + 1, lanes]
            re = own_re * partner_re + own_im * partner_im
            im = own_im * partner_re - own_re * partner_im
            real[i] = re if w == 0 else real[i] + re
            imag[i] = im if w == 0 else imag[i] + im
    return real, imag


def pairs_kernel(n_partners, keep_ref, base_ref, *refs):
    partner_refs = refs[:n_partners]
    twiddle_ref, high_ref, low_ref, out_ref, own_ref, rows_high, rows_low = refs[n_partners:]
    w_dev, _, ch, f_dev = base_ref.shape
    groups = out_ref.shape[0]
    width = out_ref.shape[-1]
    depth = 2 * CHUNK
    for w in range(w_dev):
        kept = keep_ref[w].astype(jnp.float32)
        for part in range(2):
            own_ref[w, part] = base_ref[w, part].astype(jnp.float32) * kept
    dot = functools.partial(jnp.dot, preferred_element_type=jnp.float32)
    for k, partner_ref in enumerate(partner_refs):
        total = None
        for chunk in range(f_dev // CHUNK):
            for tile in range(CHUNK // LANES):
                lanes = slice(chunk * CHUNK + tile * LANES, chunk * CHUNK + (tile + 1) * LANES)
                to_re = slice(tile * LANES, (tile + 1) * LANES)
                to_im = slice(CHUNK + tile * LANES, CHUNK + (tile + 1) * LANES)
                real, imag = cross_tile(own_ref, partner_ref, lanes)
                for q in range(groups):
                    cos_q = twiddle_ref[q:q + 1, lanes]
                    sin_q = twiddle_ref[groups + q:groups + q + 1, lanes]
                    for i in range(0, ch, 2):
                        rows = slice((q * ch + i) * ch, (q * ch + i + 2) * ch)
                        re = jnp.concatenate(real[i:i + 2], axis=0)
                        im = jnp.concatenate(imag[i:i + 2], axis=0)
                        high, low = split(re * cos_q - im * sin_q)
                        rows_high[k, chunk, rows, to_re] = high
                        rows_low[k, chunk, rows, to_re] = low
                        high, low = split(re * sin_q + im * cos_q)
                        rows_high[k, chunk, rows, to_im] = high
                        rows_low[k, chunk, rows, to_im] = low
            table = slice(chunk * depth, (chunk + 1) * depth)
            part = (dot(rows_high[k, chunk], high_ref[table])
                    + (dot(rows_low[k, chunk], high_ref[table]) + dot(rows_high[k, chunk], low_ref[table])))
            total = part if total is None else total + part
        out_ref[:, k] = total.reshape(groups, ch * ch, width)


def combine_kernel(scale, mask_ref, *refs):
    out_ref = refs[-1]
    ch, offsets = out_ref.shape[:2]
    start = 0
    for ref in refs[:-1]:
        for k in range(ref.shape[1]):
            total = ref[0, k]
            for p in range(1, ref.shape[0]):
                total = total + ref[p, k]
            for i in range(ch):
                factor = mask_ref[i, start + k].astype(jnp.float32) * scale
                out_ref[i, start + k] = total[i * ch:(i + 1) * ch] * factor
        start += ref.shape[1]


VMEM = pl.BlockSpec(memory_space=pltpu.VMEM)
SMEM = pl.BlockSpec(memory_space=pltpu.SMEM)


def local(spectra, keep, pair_mask):
    w_dev, _, ch, f_dev = spectra.shape
    reach = pair_mask.shape[1] - 1
    n_win, n_freq = (lax.axis_size(a) for a in ("win", "freq"))
    groups = n_win * n_freq
    width = LAGS // groups
    n_bins = f_dev * n_freq
    params = pltpu.CompilerParams(vmem_limit_bytes=VMEM_LIMIT)
    freq = lax.axis_index("freq")

    power = pl.pallas_call(
        power_kernel,
        out_shape=jax.ShapeDtypeStruct((w_dev, ch, 1), jnp.float32),
        in_specs=[VMEM], out_specs=VMEM, compiler_params=params,
    )(spectra)
    power = lax.psum(power, "freq")
    white = pl.pallas_call(
        functools.partial(whiten_kernel, n_bins),
        out_shape=jax.ShapeDtypeStruct(spectra.shape, jnp.bfloat16),
        in_specs=[VMEM] * 2, out_specs=VMEM, compiler_params=params,
    )(spectra, power)
    blocks = [white]
    for step in range(reach):
        blocks.append(from_behind(blocks[-1], "chan", -1))

    coarse = phases(np.arange(0, n_bins, FINE), np.arange(width))
    coarse = coarse.reshape(2, n_freq, f_dev // FINE, width)
    coarse = lax.dynamic_index_in_dim(jnp.asarray(coarse), freq, 1, keepdims=False)
    fine = jnp.asarray(phases(F_LO + np.arange(FINE), np.arange(width)))
    high, low = pl.pallas_call(
        table_kernel,
        out_shape=[jax.ShapeDtypeStruct((2 * f_dev, width), jnp.bfloat16)] * 2,
        in_specs=[VMEM] * 2, out_specs=[VMEM] * 2, compiler_params=params,
    )(coarse, fine)
    twiddle = phases(F_LO + np.arange(n_bins), np.arange(groups) * width - LAGS // 2)
    twiddle = np.moveaxis(twiddle, 1, 2).reshape(2 * groups, n_freq, f_dev)
    twiddle = lax.dynamic_index_in_dim(jnp.asarray(twiddle), freq, 1, keepdims=False)

    rows = groups * ch * ch
    depth = 2 * CHUNK

    def pairs(base, partners):
        n = len(partners)
        flops = n * 6 * rows * 2 * f_dev * width
        return pl.pallas_call(
            functools.partial(pairs_kernel, n),
            out_shape=jax.ShapeDtypeStruct((groups, n, ch * ch, width), jnp.float32),
            in_specs=[SMEM] + [VMEM] * (n + 4), out_specs=VMEM,
            scratch_shapes=[pltpu.VMEM(base.shape, jnp.float32)]
            + [pltpu.VMEM((n, f_dev // CHUNK, rows, depth), jnp.bfloat16)] * 2,
            compiler_params=params,
            cost_estimate=pl.CostEstimate(flops=flops, bytes_accessed=2 ** 22, transcendentals=0),
        )(keep, base, *partners, twiddle, high, low)

    parts = [pairs(white, blocks[:2])] + [pairs(white, [block]) for block in blocks[2:]]

    received = []
    for part in parts:
        received.append(lax.all_to_all(part, ("win", "freq"), 0, 0, tiled=True))
    scale = 1.0 / math.sqrt(w_dev * n_win * n_bins)
    return pl.pallas_call(
        functools.partial(combine_kernel, scale),
        out_shape=jax.ShapeDtypeStruct((ch, reach + 1, ch, width), jnp.float32),
        in_specs=[SMEM] + [VMEM] * len(received), out_specs=VMEM, compiler_params=params,
    )(pair_mask, *received)


def solution(mesh):
    in_specs = (
        P("win", None, ("fibre", "chan"), "freq"),
        P(("fibre", "win")),
        P(("fibre", "chan"), None),
    )
    out_specs = P(("fibre", "chan"), None, None, ("win", "freq"))
    return jax.shard_map(local, mesh=mesh, in_specs=in_specs, out_specs=out_specs, check_vma=False)
```

```python
import functools
import math

import jax
import jax.numpy as jnp
import numpy as np
from jax import lax
from jax.experimental import pallas as pl
from jax.experimental.pallas import tpu as pltpu
from jax.sharding import PartitionSpec as P

LAGS = 1024
F_LO = 60
NSAMP = 15000
EPS = 1e-06
LANES = 128
FINE = 32
CHUNK = 512
VMEM_LIMIT = 48 * 1024 * 1024


def from_behind(block, axis, distance):
    devices = range(lax.axis_size(axis))
    route = [(i - distance, i) for i in devices if i - distance in devices]
    return lax.ppermute(block, axis, route)


def phases(bins, lags):
    turns = np.remainder(np.asarray(bins, np.int64)[:, None] * np.asarray(lags, np.int64)[None, :], NSAMP)
    angle = turns * (2.0 * math.pi / NSAMP)
    return np.stack([np.cos(angle), np.sin(angle)]).astype(np.float32)


def split(value):
    high = value.astype(jnp.bfloat16)
    return high, (value - high.astype(jnp.float32)).astype(jnp.bfloat16)


def power_kernel(x_ref, out_ref):
    for w in range(x_ref.shape[0]):
        x = x_ref[w].astype(jnp.float32)
        x = x[0] * x[0] + x[1] * x[1]
        out_ref[w] = jnp.sum(x, axis=-1, keepdims=True)


def table_kernel(coarse_ref, fine_ref, high_ref, low_ref):
    f_dev = high_ref.shape[0] // 2
    per_chunk = CHUNK // FINE
    fine_cos, fine_sin = fine_ref[0], fine_ref[1]

    def body(a, carry):
        cos_a = coarse_ref[0, pl.ds(a, 1), :]
        sin_a = coarse_ref[1, pl.ds(a, 1), :]
        rows = pl.multiple_of((a + a // per_chunk * per_chunk) * FINE, FINE)
        high, low = split(cos_a * fine_cos - sin_a * fine_sin)
        high_ref[pl.ds(rows, FINE), :] = high
        low_ref[pl.ds(rows, FINE), :] = low
        high, low = split(-(cos_a * fine_sin + sin_a * fine_cos))
        high_ref[pl.ds(CHUNK + rows, FINE), :] = high
        low_ref[pl.ds(CHUNK + rows, FINE), :] = low
        return carry

    lax.fori_loop(0, f_dev // FINE, body, 0)


def whiten_kernel(n_bins, x_ref, power_ref, out_ref):
    for w in range(x_ref.shape[0]):
        scale = lax.rsqrt(power_ref[w] / n_bins + EPS)
        for part in range(2):
            out_ref[w, part] = (x_ref[w, part].astype(jnp.float32) * scale).astype(jnp.bfloat16)


def cross_tile(own_ref, partner_ref, lanes):
    w_dev, _, ch, _ = own_ref.shape
    real = [None] * ch
    imag = [None] * ch
    for w in range(w_dev):
        partner_re = partner_ref[w, 0, :, lanes].astype(jnp.float32)
        partner_im = partner_ref[w, 1, :, lanes].astype(jnp.float32)
        for i in range(ch):
            own_re = own_ref[w, 0, i:i + 1, lanes]
            own_im = own_ref[w, 1, i:i + 1, lanes]
            re = own_re * partner_re + own_im * partner_im
            im = own_im * partner_re - own_re * partner_im
            real[i] = re if w == 0 else real[i] + re
            imag[i] = im if w == 0 else imag[i] + im
    return real, imag


def pairs_kernel(n_partners, keep_ref, base_ref, *refs):
    partner_refs = refs[:n_partners]
    twiddle_ref, high_ref, low_ref, out_ref, own_ref, rows_high, rows_low = refs[n_partners:]
    w_dev, _, ch, f_dev = base_ref.shape
    groups = out_ref.shape[0]
    width = out_ref.shape[-1]
    depth = 2 * CHUNK
    for w in range(w_dev):
        kept = keep_ref[w].astype(jnp.float32)
        for part in range(2):
            own_ref[w, part] = base_ref[w, part].astype(jnp.float32) * kept
    dot = functools.partial(jnp.dot, preferred_element_type=jnp.float32)
    for k, partner_ref in enumerate(partner_refs):
        total = None
        for chunk in range(f_dev // CHUNK):
            for tile in range(CHUNK // LANES):
                lanes = slice(chunk * CHUNK + tile * LANES, chunk * CHUNK + (tile + 1) * LANES)
                to_re = slice(tile * LANES, (tile + 1) * LANES)
                to_im = slice(CHUNK + tile * LANES, CHUNK + (tile + 1) * LANES)
                real, imag = cross_tile(own_ref, partner_ref, lanes)
                for q in range(groups):
                    cos_q = twiddle_ref[q:q + 1, lanes]
                    sin_q = twiddle_ref[groups + q:groups + q + 1, lanes]
                    for i in range(0, ch, 2):
                        rows = slice((q * ch + i) * ch, (q * ch + i + 2) * ch)
                        re = jnp.concatenate(real[i:i + 2], axis=0)
                        im = jnp.concatenate(imag[i:i + 2], axis=0)
                        high, low = split(re * cos_q - im * sin_q)
                        rows_high[k, chunk, rows, to_re] = high
                        rows_low[k, chunk, rows, to_re] = low
                        high, low = split(re * sin_q + im * cos_q)
                        rows_high[k, chunk, rows, to_im] = high
                        rows_low[k, chunk, rows, to_im] = low
            table = slice(chunk * depth, (chunk + 1) * depth)
            part = (dot(rows_high[k, chunk], high_ref[table])
                    + (dot(rows_low[k, chunk], high_ref[table]) + dot(rows_high[k, chunk], low_ref[table])))
            total = part if total is None else total + part
        out_ref[:, k] = total.reshape(groups, ch * ch, width)


def combine_kernel(scale, order, mask_ref, *refs):
    out_ref = refs[-1]
    ch = out_ref.shape[0]
    places = [(ref, n) for ref in refs[:-1] for n in range(ref.shape[1])]
    for k, (ref, n) in zip(order, places):
        total = ref[0, n]
        for p in range(1, ref.shape[0]):
            total = total + ref[p, n]
        for i in range(ch):
            factor = mask_ref[i, k].astype(jnp.float32) * scale
            out_ref[i, k] = total[i * ch:(i + 1) * ch] * factor


VMEM = pl.BlockSpec(memory_space=pltpu.VMEM)
SMEM = pl.BlockSpec(memory_space=pltpu.SMEM)


def local(spectra, keep, pair_mask):
    w_dev, _, ch, f_dev = spectra.shape
    reach = pair_mask.shape[1] - 1
    n_win, n_freq = (lax.axis_size(a) for a in ("win", "freq"))
    groups = n_win * n_freq
    width = LAGS // groups
    n_bins = f_dev * n_freq
    params = pltpu.CompilerParams(vmem_limit_bytes=VMEM_LIMIT)
    freq = lax.axis_index("freq")

    def whiten(block, power):
        return pl.pallas_call(
            functools.partial(whiten_kernel, n_bins),
            out_shape=jax.ShapeDtypeStruct(block.shape, jnp.bfloat16),
            in_specs=[VMEM] * 2, out_specs=VMEM, compiler_params=params,
        )(block, power)

    far = from_behind(spectra, "chan", -reach)
    power = pl.pallas_call(
        power_kernel,
        out_shape=jax.ShapeDtypeStruct((w_dev, ch, 1), jnp.float32),
        in_specs=[VMEM], out_specs=VMEM, compiler_params=params,
    )(spectra)
    power = lax.psum(power, "freq")
    white = whiten(spectra, power)
    far_power = from_behind(power, "chan", -reach)
    near = {k: from_behind(white, "chan", -k) for k in range(reach - 1, 0, -1)}

    coarse = phases(np.arange(0, n_bins, FINE), np.arange(width))
    coarse = coarse.reshape(2, n_freq, f_dev // FINE, width)
    coarse = lax.dynamic_index_in_dim(jnp.asarray(coarse), freq, 1, keepdims=False)
    fine = jnp.asarray(phases(F_LO + np.arange(FINE), np.arange(width)))
    high, low = pl.pallas_call(
        table_kernel,
        out_shape=[jax.ShapeDtypeStruct((2 * f_dev, width), jnp.bfloat16)] * 2,
        in_specs=[VMEM] * 2, out_specs=[VMEM] * 2, compiler_params=params,
    )(coarse, fine)
    twiddle = phases(F_LO + np.arange(n_bins), np.arange(groups) * width - LAGS // 2)
    twiddle = np.moveaxis(twiddle, 1, 2).reshape(2 * groups, n_freq, f_dev)
    twiddle = lax.dynamic_index_in_dim(jnp.asarray(twiddle), freq, 1, keepdims=False)

    rows = groups * ch * ch
    depth = 2 * CHUNK

    def pairs(base, partners):
        n = len(partners)
        flops = n * 6 * rows * 2 * f_dev * width
        return pl.pallas_call(
            functools.partial(pairs_kernel, n),
            out_shape=jax.ShapeDtypeStruct((groups, n, ch * ch, width), jnp.float32),
            in_specs=[SMEM] + [VMEM] * (n + 4), out_specs=VMEM,
            scratch_shapes=[pltpu.VMEM(base.shape, jnp.float32)]
            + [pltpu.VMEM((n, f_dev // CHUNK, rows, depth), jnp.bfloat16)] * 2,
            compiler_params=params,
            cost_estimate=pl.CostEstimate(flops=flops, bytes_accessed=2 ** 22, transcendentals=0),
        )(keep, base, *partners, twiddle, high, low)

    parts = [pairs(white, [white, whiten(far, far_power)])]
    order = [0, reach]
    for k, block in near.items():
        parts.append(pairs(white, [block]))
        order.append(k)
    received = [lax.all_to_all(part, ("win", "freq"), 0, 0, tiled=True) for part in parts]
    scale = 1.0 / math.sqrt(w_dev * n_win * n_bins)
    return pl.pallas_call(
        functools.partial(combine_kernel, scale, order),
        out_shape=jax.ShapeDtypeStruct((ch, reach + 1, ch, width), jnp.float32),
        in_specs=[SMEM] + [VMEM] * len(received), out_specs=VMEM, compiler_params=params,
    )(pair_mask, *received)


def solution(mesh):
    in_specs = (
        P("win", None, ("fibre", "chan"), "freq"),
        P(("fibre", "win")),
        P(("fibre", "chan"), None),
    )
    out_specs = P(("fibre", "chan"), None, None, ("win", "freq"))
    return jax.shard_map(local, mesh=mesh, in_specs=in_specs, out_specs=out_specs, check_vma=False)
```

```python
import functools
import math

import jax
import jax.numpy as jnp
import numpy as np
from jax import lax
from jax.experimental import pallas as pl
from jax.experimental.pallas import tpu as pltpu
from jax.sharding import PartitionSpec as P

LAGS = 1024
F_LO = 60
NSAMP = 15000
EPS = 1e-06
LANES = 128
FINE = 32
TERMS = 6
VMEM_LIMIT = 48 * 1024 * 1024


def from_behind(block, axis, distance):
    devices = range(lax.axis_size(axis))
    route = [(i - distance, i) for i in devices if i - distance in devices]
    return lax.ppermute(block, axis, route)


def phases(bins, lags):
    turns = np.remainder(np.asarray(bins, np.int64)[:, None] * np.asarray(lags, np.int64)[None, :], NSAMP)
    angle = turns * (2.0 * math.pi / NSAMP)
    return np.stack([np.cos(angle), np.sin(angle)]).astype(np.float32)


def split(value):
    high = value.astype(jnp.bfloat16)
    return high, (value - high.astype(jnp.float32)).astype(jnp.bfloat16)


def power_kernel(x_ref, out_ref):
    for w in range(x_ref.shape[0]):
        x = x_ref[w].astype(jnp.float32)
        x = x[0] * x[0] + x[1] * x[1]
        out_ref[w] = jnp.sum(x, axis=-1, keepdims=True)


def table_kernel(coarse_ref, fine_ref, table_ref):
    width = table_ref.shape[-1]
    per_tile = LANES // FINE
    fine_cos, fine_sin = fine_ref[0], fine_ref[1]

    def body(a, carry):
        cos_a = coarse_ref[0, pl.ds(a, 1), :]
        sin_a = coarse_ref[1, pl.ds(a, 1), :]
        tile = a // per_tile
        start = pl.multiple_of((tile * TERMS * per_tile + a % per_tile) * FINE, FINE)
        values = (cos_a * fine_cos - sin_a * fine_sin, -(cos_a * fine_sin + sin_a * fine_cos))
        for part in range(2):
            high, low = split(values[part])
            for term, value in ((part, high), (2 + part, high), (4 + part, low)):
                table_ref[pl.ds(start + term * LANES, FINE), :] = value
        return carry

    lax.fori_loop(0, table_ref.shape[0] // (TERMS * FINE), body, 0)


def whiten_kernel(n_bins, x_ref, power_ref, out_ref):
    for w in range(x_ref.shape[0]):
        scale = lax.rsqrt(power_ref[w] / n_bins + EPS)
        for part in range(2):
            out_ref[w, part] = (x_ref[w, part].astype(jnp.float32) * scale).astype(jnp.bfloat16)


def cross_tile(own_ref, partner_ref, lanes):
    w_dev, _, ch, _ = own_ref.shape
    real = [None] * ch
    imag = [None] * ch
    for w in range(w_dev):
        partner_re = partner_ref[w, 0, :, lanes].astype(jnp.float32)
        partner_im = partner_ref[w, 1, :, lanes].astype(jnp.float32)
        for i in range(ch):
            own_re = own_ref[w, 0, i:i + 1, lanes]
            own_im = own_ref[w, 1, i:i + 1, lanes]
            re = own_re * partner_re + own_im * partner_im
            im = own_im * partner_re - own_re * partner_im
            real[i] = re if w == 0 else real[i] + re
            imag[i] = im if w == 0 else imag[i] + im
    return real, imag


def pairs_kernel(n_partners, first, groups, keep_ref, base_ref, *refs):
    partner_refs = refs[:n_partners]
    twiddle_ref, table_ref = refs[n_partners:n_partners + 2]
    own_ref, rows_ref = refs[-2:]
    out_refs = refs[-2 - groups:-2]
    w_dev, _, ch, f_dev = base_ref.shape
    tiles = f_dev // LANES
    depth = TERMS * LANES
    for w in range(w_dev):
        kept = keep_ref[w].astype(jnp.float32)
        for part in range(2):
            own_ref[w, part] = base_ref[w, part].astype(jnp.float32) * kept

    def prepare(partner_ref, tile):
        lanes = pl.ds(pl.multiple_of(tile * LANES, LANES), LANES)
        slot = tile % 2
        real, imag = cross_tile(own_ref, partner_ref, lanes)
        for q in range(groups):
            cos_q = twiddle_ref[q:q + 1, lanes]
            sin_q = twiddle_ref[groups + q:groups + q + 1, lanes]
            for i in range(0, ch, 2):
                rows = slice((q * ch + i) * ch, (q * ch + i + 2) * ch)
                re = jnp.concatenate(real[i:i + 2], axis=0)
                im = jnp.concatenate(imag[i:i + 2], axis=0)
                values = (re * cos_q - im * sin_q, re * sin_q + im * cos_q)
                for part in range(2):
                    high, low = split(values[part])
                    for term, value in ((part, high), (2 + part, low), (4 + part, high)):
                        rows_ref[slot, rows, term * LANES:(term + 1) * LANES] = value

    def transform(k, tile, start):
        table = table_ref[pl.ds(pl.multiple_of(tile * depth, depth), depth), :]
        part = jnp.dot(rows_ref[tile % 2], table, preferred_element_type=jnp.float32)
        for q, out_ref in enumerate(out_refs):
            block = part[q * ch * ch:(q + 1) * ch * ch]
            out_ref[first + k] = block if start else out_ref[first + k] + block

    for k, partner_ref in enumerate(partner_refs):
        prepare(partner_ref, 0)
        prepare(partner_ref, 1)
        transform(k, 0, True)

        def body(tile, carry):
            transform(k, tile - 1, False)
            prepare(partner_ref, tile)
            return carry

        lax.fori_loop(2, tiles, body, 0)
        transform(k, tiles - 1, False)


def combine_kernel(scale, order, groups, mask_ref, *refs):
    out_ref = refs[-1]
    ch = out_ref.shape[0]
    start = 0
    for place in range(0, len(refs) - 1, groups):
        parts = refs[place:place + groups]
        for n in range(parts[0].shape[0]):
            k = order[start + n]
            total = parts[0][n]
            for ref in parts[1:]:
                total = total + ref[n]
            for i in range(ch):
                factor = mask_ref[i, k].astype(jnp.float32) * scale
                out_ref[i, k] = total[i * ch:(i + 1) * ch] * factor
        start += parts[0].shape[0]


VMEM = pl.BlockSpec(memory_space=pltpu.VMEM)
SMEM = pl.BlockSpec(memory_space=pltpu.SMEM)


def local(spectra, keep, pair_mask):
    w_dev, _, ch, f_dev = spectra.shape
    reach = pair_mask.shape[1] - 1
    n_win, n_freq = (lax.axis_size(a) for a in ("win", "freq"))
    groups = n_win * n_freq
    width = LAGS // groups
    n_bins = f_dev * n_freq
    params = pltpu.CompilerParams(vmem_limit_bytes=VMEM_LIMIT)
    freq = lax.axis_index("freq")
    place = lax.axis_index(("win", "freq"))

    def whiten(block, power):
        return pl.pallas_call(
            functools.partial(whiten_kernel, n_bins),
            out_shape=jax.ShapeDtypeStruct(block.shape, jnp.bfloat16),
            in_specs=[VMEM] * 2, out_specs=VMEM, compiler_params=params,
        )(block, power)

    raw = from_behind(spectra, "chan", -1)
    power = pl.pallas_call(
        power_kernel,
        out_shape=jax.ShapeDtypeStruct((w_dev, ch, 1), jnp.float32),
        in_specs=[VMEM], out_specs=VMEM, compiler_params=params,
    )(spectra)
    power = lax.psum(power, "freq")
    white = whiten(spectra, power)
    moving = whiten(raw, from_behind(power, "chan", -1))

    coarse = phases(np.arange(0, n_bins, FINE), np.arange(width))
    coarse = coarse.reshape(2, n_freq, f_dev // FINE, width)
    coarse = lax.dynamic_index_in_dim(jnp.asarray(coarse), freq, 1, keepdims=False)
    fine = jnp.asarray(phases(F_LO + np.arange(FINE), np.arange(width)))
    table = pl.pallas_call(
        table_kernel,
        out_shape=jax.ShapeDtypeStruct((TERMS * f_dev, width), jnp.bfloat16),
        in_specs=[VMEM] * 2, out_specs=VMEM, compiler_params=params,
    )(coarse, fine)
    twiddle = phases(F_LO + np.arange(n_bins), np.arange(groups) * width - LAGS // 2)
    twiddle = np.moveaxis(twiddle, 1, 2).reshape(2, groups, n_freq, f_dev)
    twiddle = np.stack([np.roll(twiddle[:, :, g % n_freq], -g, axis=1) for g in range(groups)])
    twiddle = lax.dynamic_index_in_dim(jnp.asarray(twiddle), place, 0, keepdims=False)
    twiddle = twiddle.reshape(2 * groups, f_dev)

    rows = groups * ch * ch

    def pairs(base, partners):
        n = len(partners)
        flops = n * 6 * rows * 2 * f_dev * width
        return pl.pallas_call(
            functools.partial(pairs_kernel, n, 0, groups),
            out_shape=[jax.ShapeDtypeStruct((n, ch * ch, width), jnp.float32)] * groups,
            in_specs=[SMEM] + [VMEM] * (n + 3), out_specs=[VMEM] * groups,
            scratch_shapes=[
                pltpu.VMEM(base.shape, jnp.float32),
                pltpu.VMEM((2, rows, TERMS * LANES), jnp.bfloat16),
            ],
            compiler_params=params,
            cost_estimate=pl.CostEstimate(flops=flops, bytes_accessed=2 ** 22, transcendentals=0),
        )(keep, base, *partners, twiddle, table)

    def exchange(parts):
        received = [parts[0]]
        for turn in range(1, groups):
            route = [(g, (g + turn) % groups) for g in range(groups)]
            received.append(lax.ppermute(parts[turn], ("win", "freq"), route))
        return received

    parts = pairs(white, [white, moving])
    received = []
    for step in range(1, reach):
        moving = from_behind(moving, "chan", -1)
        moving, parts = lax.optimization_barrier((moving, parts))
        received += exchange(parts)
        parts = pairs(white, [moving])
    received += exchange(parts)
    scale = 1.0 / math.sqrt(w_dev * n_win * n_bins)
    return pl.pallas_call(
        functools.partial(combine_kernel, scale, list(range(reach + 1)), groups),
        out_shape=jax.ShapeDtypeStruct((ch, reach + 1, ch, width), jnp.float32),
        in_specs=[SMEM] + [VMEM] * len(received), out_specs=VMEM, compiler_params=params,
    )(pair_mask, *received)


def solution(mesh):
    in_specs = (
        P("win", None, ("fibre", "chan"), "freq"),
        P(("fibre", "win")),
        P(("fibre", "chan"), None),
    )
    out_specs = P(("fibre", "chan"), None, None, ("win", "freq"))
    return jax.shard_map(local, mesh=mesh, in_specs=in_specs, out_specs=out_specs, check_vma=False)
```

```python
import functools
import math

import jax
import jax.numpy as jnp
import numpy as np
from jax import lax
from jax.experimental import pallas as pl
from jax.experimental.pallas import tpu as pltpu
from jax.sharding import PartitionSpec as P

LAGS = 1024
F_LO = 60
NSAMP = 15000
EPS = 1e-06
LANES = 128
SUBLANES = 8
FINE = 32
VMEM_LIMIT = 48 * 1024 * 1024


def from_behind(block, axis, distance):
    devices = range(lax.axis_size(axis))
    route = [(i - distance, i) for i in devices if i - distance in devices]
    return lax.ppermute(block, axis, route)


def phases(bins, lags):
    turns = np.remainder(np.asarray(bins, np.int64)[:, None] * np.asarray(lags, np.int64)[None, :], NSAMP)
    angle = turns * (2.0 * math.pi / NSAMP)
    return np.stack([np.cos(angle), np.sin(angle)]).astype(np.float32)


def split(value):
    high = value.astype(jnp.bfloat16)
    return high, (value - high.astype(jnp.float32)).astype(jnp.bfloat16)


def bin_power(x):
    x = x.astype(jnp.float32)
    return jnp.sum(x[0] * x[0] + x[1] * x[1], axis=-1, keepdims=True)


def power_kernel(x_ref, out_ref):
    for w in range(x_ref.shape[0]):
        out_ref[w] = bin_power(x_ref[w])


def whiten_kernel(n_bins, x_ref, *refs):
    out_ref = refs[-1]
    for w in range(x_ref.shape[0]):
        power = bin_power(x_ref[w])
        for ref in refs[:-1]:
            power = power + ref[w]
        scale = lax.rsqrt(power / n_bins + EPS)
        for part in range(2):
            out_ref[w, part] = (x_ref[w, part].astype(jnp.float32) * scale).astype(jnp.bfloat16)


def table_kernel(groups, place_ref, coarse_ref, fine_ref, high_ref, low_ref):
    f_dev = high_ref.shape[0] // 2
    width = high_ref.shape[1] // groups
    start, place = place_ref[0], place_ref[1]
    for owner in range(groups):
        lags = slice(owner * width, (owner + 1) * width)
        to = pl.ds(pl.multiple_of((owner + groups - place) % groups * width, LANES), width)
        fine_cos = fine_ref[0, :, lags]
        fine_sin = fine_ref[1, :, lags]

        def body(step, carry):
            first = pl.multiple_of(start + step * SUBLANES, SUBLANES)
            coarse_cos = coarse_ref[0, pl.ds(first, SUBLANES), lags]
            coarse_sin = coarse_ref[1, pl.ds(first, SUBLANES), lags]
            for n in range(SUBLANES):
                cos_a, sin_a = coarse_cos[n:n + 1], coarse_sin[n:n + 1]
                rows = pl.multiple_of((step * SUBLANES + n) * FINE, FINE)
                high, low = split(cos_a * fine_cos - sin_a * fine_sin)
                high_ref[pl.ds(rows, FINE), to] = high
                low_ref[pl.ds(rows, FINE), to] = low
                high, low = split(-(cos_a * fine_sin + sin_a * fine_cos))
                high_ref[pl.ds(f_dev + rows, FINE), to] = high
                low_ref[pl.ds(f_dev + rows, FINE), to] = low
            return carry

        lax.fori_loop(0, f_dev // (FINE * SUBLANES), body, 0)


def cross_tile(own_ref, partner_ref, lanes):
    w_dev, _, ch, _ = own_ref.shape
    real = [None] * ch
    imag = [None] * ch
    for w in range(w_dev):
        partner_re = partner_ref[w, 0, :, lanes].astype(jnp.float32)
        partner_im = partner_ref[w, 1, :, lanes].astype(jnp.float32)
        for i in range(ch):
            own_re = own_ref[w, 0, i:i + 1, lanes]
            own_im = own_ref[w, 1, i:i + 1, lanes]
            re = own_re * partner_re + own_im * partner_im
            im = own_im * partner_re - own_re * partner_im
            real[i] = re if w == 0 else real[i] + re
            imag[i] = im if w == 0 else imag[i] + im
    return real, imag


def pairs_kernel(n_partners, groups, keep_ref, base_ref, *refs):
    partner_refs = refs[:n_partners]
    high_ref, low_ref = refs[n_partners:n_partners + 2]
    own_ref, rows_ref = refs[-2:]
    out_refs = refs[-2 - groups:-2]
    w_dev, _, ch, f_dev = base_ref.shape
    pairs = ch * ch
    width = out_refs[0].shape[-1]
    for w in range(w_dev):
        kept = keep_ref[w].astype(jnp.float32)
        for part in range(2):
            own_ref[w, part] = base_ref[w, part].astype(jnp.float32) * kept
    dot = functools.partial(jnp.dot, preferred_element_type=jnp.float32)
    for k, partner_ref in enumerate(partner_refs):

        def body(tile, carry):
            start = pl.multiple_of(tile * LANES, LANES)
            crosses = cross_tile(own_ref, partner_ref, pl.ds(start, LANES))
            for part in range(2):
                lanes = pl.ds(pl.multiple_of(part * f_dev + start, LANES), LANES)
                for i in range(0, ch, 2):
                    high, low = split(jnp.concatenate(crosses[part][i:i + 2], axis=0))
                    rows_ref[i * ch:(i + 2) * ch, lanes] = high
                    rows_ref[pairs + i * ch:pairs + (i + 2) * ch, lanes] = low
            return carry

        lax.fori_loop(0, f_dev // LANES, body, 0)
        both = dot(rows_ref[...], high_ref[...])
        total = both[:pairs] + both[pairs:] + dot(rows_ref[:pairs], low_ref[...])
        for turn, out_ref in enumerate(out_refs):
            out_ref[k] = total[:, turn * width:(turn + 1) * width]


def combine_kernel(scale, order, groups, mask_ref, *refs):
    out_ref = refs[-1]
    ch = out_ref.shape[0]
    start = 0
    for place in range(0, len(refs) - 1, groups):
        parts = refs[place:place + groups]
        for n in range(parts[0].shape[0]):
            k = order[start + n]
            total = parts[0][n]
            for ref in parts[1:]:
                total = total + ref[n]
            for i in range(ch):
                factor = mask_ref[i, k].astype(jnp.float32) * scale
                out_ref[i, k] = total[i * ch:(i + 1) * ch] * factor
        start += parts[0].shape[0]


VMEM = pl.BlockSpec(memory_space=pltpu.VMEM)
SMEM = pl.BlockSpec(memory_space=pltpu.SMEM)


def local(spectra, keep, pair_mask):
    w_dev, _, ch, f_dev = spectra.shape
    reach = pair_mask.shape[1] - 1
    n_chan, n_win, n_freq = (lax.axis_size(a) for a in ("chan", "win", "freq"))
    groups = n_win * n_freq
    width = LAGS // groups
    n_bins = f_dev * n_freq
    params = pltpu.CompilerParams(vmem_limit_bytes=VMEM_LIMIT)
    freq = lax.axis_index("freq")
    place = lax.axis_index(("win", "freq"))

    def whiten(block, others):
        return pl.pallas_call(
            functools.partial(whiten_kernel, n_bins),
            out_shape=jax.ShapeDtypeStruct(block.shape, jnp.bfloat16),
            in_specs=[VMEM] * (1 + len(others)), out_specs=VMEM, compiler_params=params,
        )(block, *others)

    raw = from_behind(spectra, "chan", -1)
    power = pl.pallas_call(
        power_kernel,
        out_shape=jax.ShapeDtypeStruct((w_dev, ch, 1), jnp.float32),
        in_specs=[VMEM], out_specs=VMEM, compiler_params=params,
    )(spectra)
    own_power, next_power = [], []
    for turn in range(1, n_freq):
        route = [(f, (f + turn) % n_freq) for f in range(n_freq)]
        own_power.append(lax.ppermute(power, "freq", route))
        route = [(c * n_freq + f, (c - 1) * n_freq + to) for c in range(1, n_chan) for f, to in route]
        next_power.append(lax.ppermute(power, ("chan", "freq"), route))
    white = whiten(spectra, own_power)
    moving = whiten(raw, next_power)

    lags = np.arange(LAGS) - LAGS // 2
    coarse = jnp.asarray(phases(np.arange(0, n_bins, FINE), lags))
    fine = jnp.asarray(phases(F_LO + np.arange(FINE), lags))
    places = jnp.stack([freq * (f_dev // FINE), place]).astype(jnp.int32)
    high, low = pl.pallas_call(
        functools.partial(table_kernel, groups),
        out_shape=[jax.ShapeDtypeStruct((2 * f_dev, LAGS), jnp.bfloat16)] * 2,
        in_specs=[SMEM] + [VMEM] * 2, out_specs=[VMEM] * 2, compiler_params=params,
    )(places, coarse, fine)

    def pairs(base, partners):
        n = len(partners)
        flops = n * 6 * ch * ch * 2 * f_dev * LAGS
        return pl.pallas_call(
            functools.partial(pairs_kernel, n, groups),
            out_shape=[jax.ShapeDtypeStruct((n, ch * ch, width), jnp.float32)] * groups,
            in_specs=[SMEM] + [VMEM] * (n + 3), out_specs=[VMEM] * groups,
            scratch_shapes=[
                pltpu.VMEM(base.shape, jnp.float32),
                pltpu.VMEM((2 * ch * ch, 2 * f_dev), jnp.bfloat16),
            ],
            compiler_params=params,
            cost_estimate=pl.CostEstimate(flops=flops, bytes_accessed=2 ** 22, transcendentals=0),
        )(keep, base, *partners, high, low)

    def exchange(parts):
        received = [parts[0]]
        for turn in range(1, groups):
            route = [(g, (g + turn) % groups) for g in range(groups)]
            received.append(lax.ppermute(parts[turn], ("win", "freq"), route))
        return received

    parts = pairs(white, [white, moving])
    received = []
    for step in range(1, reach):
        moving = from_behind(moving, "chan", -1)
        moving, parts = lax.optimization_barrier((moving, parts))
        received += exchange(parts)
        parts = pairs(white, [moving])
    received += exchange(parts)
    scale = 1.0 / math.sqrt(w_dev * n_win * n_bins)
    return pl.pallas_call(
        functools.partial(combine_kernel, scale, list(range(reach + 1)), groups),
        out_shape=jax.ShapeDtypeStruct((ch, reach + 1, ch, width), jnp.float32),
        in_specs=[SMEM] + [VMEM] * len(received), out_specs=VMEM, compiler_params=params,
    )(pair_mask, *received)


def solution(mesh):
    in_specs = (
        P("win", None, ("fibre", "chan"), "freq"),
        P(("fibre", "win")),
        P(("fibre", "chan"), None),
    )
    out_specs = P(("fibre", "chan"), None, None, ("win", "freq"))
    return jax.shard_map(local, mesh=mesh, in_specs=in_specs, out_specs=out_specs, check_vma=False)
```

```python
import functools
import math

import jax
import jax.numpy as jnp
import numpy as np
from jax import lax
from jax.experimental import pallas as pl
from jax.experimental.pallas import tpu as pltpu
from jax.sharding import PartitionSpec as P

LAGS = 1024
F_LO = 60
NSAMP = 15000
EPS = 1e-06
LANES = 128
SUBLANES = 8
FINE = 32
BLOCK = 256
VMEM_LIMIT = 16 * 1024 * 1024


def from_behind(block, axis, distance):
    devices = range(lax.axis_size(axis))
    route = [(i - distance, i) for i in devices if i - distance in devices]
    return lax.ppermute(block, axis, route)


def phases(bins, half_lags):
    turns = np.remainder(np.asarray(bins, np.int64)[:, None] * np.asarray(half_lags, np.int64)[None, :], 2 * NSAMP)
    angle = turns * (math.pi / NSAMP)
    return np.stack([np.cos(angle), np.sin(angle)]).astype(np.float32)


def split(value):
    high = value.astype(jnp.bfloat16)
    return high, (value - high.astype(jnp.float32)).astype(jnp.bfloat16)


def bin_power(x):
    x = x.astype(jnp.float32)
    return jnp.sum(x[0] * x[0] + x[1] * x[1], axis=-1, keepdims=True)


def power_kernel(x_ref, power_ref, copy_ref):
    for w in range(x_ref.shape[0]):
        x = x_ref[w]
        power_ref[w] = bin_power(x)
        copy_ref[w] = x


def whiten_kernel(n_bins, x_ref, *refs):
    out_ref = refs[-1]
    for w in range(x_ref.shape[0]):
        power = bin_power(x_ref[w])
        for ref in refs[:-1]:
            power = power + ref[w]
        scale = lax.rsqrt(power / n_bins + EPS)
        for part in range(2):
            out_ref[w, part] = (x_ref[w, part].astype(jnp.float32) * scale).astype(jnp.bfloat16)


def own_kernel(n_bins, keep_ref, x_ref, *refs):
    white_ref, own_ref = refs[-2:]
    whiten_kernel(n_bins, x_ref, *refs[:-2], white_ref)
    for w in range(x_ref.shape[0]):
        own_ref[w] = white_ref[w].astype(jnp.float32) * keep_ref[w].astype(jnp.float32)


def table_kernel(place_ref, base_ref, table_ref):
    f_dev, width = table_ref.shape[1:]
    coarse = base_ref.shape[1] - FINE
    start = place_ref[0] * (f_dev // FINE)
    for block in range(0, width, BLOCK):
        lags = slice(block, block + BLOCK)
        fine_cos = base_ref[0, coarse:, lags]
        fine_sin = base_ref[1, coarse:, lags]

        def body(step, carry):
            first = pl.multiple_of(start + step * SUBLANES, SUBLANES)
            coarse_cos = base_ref[0, pl.ds(first, SUBLANES), lags]
            coarse_sin = base_ref[1, pl.ds(first, SUBLANES), lags]
            for n in range(SUBLANES):
                cos_a, sin_a = coarse_cos[n:n + 1], coarse_sin[n:n + 1]
                rows = pl.ds(pl.multiple_of((step * SUBLANES + n) * FINE, FINE), FINE)
                table_ref[0, rows, lags], table_ref[1, rows, lags] = split(cos_a * fine_cos - sin_a * fine_sin)
                table_ref[2, rows, lags], table_ref[3, rows, lags] = split(cos_a * fine_sin + sin_a * fine_cos)
            return carry

        lax.fori_loop(0, f_dev // (FINE * SUBLANES), body, 0)


def cross_tile(own_ref, partner_ref, lanes):
    w_dev, _, ch, _ = own_ref.shape
    real = [None] * ch
    imag = [None] * ch
    for w in range(w_dev):
        partner_re = partner_ref[w, 0, :, lanes].astype(jnp.float32)
        partner_im = partner_ref[w, 1, :, lanes].astype(jnp.float32)
        for i in range(ch):
            own_re = own_ref[w, 0, i:i + 1, lanes]
            own_im = own_ref[w, 1, i:i + 1, lanes]
            re = own_re * partner_re + own_im * partner_im
            im = own_im * partner_re - own_re * partner_im
            real[i] = re if w == 0 else real[i] + re
            imag[i] = im if w == 0 else imag[i] + im
    return real, imag


def pairs_kernel(n_partners, groups, place_ref, own_ref, *refs):
    partner_refs = refs[:n_partners]
    twist_ref, table_ref = refs[n_partners:n_partners + 2]
    rows_ref, sums_ref = refs[-2:]
    out_refs = refs[-2 - groups:-2]
    ch, f_dev = own_ref.shape[2:]
    pairs = ch * ch
    width = out_refs[0].shape[-1]
    freq, place = place_ref[0], place_ref[1]
    dot = functools.partial(jnp.dot, preferred_element_type=jnp.float32)
    for k, partner_ref in enumerate(partner_refs):

        def body(tile, carry):
            lanes = pl.ds(pl.multiple_of(tile * LANES, LANES), LANES)
            real, imag = cross_tile(own_ref, partner_ref, lanes)
            cos = twist_ref[freq, 0:1, lanes]
            sin = twist_ref[freq, 1:2, lanes]
            for i in range(0, ch, 2):
                re = jnp.concatenate(real[i:i + 2], axis=0)
                im = jnp.concatenate(imag[i:i + 2], axis=0)
                for part, value in enumerate((re * cos + im * sin, im * cos - re * sin)):
                    high, low = split(value)
                    rows_ref[part, i * ch:(i + 2) * ch, lanes] = high
                    rows_ref[part, pairs + i * ch:pairs + (i + 2) * ch, lanes] = low
            return carry

        lax.fori_loop(0, f_dev // LANES, body, 0)
        for part in range(2):
            both = dot(rows_ref[part], table_ref[2 * part])
            sums_ref[part] = both[:pairs] + both[pairs:] + dot(rows_ref[part, :pairs], table_ref[2 * part + 1])
        for turn, out_ref in enumerate(out_refs):
            owner = (place + turn) % groups
            upper = owner >= groups // 2
            block = jnp.where(upper, owner - groups // 2, groups // 2 - 1 - owner)
            sign = jnp.where(upper, -1.0, 1.0)
            lags = pl.ds(pl.multiple_of(block * width, LANES), width)
            out_ref[k] = sums_ref[0, :, lags] + sign * sums_ref[1, :, lags]


def reverse_lanes(value):
    backward = LANES - 1 - lax.broadcasted_iota(jnp.int32, (value.shape[0], LANES), 1)
    pieces = [
        jnp.take_along_axis(value[:, start:start + LANES], backward, axis=1, mode="promise_in_bounds")
        for start in range(0, value.shape[1], LANES)
    ]
    return jnp.concatenate(pieces[::-1], axis=1)


def combine_kernel(scale, groups, mask_ref, place_ref, *refs):
    out_ref = refs[-1]
    ch = out_ref.shape[0]
    lower = place_ref[1] < groups // 2
    k = 0
    for first in range(0, len(refs) - 1, groups):
        parts = refs[first:first + groups]
        for n in range(parts[0].shape[0]):
            total = parts[0][n]
            for ref in parts[1:]:
                total = total + ref[n]
            total = jnp.where(lower, reverse_lanes(total), total)
            for i in range(ch):
                factor = mask_ref[i, k].astype(jnp.float32) * scale
                out_ref[i, k] = total[i * ch:(i + 1) * ch] * factor
            k += 1


VMEM = pl.BlockSpec(memory_space=pltpu.VMEM)
SMEM = pl.BlockSpec(memory_space=pltpu.SMEM)


def local(spectra, keep, pair_mask):
    w_dev, _, ch, f_dev = spectra.shape
    reach = pair_mask.shape[1] - 1
    n_chan, n_win, n_freq = (lax.axis_size(a) for a in ("chan", "win", "freq"))
    groups = n_win * n_freq
    width = LAGS // groups
    n_bins = f_dev * n_freq
    params = pltpu.CompilerParams(vmem_limit_bytes=VMEM_LIMIT)
    freq = lax.axis_index("freq")
    place = lax.axis_index(("win", "freq"))

    places = jnp.stack([freq, place]).astype(jnp.int32)

    def cost(flops, size):
        return pl.CostEstimate(flops=flops, bytes_accessed=size, transcendentals=0)

    raw = from_behind(spectra, "chan", -1)
    power, copied = pl.pallas_call(
        power_kernel,
        out_shape=[
            jax.ShapeDtypeStruct((w_dev, ch, 1), jnp.float32),
            jax.ShapeDtypeStruct(spectra.shape, spectra.dtype),
        ],
        in_specs=[VMEM], out_specs=[VMEM] * 2, compiler_params=params, cost_estimate=cost(0, 2 ** 22),
    )(spectra)
    own_power, next_power = [], []
    for turn in range(1, n_freq):
        route = [(f, (f + turn) % n_freq) for f in range(n_freq)]
        own_power.append(lax.ppermute(power, "freq", route))
        route = [(c * n_freq + f, (c - 1) * n_freq + to) for c in range(1, n_chan) for f, to in route]
        next_power.append(lax.ppermute(power, ("chan", "freq"), route))

    half_lags = 2 * np.arange(LAGS // 2) + 1
    coarse = phases(np.arange(0, n_bins, FINE), half_lags)
    fine = phases(F_LO + np.arange(FINE), half_lags)
    table = pl.pallas_call(
        table_kernel,
        out_shape=jax.ShapeDtypeStruct((4, f_dev, LAGS // 2), jnp.bfloat16),
        in_specs=[SMEM, VMEM], out_specs=VMEM, compiler_params=params, cost_estimate=cost(0, 2 ** 23),
    )(places, jnp.asarray(np.concatenate([coarse, fine], axis=1)))
    twist = phases(F_LO + np.arange(n_bins), np.ones(1)).reshape(2, n_freq, f_dev)
    twist = jnp.asarray(np.moveaxis(twist, 0, 1))

    raw, table, own_power = lax.optimization_barrier((raw, table, own_power))
    moving = pl.pallas_call(
        functools.partial(whiten_kernel, n_bins),
        out_shape=jax.ShapeDtypeStruct(raw.shape, jnp.bfloat16),
        in_specs=[VMEM] * n_freq, out_specs=VMEM, compiler_params=params,
    )(raw, *next_power)
    white, own = pl.pallas_call(
        functools.partial(own_kernel, n_bins),
        out_shape=[
            jax.ShapeDtypeStruct(spectra.shape, jnp.bfloat16),
            jax.ShapeDtypeStruct(spectra.shape, jnp.float32),
        ],
        in_specs=[SMEM] + [VMEM] * n_freq, out_specs=[VMEM] * 2, compiler_params=params,
    )(keep, copied, *own_power)

    def pairs(partners):
        n = len(partners)
        return pl.pallas_call(
            functools.partial(pairs_kernel, n, groups),
            out_shape=[jax.ShapeDtypeStruct((n, ch * ch, width), jnp.float32)] * groups,
            in_specs=[SMEM] + [VMEM] * (n + 3), out_specs=[VMEM] * groups,
            scratch_shapes=[
                pltpu.VMEM((2, 2 * ch * ch, f_dev), jnp.bfloat16),
                pltpu.VMEM((2, ch * ch, LAGS // 2), jnp.float32),
            ],
            compiler_params=params,
            cost_estimate=cost(n * 6 * ch * ch * 2 * f_dev * LAGS, 2 ** 22),
        )(places, own, *partners, twist, table)

    def exchange(parts):
        received = [parts[0]]
        for turn in range(1, groups):
            route = [(g, (g + turn) % groups) for g in range(groups)]
            received.append(lax.ppermute(parts[turn], ("win", "freq"), route))
        return received

    parts = pairs([white, moving])
    received = []
    for step in range(1, reach):
        moving = from_behind(moving, "chan", -1)
        moving, parts = lax.optimization_barrier((moving, parts))
        received += exchange(parts)
        parts = pairs([moving])
    received += exchange(parts)
    scale = 1.0 / math.sqrt(w_dev * n_win * n_bins)
    return pl.pallas_call(
        functools.partial(combine_kernel, scale, groups),
        out_shape=jax.ShapeDtypeStruct((ch, reach + 1, ch, width), jnp.float32),
        in_specs=[SMEM] * 2 + [VMEM] * len(received), out_specs=VMEM, compiler_params=params,
    )(pair_mask, places, *received)


def solution(mesh):
    in_specs = (
        P("win", None, ("fibre", "chan"), "freq"),
        P(("fibre", "win")),
        P(("fibre", "chan"), None),
    )
    out_specs = P(("fibre", "chan"), None, None, ("win", "freq"))
    return jax.shard_map(local, mesh=mesh, in_specs=in_specs, out_specs=out_specs, check_vma=False)
```

```python
import functools
import math

import jax
import jax.numpy as jnp
import numpy as np
from jax import lax
from jax.experimental import pallas as pl
from jax.experimental.pallas import tpu as pltpu
from jax.sharding import PartitionSpec as P

LAGS = 1024
F_LO = 60
NSAMP = 15000
EPS = 1e-06
LANES = 128
SUBLANES = 8
FINE = 32
BLOCK = 256
PIECES = 2
VMEM_LIMIT = 16 * 1024 * 1024


def from_behind(block, axis, distance):
    devices = range(lax.axis_size(axis))
    route = [(i - distance, i) for i in devices if i - distance in devices]
    return lax.ppermute(block, axis, route)


def phases(bins, half_lags):
    turns = np.remainder(np.asarray(bins, np.int64)[:, None] * np.asarray(half_lags, np.int64)[None, :], 2 * NSAMP)
    angle = turns * (math.pi / NSAMP)
    return np.stack([np.cos(angle), np.sin(angle)]).astype(np.float32)


def split(value):
    high = value.astype(jnp.bfloat16)
    return high, (value - high.astype(jnp.float32)).astype(jnp.bfloat16)


def bin_power(x):
    x = x.astype(jnp.float32)
    return jnp.sum(x[0] * x[0] + x[1] * x[1], axis=-1, keepdims=True)


def power_kernel(x_ref, power_ref, copy_ref):
    for w in range(x_ref.shape[0]):
        x = x_ref[w]
        power_ref[w] = bin_power(x)
        copy_ref[w] = x


def whiten_kernel(n_bins, n_pieces, x_ref, *refs):
    out_refs = refs[-n_pieces:]
    per_piece = x_ref.shape[0] // n_pieces
    for w in range(x_ref.shape[0]):
        power = bin_power(x_ref[w])
        for ref in refs[:-n_pieces]:
            power = power + ref[w]
        scale = lax.rsqrt(power / n_bins + EPS)
        for part in range(2):
            value = x_ref[w, part].astype(jnp.float32) * scale
            out_refs[w // per_piece][w % per_piece, part] = value.astype(jnp.bfloat16)


def own_kernel(n_bins, keep_ref, x_ref, *refs):
    white_ref, own_ref = refs[-2:]
    whiten_kernel(n_bins, 1, x_ref, *refs[:-2], white_ref)
    for w in range(x_ref.shape[0]):
        own_ref[w] = white_ref[w].astype(jnp.float32) * keep_ref[w].astype(jnp.float32)


def table_kernel(place_ref, base_ref, table_ref):
    f_dev, width = table_ref.shape[1:]
    coarse = base_ref.shape[1] - FINE
    start = place_ref[0] * (f_dev // FINE)
    for block in range(0, width, BLOCK):
        lags = slice(block, block + BLOCK)
        fine_cos = base_ref[0, coarse:, lags]
        fine_sin = base_ref[1, coarse:, lags]

        def body(step, carry):
            first = pl.multiple_of(start + step * SUBLANES, SUBLANES)
            coarse_cos = base_ref[0, pl.ds(first, SUBLANES), lags]
            coarse_sin = base_ref[1, pl.ds(first, SUBLANES), lags]
            for n in range(SUBLANES):
                cos_a, sin_a = coarse_cos[n:n + 1], coarse_sin[n:n + 1]
                rows = pl.ds(pl.multiple_of((step * SUBLANES + n) * FINE, FINE), FINE)
                table_ref[0, rows, lags], table_ref[1, rows, lags] = split(cos_a * fine_cos - sin_a * fine_sin)
                table_ref[2, rows, lags], table_ref[3, rows, lags] = split(cos_a * fine_sin + sin_a * fine_cos)
            return carry

        lax.fori_loop(0, f_dev // (FINE * SUBLANES), body, 0)


def cross_tile(own_ref, piece_refs, lanes):
    ch = own_ref.shape[2]
    real = [None] * ch
    imag = [None] * ch
    windows = [(ref, n) for ref in piece_refs for n in range(ref.shape[0])]
    for w, (ref, n) in enumerate(windows):
        partner_re = ref[n, 0, :, lanes].astype(jnp.float32)
        partner_im = ref[n, 1, :, lanes].astype(jnp.float32)
        for i in range(ch):
            own_re = own_ref[w, 0, i:i + 1, lanes]
            own_im = own_ref[w, 1, i:i + 1, lanes]
            re = own_re * partner_re + own_im * partner_im
            im = own_im * partner_re - own_re * partner_im
            real[i] = re if w == 0 else real[i] + re
            imag[i] = im if w == 0 else imag[i] + im
    return real, imag


def pairs_kernel(n_pieces, n_win, n_freq, place_ref, own_ref, *refs):
    total_pieces = sum(n_pieces)
    piece_refs = refs[:total_pieces]
    twist_ref, table_ref = refs[total_pieces:total_pieces + 2]
    before_refs = refs[total_pieces + 2:-2 - n_freq]
    out_refs = refs[-2 - n_freq:-2]
    rows_ref, sums_ref = refs[-2:]
    ch, f_dev = own_ref.shape[2:]
    pairs = ch * ch
    groups = n_win * n_freq
    done = out_refs[0].shape[0] - len(n_pieces)
    width = out_refs[0].shape[-1]
    freq, win = place_ref[0], place_ref[1]
    dot = functools.partial(jnp.dot, preferred_element_type=jnp.float32)
    for before_ref, out_ref in zip(before_refs, out_refs):
        out_ref[:done] = before_ref[...]
    for n, count in enumerate(n_pieces):
        partner_refs = piece_refs[sum(n_pieces[:n]):sum(n_pieces[:n]) + count]

        def body(tile, carry):
            lanes = pl.ds(pl.multiple_of(tile * LANES, LANES), LANES)
            real, imag = cross_tile(own_ref, partner_refs, lanes)
            cos = twist_ref[freq, 0:1, lanes]
            sin = twist_ref[freq, 1:2, lanes]
            for i in range(0, ch, 2):
                re = jnp.concatenate(real[i:i + 2], axis=0)
                im = jnp.concatenate(imag[i:i + 2], axis=0)
                for part, value in enumerate((re * cos + im * sin, im * cos - re * sin)):
                    high, low = split(value)
                    rows_ref[part, i * ch:(i + 2) * ch, lanes] = high
                    rows_ref[part, pairs + i * ch:pairs + (i + 2) * ch, lanes] = low
            return carry

        lax.fori_loop(0, f_dev // LANES, body, 0)
        for part in range(2):
            both = dot(rows_ref[part], table_ref[2 * part])
            sums_ref[part] = both[:pairs] + both[pairs:] + dot(rows_ref[part, :pairs], table_ref[2 * part + 1])
        for turn_freq, out_ref in enumerate(out_refs):
            for turn_win in range(n_win):
                owner = (win + turn_win) % n_win * n_freq + (freq + turn_freq) % n_freq
                upper = owner >= groups // 2
                block = jnp.where(upper, owner - groups // 2, groups // 2 - 1 - owner)
                sign = jnp.where(upper, -1.0, 1.0)
                lags = pl.ds(pl.multiple_of(block * width, LANES), width)
                out_ref[done + n, turn_win] = sums_ref[0, :, lags] + sign * sums_ref[1, :, lags]


def add_kernel(n_parts, *refs):
    for turn, out_ref in enumerate(refs[n_parts:]):
        total = refs[0][:, turn]
        for ref in refs[1:n_parts]:
            total = total + ref[:, turn]
        out_ref[...] = total


def total_kernel(*refs):
    total = refs[0][...]
    for ref in refs[1:-1]:
        total = total + ref[...]
    refs[-1][...] = total


def reverse_lanes(value):
    backward = LANES - 1 - lax.broadcasted_iota(jnp.int32, (value.shape[0], LANES), 1)
    pieces = [
        jnp.take_along_axis(value[:, start:start + LANES], backward, axis=1, mode="promise_in_bounds")
        for start in range(0, value.shape[1], LANES)
    ]
    return jnp.concatenate(pieces[::-1], axis=1)


def combine_kernel(scale, groups, n_freq, mask_ref, place_ref, *refs):
    out_ref = refs[-1]
    ch = out_ref.shape[0]
    lower = place_ref[1] * n_freq + place_ref[0] < groups // 2
    k = 0
    for parts in (refs[:1], refs[1:-1]):
        for n in range(parts[0].shape[0]):
            total = parts[0][n]
            for ref in parts[1:]:
                total = total + ref[n]
            total = jnp.where(lower, reverse_lanes(total), total)
            for i in range(ch):
                factor = mask_ref[i, k].astype(jnp.float32) * scale
                out_ref[i, k] = total[i * ch:(i + 1) * ch] * factor
            k += 1


VMEM = pl.BlockSpec(memory_space=pltpu.VMEM)
SMEM = pl.BlockSpec(memory_space=pltpu.SMEM)


def local(spectra, keep, pair_mask):
    w_dev, _, ch, f_dev = spectra.shape
    reach = pair_mask.shape[1] - 1
    n_chan, n_win, n_freq = (lax.axis_size(a) for a in ("chan", "win", "freq"))
    width = LAGS // (n_win * n_freq)
    n_bins = f_dev * n_freq
    params = pltpu.CompilerParams(vmem_limit_bytes=VMEM_LIMIT)
    freq = lax.axis_index("freq")

    places = jnp.stack([freq, lax.axis_index("win")]).astype(jnp.int32)

    def cost(flops, size):
        return pl.CostEstimate(flops=flops, bytes_accessed=size, transcendentals=0)

    raw = from_behind(spectra, "chan", -1)
    power, copied = pl.pallas_call(
        power_kernel,
        out_shape=[
            jax.ShapeDtypeStruct((w_dev, ch, 1), jnp.float32),
            jax.ShapeDtypeStruct(spectra.shape, spectra.dtype),
        ],
        in_specs=[VMEM], out_specs=[VMEM] * 2, compiler_params=params, cost_estimate=cost(0, 2 ** 22),
    )(spectra)
    own_power, next_power = [], []
    for turn in range(1, n_freq):
        route = [(f, (f + turn) % n_freq) for f in range(n_freq)]
        own_power.append(lax.ppermute(power, "freq", route))
        route = [(c * n_freq + f, (c - 1) * n_freq + to) for c in range(1, n_chan) for f, to in route]
        next_power.append(lax.ppermute(power, ("chan", "freq"), route))

    half_lags = 2 * np.arange(LAGS // 2) + 1
    coarse = phases(np.arange(0, n_bins, FINE), half_lags)
    fine = phases(F_LO + np.arange(FINE), half_lags)
    table = pl.pallas_call(
        table_kernel,
        out_shape=jax.ShapeDtypeStruct((4, f_dev, LAGS // 2), jnp.bfloat16),
        in_specs=[SMEM, VMEM], out_specs=VMEM, compiler_params=params, cost_estimate=cost(0, 2 ** 23),
    )(places, jnp.asarray(np.concatenate([coarse, fine], axis=1)))
    twist = phases(F_LO + np.arange(n_bins), np.ones(1)).reshape(2, n_freq, f_dev)
    twist = jnp.asarray(np.moveaxis(twist, 0, 1))

    white, own = pl.pallas_call(
        functools.partial(own_kernel, n_bins),
        out_shape=[
            jax.ShapeDtypeStruct(spectra.shape, jnp.bfloat16),
            jax.ShapeDtypeStruct(spectra.shape, jnp.float32),
        ],
        in_specs=[SMEM] + [VMEM] * n_freq, out_specs=[VMEM] * 2, compiler_params=params,
    )(keep, copied, *own_power)
    raw, table, white = lax.optimization_barrier((raw, table, white))
    piece = jax.ShapeDtypeStruct((w_dev // PIECES,) + raw.shape[1:], jnp.bfloat16)
    moving = pl.pallas_call(
        functools.partial(whiten_kernel, n_bins, PIECES),
        out_shape=[piece] * PIECES,
        in_specs=[VMEM] * n_freq, out_specs=[VMEM] * PIECES, compiler_params=params,
    )(raw, *next_power)

    def pairs(partners, before):
        pieces = [piece for partner in partners for piece in partner]
        n = len(partners) + (before[0].shape[0] if before else 0)
        return pl.pallas_call(
            functools.partial(pairs_kernel, [len(partner) for partner in partners], n_win, n_freq),
            out_shape=[jax.ShapeDtypeStruct((n, n_win, ch * ch, width), jnp.float32)] * n_freq,
            in_specs=[SMEM] + [VMEM] * (3 + len(pieces) + len(before)), out_specs=[VMEM] * n_freq,
            scratch_shapes=[
                pltpu.VMEM((2, 2 * ch * ch, f_dev), jnp.bfloat16),
                pltpu.VMEM((2, ch * ch, LAGS // 2), jnp.float32),
            ],
            compiler_params=params,
            cost_estimate=cost(2 ** 33, 2 ** 22),
        )(places, own, *pieces, twist, table, *before)

    def turns(parts, axis, size):
        received = [parts[0]]
        for turn in range(1, size):
            route = [(g, (g + turn) % size) for g in range(size)]
            received.append(lax.ppermute(parts[turn], axis, route))
        return received

    def gather_bins(parts):
        n = parts[0].shape[0]
        return pl.pallas_call(
            functools.partial(add_kernel, n_freq),
            out_shape=[jax.ShapeDtypeStruct((n, ch * ch, width), jnp.float32)] * n_win,
            in_specs=[VMEM] * n_freq, out_specs=[VMEM] * n_win, compiler_params=params,
        )(*turns(parts, "freq", n_freq))

    def total(parts):
        return pl.pallas_call(
            total_kernel,
            out_shape=jax.ShapeDtypeStruct(parts[0].shape, jnp.float32),
            in_specs=[VMEM] * len(parts), out_specs=VMEM, compiler_params=params,
        )(*parts)

    parts = list(pairs([[white], moving], []))
    early = None
    for step in range(1, reach):
        arrived = [from_behind(block, "chan", -1) for block in moving]
        if step == 1:
            arrived, parts = lax.optimization_barrier((arrived, parts))
            sums = list(gather_bins(parts))
            early = total(turns(sums, "win", n_win))
            parts = []
        else:
            parts = pairs([moving], parts)
        moving = arrived
    if early is not None:
        moving[-1], early = lax.optimization_barrier((moving[-1], early))
        parts = pairs([moving], parts)
    received = turns(gather_bins(parts), "win", n_win)
    scale = 1.0 / math.sqrt(w_dev * n_win * n_bins)
    return pl.pallas_call(
        functools.partial(combine_kernel, scale, n_win * n_freq, n_freq),
        out_shape=jax.ShapeDtypeStruct((ch, reach + 1, ch, width), jnp.float32),
        in_specs=[SMEM] * 2 + [VMEM] * (1 + len(received)), out_specs=VMEM, compiler_params=params,
    )(pair_mask, places, early, *received)


def solution(mesh):
    in_specs = (
        P("win", None, ("fibre", "chan"), "freq"),
        P(("fibre", "win")),
        P(("fibre", "chan"), None),
    )
    out_specs = P(("fibre", "chan"), None, None, ("win", "freq"))
    return jax.shard_map(local, mesh=mesh, in_specs=in_specs, out_specs=out_specs, check_vma=False)
```

```python
import functools
import math

import jax
import jax.numpy as jnp
import numpy as np
from jax import lax
from jax.experimental import pallas as pl
from jax.experimental.pallas import tpu as pltpu
from jax.sharding import PartitionSpec as P

LAGS = 1024
F_LO = 60
NSAMP = 15000
EPS = 1e-06
LANES = 128
SUBLANES = 8
FINE = 32
BLOCK = 256
VMEM_LIMIT = 16 * 1024 * 1024


def from_behind(block, axis, distance):
    devices = range(lax.axis_size(axis))
    route = [(i - distance, i) for i in devices if i - distance in devices]
    return lax.ppermute(block, axis, route)


def phases(bins, half_lags):
    turns = np.remainder(np.asarray(bins, np.int64)[:, None] * np.asarray(half_lags, np.int64)[None, :], 2 * NSAMP)
    angle = turns * (math.pi / NSAMP)
    return np.stack([np.cos(angle), np.sin(angle)]).astype(np.float32)


def split(value):
    high = value.astype(jnp.bfloat16)
    return high, (value - high.astype(jnp.float32)).astype(jnp.bfloat16)


def bin_power(x):
    x = x.astype(jnp.float32)
    return jnp.sum(x[0] * x[0] + x[1] * x[1], axis=-1, keepdims=True)


def power_kernel(x_ref, power_ref, copy_ref):
    for w in range(x_ref.shape[0]):
        x = x_ref[w]
        power_ref[w] = bin_power(x)
        copy_ref[w] = x


def whiten_kernel(n_bins, x_ref, *refs):
    out_ref = refs[-1]
    for w in range(x_ref.shape[0]):
        power = bin_power(x_ref[w])
        for ref in refs[:-1]:
            power = power + ref[w]
        scale = lax.rsqrt(power / n_bins + EPS)
        for part in range(2):
            out_ref[w, part] = (x_ref[w, part].astype(jnp.float32) * scale).astype(jnp.bfloat16)


def keep_kernel(keep_ref, white_ref, out_ref):
    for w in range(white_ref.shape[0]):
        out_ref[w] = white_ref[w].astype(jnp.float32) * keep_ref[w].astype(jnp.float32)


def table_kernel(place_ref, base_ref, table_ref):
    f_dev, width = table_ref.shape[1:]
    coarse = base_ref.shape[1] - FINE
    start = place_ref[0] * (f_dev // FINE)
    for block in range(0, width, BLOCK):
        lags = slice(block, block + BLOCK)
        fine_cos = base_ref[0, coarse:, lags]
        fine_sin = base_ref[1, coarse:, lags]

        def body(step, carry):
            first = pl.multiple_of(start + step * SUBLANES, SUBLANES)
            coarse_cos = base_ref[0, pl.ds(first, SUBLANES), lags]
            coarse_sin = base_ref[1, pl.ds(first, SUBLANES), lags]
            for n in range(SUBLANES):
                cos_a, sin_a = coarse_cos[n:n + 1], coarse_sin[n:n + 1]
                rows = pl.ds(pl.multiple_of((step * SUBLANES + n) * FINE, FINE), FINE)
                table_ref[0, rows, lags], table_ref[1, rows, lags] = split(cos_a * fine_cos - sin_a * fine_sin)
                table_ref[2, rows, lags], table_ref[3, rows, lags] = split(cos_a * fine_sin + sin_a * fine_cos)
            return carry

        lax.fori_loop(0, f_dev // (FINE * SUBLANES), body, 0)


def cross_tile(base_ref, partner_ref, lanes):
    w_dev, _, ch, _ = base_ref.shape
    real = [None] * ch
    imag = [None] * ch
    for w in range(w_dev):
        partner_re = partner_ref[w, 0, :, lanes].astype(jnp.float32)
        partner_im = partner_ref[w, 1, :, lanes].astype(jnp.float32)
        for i in range(ch):
            base_re = base_ref[w, 0, i:i + 1, lanes]
            base_im = base_ref[w, 1, i:i + 1, lanes]
            re = base_re * partner_re + base_im * partner_im
            im = base_im * partner_re - base_re * partner_im
            real[i] = re if w == 0 else real[i] + re
            imag[i] = im if w == 0 else imag[i] + im
    return real, imag


def pairs_kernel(n_partners, n_win, n_freq, place_ref, base_ref, *refs):
    partner_refs = refs[:n_partners]
    twist_ref, table_ref = refs[n_partners:n_partners + 2]
    out_refs = refs[-2 - n_freq:-2]
    rows_ref, sums_ref = refs[-2:]
    ch, f_dev = base_ref.shape[2:]
    pairs = ch * ch
    groups = n_win * n_freq
    width = out_refs[0].shape[-1]
    freq, win = place_ref[0], place_ref[1]
    dot = functools.partial(jnp.dot, preferred_element_type=jnp.float32)
    for k, partner_ref in enumerate(partner_refs):

        def body(tile, carry):
            lanes = pl.ds(pl.multiple_of(tile * LANES, LANES), LANES)
            real, imag = cross_tile(base_ref, partner_ref, lanes)
            cos = twist_ref[freq, 0:1, lanes]
            sin = twist_ref[freq, 1:2, lanes]
            for i in range(0, ch, 2):
                re = jnp.concatenate(real[i:i + 2], axis=0)
                im = jnp.concatenate(imag[i:i + 2], axis=0)
                for part, value in enumerate((re * cos + im * sin, im * cos - re * sin)):
                    high, low = split(value)
                    rows_ref[part, i * ch:(i + 2) * ch, lanes] = high
                    rows_ref[part, pairs + i * ch:pairs + (i + 2) * ch, lanes] = low
            return carry

        lax.fori_loop(0, f_dev // LANES, body, 0)
        for part in range(2):
            both = dot(rows_ref[part], table_ref[2 * part])
            sums_ref[part] = both[:pairs] + both[pairs:] + dot(rows_ref[part, :pairs], table_ref[2 * part + 1])
        for turn_freq, out_ref in enumerate(out_refs):
            for turn_win in range(n_win):
                owner = (win + turn_win) % n_win * n_freq + (freq + turn_freq) % n_freq
                upper = owner >= groups // 2
                block = jnp.where(upper, owner - groups // 2, groups // 2 - 1 - owner)
                sign = jnp.where(upper, -1.0, 1.0)
                lags = pl.ds(pl.multiple_of(block * width, LANES), width)
                out_ref[k, turn_win] = sums_ref[0, :, lags] + sign * sums_ref[1, :, lags]


def add_kernel(n_parts, *refs):
    for turn, out_ref in enumerate(refs[n_parts:]):
        total = refs[0][:, turn]
        for ref in refs[1:n_parts]:
            total = total + ref[:, turn]
        out_ref[...] = total.astype(out_ref.dtype)


def total_kernel(n_parts, *refs):
    out_ref = refs[-1]
    total = refs[0][...]
    for ref in refs[1:n_parts]:
        total = total + ref[...].astype(jnp.float32)
    start = 0
    for ref in refs[n_parts:-1]:
        out_ref[start:start + ref.shape[0]] = ref[...].astype(out_ref.dtype)
        start += ref.shape[0]
    out_ref[start:] = total.astype(out_ref.dtype)


def reverse_lanes(value):
    backward = LANES - 1 - lax.broadcasted_iota(jnp.int32, (value.shape[0], LANES), 1)
    pieces = [
        jnp.take_along_axis(value[:, start:start + LANES], backward, axis=1, mode="promise_in_bounds")
        for start in range(0, value.shape[1], LANES)
    ]
    return jnp.concatenate(pieces[::-1], axis=1)


def combine_kernel(scale, groups, n_freq, mask_ref, place_ref, *refs):
    out_ref = refs[-1]
    ch = out_ref.shape[0]
    lower = place_ref[1] * n_freq + place_ref[0] < groups // 2
    k = 0
    for ref in refs[:-1]:
        for n in range(ref.shape[0]):
            total = ref[n].astype(jnp.float32)
            total = jnp.where(lower, reverse_lanes(total), total)
            for i in range(ch):
                factor = mask_ref[i, k].astype(jnp.float32) * scale
                out_ref[i, k] = total[i * ch:(i + 1) * ch] * factor
            k += 1


VMEM = pl.BlockSpec(memory_space=pltpu.VMEM)
SMEM = pl.BlockSpec(memory_space=pltpu.SMEM)


def local(spectra, keep, pair_mask):
    w_dev, _, ch, f_dev = spectra.shape
    reach = pair_mask.shape[1] - 1
    n_chan, n_win, n_freq = (lax.axis_size(a) for a in ("chan", "win", "freq"))
    width = LAGS // (n_win * n_freq)
    n_bins = f_dev * n_freq
    params = pltpu.CompilerParams(vmem_limit_bytes=VMEM_LIMIT)
    freq = lax.axis_index("freq")

    places = jnp.stack([freq, lax.axis_index("win")]).astype(jnp.int32)

    def cost(flops, size):
        return pl.CostEstimate(flops=flops, bytes_accessed=size, transcendentals=0)

    raw = from_behind(spectra, "chan", -1)
    power, copied = pl.pallas_call(
        power_kernel,
        out_shape=[
            jax.ShapeDtypeStruct((w_dev, ch, 1), jnp.float32),
            jax.ShapeDtypeStruct(spectra.shape, spectra.dtype),
        ],
        in_specs=[VMEM], out_specs=[VMEM] * 2, compiler_params=params, cost_estimate=cost(0, 2 ** 22),
    )(spectra)
    own_power, next_power = [], []
    for turn in range(1, n_freq):
        route = [(f, (f + turn) % n_freq) for f in range(n_freq)]
        own_power.append(lax.ppermute(power, "freq", route))
        route = [(c * n_freq + f, (c - 1) * n_freq + to) for c in range(1, n_chan) for f, to in route]
        next_power.append(lax.ppermute(power, ("chan", "freq"), route))

    half_lags = 2 * np.arange(LAGS // 2) + 1
    coarse = phases(np.arange(0, n_bins, FINE), half_lags)
    fine = phases(F_LO + np.arange(FINE), half_lags)
    table = pl.pallas_call(
        table_kernel,
        out_shape=jax.ShapeDtypeStruct((4, f_dev, LAGS // 2), jnp.bfloat16),
        in_specs=[SMEM, VMEM], out_specs=VMEM, compiler_params=params, cost_estimate=cost(0, 2 ** 23),
    )(places, jnp.asarray(np.concatenate([coarse, fine], axis=1)))
    twist = phases(F_LO + np.arange(n_bins), np.ones(1)).reshape(2, n_freq, f_dev)
    twist = jnp.asarray(np.moveaxis(twist, 0, 1))

    def whiten(block, others):
        return pl.pallas_call(
            functools.partial(whiten_kernel, n_bins),
            out_shape=jax.ShapeDtypeStruct(block.shape, jnp.bfloat16),
            in_specs=[VMEM] * (1 + len(others)), out_specs=VMEM, compiler_params=params,
        )(block, *others)

    def kept(block):
        return pl.pallas_call(
            keep_kernel,
            out_shape=jax.ShapeDtypeStruct(block.shape, jnp.float32),
            in_specs=[SMEM, VMEM], out_specs=VMEM, compiler_params=params,
        )(keep, block)

    def pairs(base, partners):
        return pl.pallas_call(
            functools.partial(pairs_kernel, len(partners), n_win, n_freq),
            out_shape=[jax.ShapeDtypeStruct((len(partners), n_win, ch * ch, width), jnp.float32)] * n_freq,
            in_specs=[SMEM] + [VMEM] * (3 + len(partners)), out_specs=[VMEM] * n_freq,
            scratch_shapes=[
                pltpu.VMEM((2, 2 * ch * ch, f_dev), jnp.bfloat16),
                pltpu.VMEM((2, ch * ch, LAGS // 2), jnp.float32),
            ],
            compiler_params=params,
            cost_estimate=cost(2 ** 33, 2 ** 22),
        )(places, base, *partners, twist, table)

    def turns(parts, axis, size):
        received = [parts[0]]
        for turn in range(1, size):
            route = [(g, (g + turn) % size) for g in range(size)]
            received.append(lax.ppermute(parts[turn], axis, route))
        return received

    def reduce(parts, before, dtype):
        n = parts[0].shape[0]
        kinds = [jnp.float32] + [jnp.bfloat16] * (n_win - 1)
        sums = pl.pallas_call(
            functools.partial(add_kernel, n_freq),
            out_shape=[jax.ShapeDtypeStruct((n, ch * ch, width), kind) for kind in kinds],
            in_specs=[VMEM] * n_freq, out_specs=[VMEM] * n_win, compiler_params=params,
        )(*turns(parts, "freq", n_freq))
        n += sum(part.shape[0] for part in before)
        return pl.pallas_call(
            functools.partial(total_kernel, n_win),
            out_shape=jax.ShapeDtypeStruct((n, ch * ch, width), dtype),
            in_specs=[VMEM] * (n_win + len(before)), out_specs=VMEM, compiler_params=params,
        )(*turns(sums, "win", n_win), *before)

    white = whiten(copied, own_power)
    above = from_behind(white, "chan", 1)
    raw, table, white = lax.optimization_barrier((raw, table, white))
    moving = whiten(raw, next_power)
    parts = pairs(kept(white), [white, moving])
    base = kept(above)
    finished = []
    for step in range(1, reach - 1):
        arrived = from_behind(moving, "chan", -1)
        finished.append(reduce(pairs(base, [moving]), [], jnp.float32))
        if step == 1:
            near = reduce(parts, [], jnp.float32)
            arrived, near, finished = lax.optimization_barrier((arrived, near, finished))
        moving = arrived
    shipped = reduce(pairs(base, [moving]), finished, jnp.bfloat16)
    shipped = from_behind(shipped, "chan", -1)
    scale = 1.0 / math.sqrt(w_dev * n_win * n_bins)
    return pl.pallas_call(
        functools.partial(combine_kernel, scale, n_win * n_freq, n_freq),
        out_shape=jax.ShapeDtypeStruct((ch, reach + 1, ch, width), jnp.float32),
        in_specs=[SMEM] * 2 + [VMEM] * 2, out_specs=VMEM, compiler_params=params,
    )(pair_mask, places, near, shipped)


def solution(mesh):
    in_specs = (
        P("win", None, ("fibre", "chan"), "freq"),
        P(("fibre", "win")),
        P(("fibre", "chan"), None),
    )
    out_specs = P(("fibre", "chan"), None, None, ("win", "freq"))
    return jax.shard_map(local, mesh=mesh, in_specs=in_specs, out_specs=out_specs, check_vma=False)
```

```python
import functools
import math

import jax
import jax.numpy as jnp
import numpy as np
from jax import lax
from jax.experimental import pallas as pl
from jax.experimental.pallas import tpu as pltpu
from jax.sharding import PartitionSpec as P

LAGS = 1024
F_LO = 60
NSAMP = 15000
EPS = 1e-06
LANES = 128
SUBLANES = 8
FINE = 32
BLOCK = 256
VMEM_LIMIT = 16 * 1024 * 1024


def from_behind(block, axis, distance):
    devices = range(lax.axis_size(axis))
    route = [(i - distance, i) for i in devices if i - distance in devices]
    return lax.ppermute(block, axis, route)


def phases(bins, half_lags):
    turns = np.remainder(np.asarray(bins, np.int64)[:, None] * np.asarray(half_lags, np.int64)[None, :], 2 * NSAMP)
    angle = turns * (math.pi / NSAMP)
    return np.stack([np.cos(angle), np.sin(angle)]).astype(np.float32)


def split(value):
    high = value.astype(jnp.bfloat16)
    return high, (value - high.astype(jnp.float32)).astype(jnp.bfloat16)


def bin_power(x):
    x = x.astype(jnp.float32)
    return jnp.sum(x[0] * x[0] + x[1] * x[1], axis=-1, keepdims=True)


def power_kernel(x_ref, power_ref, copy_ref):
    for w in range(x_ref.shape[0]):
        x = x_ref[w]
        power_ref[w] = bin_power(x)
        copy_ref[w] = x


def whiten_kernel(n_bins, x_ref, *refs):
    out_ref = refs[-1]
    for w in range(x_ref.shape[0]):
        power = bin_power(x_ref[w])
        for ref in refs[:-1]:
            power = power + ref[w]
        scale = lax.rsqrt(power / n_bins + EPS)
        for part in range(2):
            out_ref[w, part] = (x_ref[w, part].astype(jnp.float32) * scale).astype(jnp.bfloat16)


def keep_kernel(keep_ref, white_ref, out_ref):
    for w in range(white_ref.shape[0]):
        out_ref[w] = white_ref[w].astype(jnp.float32) * keep_ref[w, :, :, 0:1]


def table_kernel(base_ref, table_ref):
    f_dev, width = table_ref.shape[1:]
    coarse = base_ref.shape[1] - FINE
    start = lax.axis_index("freq") * (f_dev // FINE)
    for block in range(0, width, BLOCK):
        lags = slice(block, block + BLOCK)
        fine_cos = base_ref[0, coarse:, lags]
        fine_sin = base_ref[1, coarse:, lags]

        def body(step, carry):
            first = pl.multiple_of(start + step * SUBLANES, SUBLANES)
            coarse_cos = base_ref[0, pl.ds(first, SUBLANES), lags]
            coarse_sin = base_ref[1, pl.ds(first, SUBLANES), lags]
            for n in range(SUBLANES):
                cos_a, sin_a = coarse_cos[n:n + 1], coarse_sin[n:n + 1]
                rows = pl.ds(pl.multiple_of((step * SUBLANES + n) * FINE, FINE), FINE)
                table_ref[0, rows, lags], table_ref[1, rows, lags] = split(cos_a * fine_cos - sin_a * fine_sin)
                table_ref[2, rows, lags], table_ref[3, rows, lags] = split(cos_a * fine_sin + sin_a * fine_cos)
            return carry

        lax.fori_loop(0, f_dev // (FINE * SUBLANES), body, 0)


def cross_tile(base_ref, partner_ref, lanes):
    w_dev, _, ch, _ = base_ref.shape
    real = [None] * ch
    imag = [None] * ch
    for w in range(w_dev):
        partner_re = partner_ref[w, 0, :, lanes].astype(jnp.float32)
        partner_im = partner_ref[w, 1, :, lanes].astype(jnp.float32)
        for i in range(ch):
            base_re = base_ref[w, 0, i:i + 1, lanes]
            base_im = base_ref[w, 1, i:i + 1, lanes]
            re = base_re * partner_re + base_im * partner_im
            im = base_im * partner_re - base_re * partner_im
            real[i] = re if w == 0 else real[i] + re
            imag[i] = im if w == 0 else imag[i] + im
    return real, imag


def pairs_kernel(n_partners, n_win, n_freq, base_ref, *refs):
    partner_refs = refs[:n_partners]
    twist_ref, table_ref = refs[n_partners:n_partners + 2]
    out_refs = refs[-2 - n_freq:-2]
    rows_ref, sums_ref = refs[-2:]
    ch, f_dev = base_ref.shape[2:]
    pairs = ch * ch
    groups = n_win * n_freq
    width = out_refs[0].shape[-1]
    freq, win = lax.axis_index("freq"), lax.axis_index("win")
    dot = functools.partial(jnp.dot, preferred_element_type=jnp.float32)
    for k, partner_ref in enumerate(partner_refs):

        def body(tile, carry):
            lanes = pl.ds(pl.multiple_of(tile * LANES, LANES), LANES)
            real, imag = cross_tile(base_ref, partner_ref, lanes)
            cos = twist_ref[freq, 0:1, lanes]
            sin = twist_ref[freq, 1:2, lanes]
            for i in range(0, ch, 2):
                re = jnp.concatenate(real[i:i + 2], axis=0)
                im = jnp.concatenate(imag[i:i + 2], axis=0)
                for part, value in enumerate((re * cos + im * sin, im * cos - re * sin)):
                    high, low = split(value)
                    rows_ref[part, i * ch:(i + 2) * ch, lanes] = high
                    rows_ref[part, pairs + i * ch:pairs + (i + 2) * ch, lanes] = low
            return carry

        lax.fori_loop(0, f_dev // LANES, body, 0)
        for part in range(2):
            both = dot(rows_ref[part], table_ref[2 * part])
            sums_ref[part] = both[:pairs] + both[pairs:] + dot(rows_ref[part, :pairs], table_ref[2 * part + 1])
        for turn_freq, out_ref in enumerate(out_refs):
            for turn_win in range(n_win):
                owner = (win + turn_win) % n_win * n_freq + (freq + turn_freq) % n_freq
                upper = owner >= groups // 2
                block = jnp.where(upper, owner - groups // 2, groups // 2 - 1 - owner)
                sign = jnp.where(upper, -1.0, 1.0)
                lags = pl.ds(pl.multiple_of(block * width, LANES), width)
                out_ref[k, turn_win] = sums_ref[0, :, lags] + sign * sums_ref[1, :, lags]


def add_kernel(n_parts, n_before, *refs):
    parts, befores, out_refs = refs[:n_parts], refs[n_parts:n_parts + n_before], refs[n_parts + n_before:]
    for turn, out_ref in enumerate(out_refs):
        start = 0
        for before in befores:
            out_ref[start:start + before.shape[0]] = before[:, turn].astype(out_ref.dtype)
            start += before.shape[0]
        total = parts[0][:, turn]
        for ref in parts[1:]:
            total = total + ref[:, turn]
        out_ref[start:] = total.astype(out_ref.dtype)


def plain_add_kernel(*refs):
    total = refs[0][...]
    for ref in refs[1:-1]:
        total = total + ref[...]
    refs[-1][...] = total


def reverse_lanes(value):
    backward = LANES - 1 - lax.broadcasted_iota(jnp.int32, (value.shape[0], LANES), 1)
    pieces = [
        jnp.take_along_axis(value[:, start:start + LANES], backward, axis=1, mode="promise_in_bounds")
        for start in range(0, value.shape[1], LANES)
    ]
    return jnp.concatenate(pieces[::-1], axis=1)


def combine_kernel(n_win, n_freq, factor_ref, *refs):
    out_ref = refs[-1]
    ch = out_ref.shape[0]
    lower = lax.axis_index("win") * n_freq + lax.axis_index("freq") < n_win * n_freq // 2
    k = 0
    for first in range(0, len(refs) - 1, n_win):
        parts = refs[first:first + n_win]
        for n in range(parts[0].shape[0]):
            total = parts[0][n].astype(jnp.float32)
            for ref in parts[1:]:
                total = total + ref[n].astype(jnp.float32)
            total = jnp.where(lower, reverse_lanes(total), total) * factor_ref[k]
            for i in range(ch):
                out_ref[i, k] = total[i * ch:(i + 1) * ch]
            k += 1


VMEM = pl.BlockSpec(memory_space=pltpu.VMEM)


def local(spectra, keep, pair_mask):
    w_dev, _, ch, f_dev = spectra.shape
    reach = pair_mask.shape[1] - 1
    n_chan, n_win, n_freq = (lax.axis_size(a) for a in ("chan", "win", "freq"))
    width = LAGS // (n_win * n_freq)
    n_bins = f_dev * n_freq
    params = pltpu.CompilerParams(vmem_limit_bytes=VMEM_LIMIT)


    def cost(flops, size):
        return pl.CostEstimate(flops=flops, bytes_accessed=size, transcendentals=0)

    raw = from_behind(spectra, "chan", -1)
    power, copied = pl.pallas_call(
        power_kernel,
        out_shape=[
            jax.ShapeDtypeStruct((w_dev, ch, 1), jnp.float32),
            jax.ShapeDtypeStruct(spectra.shape, spectra.dtype),
        ],
        in_specs=[VMEM], out_specs=[VMEM] * 2, compiler_params=params, cost_estimate=cost(0, 2 ** 22),
    )(spectra)
    own_power, next_power = [], []
    for turn in range(1, n_freq):
        route = [(f, (f + turn) % n_freq) for f in range(n_freq)]
        own_power.append(lax.ppermute(power, "freq", route))
        route = [(c * n_freq + f, (c - 1) * n_freq + to) for c in range(1, n_chan) for f, to in route]
        next_power.append(lax.ppermute(power, ("chan", "freq"), route))

    half_lags = 2 * np.arange(LAGS // 2) + 1
    coarse = phases(np.arange(0, n_bins, FINE), half_lags)
    fine = phases(F_LO + np.arange(FINE), half_lags)
    table = pl.pallas_call(
        table_kernel,
        out_shape=jax.ShapeDtypeStruct((4, f_dev, LAGS // 2), jnp.bfloat16),
        in_specs=[VMEM], out_specs=VMEM, compiler_params=params, cost_estimate=cost(0, 2 ** 23),
    )(jnp.asarray(np.concatenate([coarse, fine], axis=1)))
    twist = phases(F_LO + np.arange(n_bins), np.ones(1)).reshape(2, n_freq, f_dev)
    twist = jnp.asarray(np.moveaxis(twist, 0, 1))

    def whiten(block, others):
        return pl.pallas_call(
            functools.partial(whiten_kernel, n_bins),
            out_shape=jax.ShapeDtypeStruct(block.shape, jnp.bfloat16),
            in_specs=[VMEM] * (1 + len(others)), out_specs=VMEM, compiler_params=params,
        )(block, *others)

    kept_windows = jnp.broadcast_to(keep.astype(jnp.float32)[:, None, None, None], (w_dev, 1, 1, LANES))

    def kept(block):
        return pl.pallas_call(
            keep_kernel,
            out_shape=jax.ShapeDtypeStruct(block.shape, jnp.float32),
            in_specs=[VMEM] * 2, out_specs=VMEM, compiler_params=params,
        )(kept_windows, block)

    def pairs(base, partners):
        return pl.pallas_call(
            functools.partial(pairs_kernel, len(partners), n_win, n_freq),
            out_shape=[jax.ShapeDtypeStruct((len(partners), n_win, ch * ch, width), jnp.float32)] * n_freq,
            in_specs=[VMEM] * (3 + len(partners)), out_specs=[VMEM] * n_freq,
            scratch_shapes=[
                pltpu.VMEM((2, 2 * ch * ch, f_dev), jnp.bfloat16),
                pltpu.VMEM((2, ch * ch, LAGS // 2), jnp.float32),
            ],
            compiler_params=params,
            cost_estimate=cost(2 ** 33, 2 ** 22),
        )(base, *partners, twist, table)

    def turns(parts, axis, size):
        received = [parts[0]]
        for turn in range(1, size):
            route = [(g, (g + turn) % size) for g in range(size)]
            received.append(lax.ppermute(parts[turn], axis, route))
        return received

    def sum_bins(parts):
        return pl.pallas_call(
            plain_add_kernel,
            out_shape=jax.ShapeDtypeStruct(parts[0].shape, jnp.float32),
            in_specs=[VMEM] * n_freq, out_specs=VMEM, compiler_params=params,
        )(*turns(parts, "freq", n_freq))

    def split_windows(parts, before, kinds):
        n = sum(part.shape[0] for part in before) + parts[0].shape[0]
        return pl.pallas_call(
            functools.partial(add_kernel, n_freq, len(before)),
            out_shape=[jax.ShapeDtypeStruct((n, ch * ch, width), kind) for kind in kinds],
            in_specs=[VMEM] * (n_freq + len(before)), out_specs=[VMEM] * n_win, compiler_params=params,
        )(*turns(parts, "freq", n_freq), *before)

    white = whiten(copied, own_power)
    above = from_behind(white, "chan", 1)
    raw, table, white = lax.optimization_barrier((raw, table, white))
    moving = whiten(raw, next_power)
    parts = pairs(kept(white), [white, moving])
    base = kept(above)
    before = []
    for step in range(1, reach - 1):
        arrived = from_behind(moving, "chan", -1)
        remote = sum_bins(pairs(base, [moving]))
        if step == 1:
            sums = split_windows(parts, [], [jnp.float32] + [jnp.bfloat16] * (n_win - 1))
            arrived, sums, remote = lax.optimization_barrier((arrived, sums, remote))
        before.append(remote)
        moving = arrived
    shipped = split_windows(pairs(base, [moving]), before, [jnp.bfloat16] * n_win)
    received = turns(sums, "win", n_win)
    received.append(from_behind(shipped[0], "chan", -1))
    for turn in range(1, n_win):
        route = [
            (c * n_win + w, (c - 1) * n_win + (w + turn) % n_win) for c in range(1, n_chan) for w in range(n_win)
        ]
        received.append(lax.ppermute(shipped[turn], ("chan", "win"), route))
    scale = 1.0 / math.sqrt(w_dev * n_win * n_bins)
    factors = jnp.repeat(pair_mask.T.astype(jnp.float32) * scale, ch, axis=1)[..., None]
    return pl.pallas_call(
        functools.partial(combine_kernel, n_win, n_freq),
        out_shape=jax.ShapeDtypeStruct((ch, reach + 1, ch, width), jnp.float32),
        in_specs=[VMEM] * (1 + len(received)), out_specs=VMEM, compiler_params=params,
    )(factors, *received)


def solution(mesh):
    in_specs = (
        P("win", None, ("fibre", "chan"), "freq"),
        P(("fibre", "win")),
        P(("fibre", "chan"), None),
    )
    out_specs = P(("fibre", "chan"), None, None, ("win", "freq"))
    return jax.shard_map(local, mesh=mesh, in_specs=in_specs, out_specs=out_specs, check_vma=False)
```

```python
import functools
import math

import jax
import jax.numpy as jnp
import numpy as np
from jax import lax
from jax.experimental import pallas as pl
from jax.experimental.pallas import tpu as pltpu
from jax.sharding import PartitionSpec as P

LAGS = 1024
F_LO = 60
NSAMP = 15000
EPS = 1e-06
LANES = 128
SUBLANES = 8
FINE = 32
BLOCK = 256
VMEM_LIMIT = 16 * 1024 * 1024


def from_behind(block, axis, distance):
    devices = range(lax.axis_size(axis))
    route = [(i - distance, i) for i in devices if i - distance in devices]
    return lax.ppermute(block, axis, route)


def phases(bins, half_lags):
    turns = np.remainder(np.asarray(bins, np.int64)[:, None] * np.asarray(half_lags, np.int64)[None, :], 2 * NSAMP)
    angle = turns * (math.pi / NSAMP)
    return np.stack([np.cos(angle), np.sin(angle)]).astype(np.float32)


def split(value):
    high = value.astype(jnp.bfloat16)
    return high, (value - high.astype(jnp.float32)).astype(jnp.bfloat16)


def bin_power(x):
    x = x.astype(jnp.float32)
    return jnp.sum(x[0] * x[0] + x[1] * x[1], axis=-1, keepdims=True)


def power_kernel(x_ref, power_ref, copy_ref):
    for w in range(x_ref.shape[0]):
        x = x_ref[w]
        power_ref[w] = bin_power(x)
        copy_ref[w] = x


def whiten_kernel(n_bins, x_ref, *refs):
    out_ref = refs[-1]
    for w in range(x_ref.shape[0]):
        power = bin_power(x_ref[w])
        for ref in refs[:-1]:
            power = power + ref[w]
        scale = lax.rsqrt(power / n_bins + EPS)
        for part in range(2):
            out_ref[w, part] = (x_ref[w, part].astype(jnp.float32) * scale).astype(jnp.bfloat16)


def keep_kernel(keep_ref, white_ref, out_ref):
    for w in range(white_ref.shape[0]):
        out_ref[w] = white_ref[w].astype(jnp.float32) * keep_ref[w, :, :, 0:1]


def table_kernel(base_ref, table_ref):
    f_dev, width = table_ref.shape[1:]
    coarse = base_ref.shape[1] - FINE
    start = lax.axis_index("freq") * (f_dev // FINE)
    for block in range(0, width, BLOCK):
        lags = slice(block, block + BLOCK)
        fine_cos = base_ref[0, coarse:, lags]
        fine_sin = base_ref[1, coarse:, lags]

        def body(step, carry):
            first = pl.multiple_of(start + step * SUBLANES, SUBLANES)
            coarse_cos = base_ref[0, pl.ds(first, SUBLANES), lags]
            coarse_sin = base_ref[1, pl.ds(first, SUBLANES), lags]
            for n in range(SUBLANES):
                cos_a, sin_a = coarse_cos[n:n + 1], coarse_sin[n:n + 1]
                rows = pl.ds(pl.multiple_of((step * SUBLANES + n) * FINE, FINE), FINE)
                table_ref[0, rows, lags], table_ref[1, rows, lags] = split(cos_a * fine_cos - sin_a * fine_sin)
                table_ref[2, rows, lags], table_ref[3, rows, lags] = split(cos_a * fine_sin + sin_a * fine_cos)
            return carry

        lax.fori_loop(0, f_dev // (FINE * SUBLANES), body, 0)


def cross_tile(base_ref, partner_ref, lanes):
    w_dev, _, ch, _ = base_ref.shape
    real = [None] * ch
    imag = [None] * ch
    for w in range(w_dev):
        partner_re = partner_ref[w, 0, :, lanes].astype(jnp.float32)
        partner_im = partner_ref[w, 1, :, lanes].astype(jnp.float32)
        for i in range(ch):
            base_re = base_ref[w, 0, i:i + 1, lanes]
            base_im = base_ref[w, 1, i:i + 1, lanes]
            re = base_re * partner_re + base_im * partner_im
            im = base_im * partner_re - base_re * partner_im
            real[i] = re if w == 0 else real[i] + re
            imag[i] = im if w == 0 else imag[i] + im
    return real, imag


def pairs_kernel(n_partners, n_win, n_freq, base_ref, *refs):
    partner_refs = refs[:n_partners]
    twist_ref, table_ref = refs[n_partners:n_partners + 2]
    out_refs = refs[-2 - n_freq:-2]
    rows_ref, sums_ref = refs[-2:]
    ch, f_dev = base_ref.shape[2:]
    pairs = ch * ch
    groups = n_win * n_freq
    width = out_refs[0].shape[-1]
    freq, win = lax.axis_index("freq"), lax.axis_index("win")
    dot = functools.partial(jnp.dot, preferred_element_type=jnp.float32)
    for k, partner_ref in enumerate(partner_refs):

        def body(tile, carry):
            lanes = pl.ds(pl.multiple_of(tile * LANES, LANES), LANES)
            real, imag = cross_tile(base_ref, partner_ref, lanes)
            cos = twist_ref[freq, 0:1, lanes]
            sin = twist_ref[freq, 1:2, lanes]
            for i in range(0, ch, 2):
                re = jnp.concatenate(real[i:i + 2], axis=0)
                im = jnp.concatenate(imag[i:i + 2], axis=0)
                for part, value in enumerate((re * cos + im * sin, im * cos - re * sin)):
                    high, low = split(value)
                    rows_ref[part, i * ch:(i + 2) * ch, lanes] = high
                    rows_ref[part, pairs + i * ch:pairs + (i + 2) * ch, lanes] = low
            return carry

        lax.fori_loop(0, f_dev // LANES, body, 0)
        for part in range(2):
            both = dot(rows_ref[part], table_ref[2 * part])
            sums_ref[part] = both[:pairs] + both[pairs:] + dot(rows_ref[part, :pairs], table_ref[2 * part + 1])
        for turn_freq, out_ref in enumerate(out_refs):
            for turn_win in range(n_win):
                owner = (win + turn_win) % n_win * n_freq + (freq + turn_freq) % n_freq
                upper = owner >= groups // 2
                block = jnp.where(upper, owner - groups // 2, groups // 2 - 1 - owner)
                sign = jnp.where(upper, -1.0, 1.0)
                lags = pl.ds(pl.multiple_of(block * width, LANES), width)
                out_ref[k, turn_win] = sums_ref[0, :, lags] + sign * sums_ref[1, :, lags]


def add_kernel(n_parts, n_before, *refs):
    parts, befores, out_refs = refs[:n_parts], refs[n_parts:n_parts + n_before], refs[n_parts + n_before:]
    for turn, out_ref in enumerate(out_refs):
        start = 0
        for before in befores:
            out_ref[start:start + before.shape[0]] = before[:, turn].astype(out_ref.dtype)
            start += before.shape[0]
        total = parts[0][:, turn]
        for ref in parts[1:]:
            total = total + ref[:, turn]
        out_ref[start:] = total.astype(out_ref.dtype)


def plain_add_kernel(*refs):
    total = refs[0][...]
    for ref in refs[1:-1]:
        total = total + ref[...]
    refs[-1][...] = total


def reverse_lanes(value):
    backward = LANES - 1 - lax.broadcasted_iota(jnp.int32, (value.shape[0], LANES), 1)
    pieces = [
        jnp.take_along_axis(value[:, start:start + LANES], backward, axis=1, mode="promise_in_bounds")
        for start in range(0, value.shape[1], LANES)
    ]
    return jnp.concatenate(pieces[::-1], axis=1)


def combine_kernel(n_win, n_freq, factor_ref, *refs):
    out_ref = refs[-1]
    ch = out_ref.shape[0]
    lower = lax.axis_index("win") * n_freq + lax.axis_index("freq") < n_win * n_freq // 2
    k = 0
    for first in range(0, len(refs) - 1, n_win):
        parts = refs[first:first + n_win]
        for n in range(parts[0].shape[0]):
            total = parts[0][n].astype(jnp.float32)
            for ref in parts[1:]:
                total = total + ref[n].astype(jnp.float32)
            total = jnp.where(lower, reverse_lanes(total), total) * factor_ref[k]
            for i in range(ch):
                out_ref[i, k] = total[i * ch:(i + 1) * ch]
            k += 1


VMEM = pl.BlockSpec(memory_space=pltpu.VMEM)


def local(spectra, keep, pair_mask):
    w_dev, _, ch, f_dev = spectra.shape
    reach = pair_mask.shape[1] - 1
    n_chan, n_win, n_freq = (lax.axis_size(a) for a in ("chan", "win", "freq"))
    width = LAGS // (n_win * n_freq)
    n_bins = f_dev * n_freq
    params = pltpu.CompilerParams(vmem_limit_bytes=VMEM_LIMIT)


    def cost(flops, size):
        return pl.CostEstimate(flops=flops, bytes_accessed=size, transcendentals=0)

    power, copied = pl.pallas_call(
        power_kernel,
        out_shape=[
            jax.ShapeDtypeStruct((w_dev, ch, 1), jnp.float32),
            jax.ShapeDtypeStruct(spectra.shape, spectra.dtype),
        ],
        in_specs=[VMEM], out_specs=[VMEM] * 2, compiler_params=params, cost_estimate=cost(ch, ch),
    )(spectra)
    own_power = []
    for turn in range(1, n_freq):
        route = [(f, (f + turn) % n_freq) for f in range(n_freq)]
        own_power.append(lax.ppermute(power, "freq", route))

    half_lags = 2 * np.arange(LAGS // 2) + 1
    coarse = phases(np.arange(0, n_bins, FINE), half_lags)
    fine = phases(F_LO + np.arange(FINE), half_lags)
    table = pl.pallas_call(
        table_kernel,
        out_shape=jax.ShapeDtypeStruct((4, f_dev, LAGS // 2), jnp.bfloat16),
        in_specs=[VMEM], out_specs=VMEM, compiler_params=params, cost_estimate=cost(ch, ch),
    )(jnp.asarray(np.concatenate([coarse, fine], axis=1)))
    twist = phases(F_LO + np.arange(n_bins), np.ones(1)).reshape(2, n_freq, f_dev)
    twist = jnp.asarray(np.moveaxis(twist, 0, 1))

    def whiten(block, others):
        return pl.pallas_call(
            functools.partial(whiten_kernel, n_bins),
            out_shape=jax.ShapeDtypeStruct(block.shape, jnp.bfloat16),
            in_specs=[VMEM] * (1 + len(others)), out_specs=VMEM, compiler_params=params,
        )(block, *others)

    kept_windows = jnp.broadcast_to(keep.astype(jnp.float32)[:, None, None, None], (w_dev, 1, 1, LANES))

    def kept(block):
        return pl.pallas_call(
            keep_kernel,
            out_shape=jax.ShapeDtypeStruct(block.shape, jnp.float32),
            in_specs=[VMEM] * 2, out_specs=VMEM, compiler_params=params,
        )(kept_windows, block)

    def pairs(base, partners):
        return pl.pallas_call(
            functools.partial(pairs_kernel, len(partners), n_win, n_freq),
            out_shape=[jax.ShapeDtypeStruct((len(partners), n_win, ch * ch, width), jnp.float32)] * n_freq,
            in_specs=[VMEM] * (3 + len(partners)), out_specs=[VMEM] * n_freq,
            scratch_shapes=[
                pltpu.VMEM((2, 2 * ch * ch, f_dev), jnp.bfloat16),
                pltpu.VMEM((2, ch * ch, LAGS // 2), jnp.float32),
            ],
            compiler_params=params,
            cost_estimate=cost(ch, ch),
        )(base, *partners, twist, table)

    def turns(parts, axis, size):
        received = [parts[0]]
        for turn in range(1, size):
            route = [(g, (g + turn) % size) for g in range(size)]
            received.append(lax.ppermute(parts[turn], axis, route))
        return received

    def sum_bins(parts):
        return pl.pallas_call(
            plain_add_kernel,
            out_shape=jax.ShapeDtypeStruct(parts[0].shape, jnp.float32),
            in_specs=[VMEM] * n_freq, out_specs=VMEM, compiler_params=params,
        )(*turns(parts, "freq", n_freq))

    def split_windows(parts, before, kinds):
        n = sum(part.shape[0] for part in before) + parts[0].shape[0]
        return pl.pallas_call(
            functools.partial(add_kernel, n_freq, len(before)),
            out_shape=[jax.ShapeDtypeStruct((n, ch * ch, width), kind) for kind in kinds],
            in_specs=[VMEM] * (n_freq + len(before)), out_specs=[VMEM] * n_win, compiler_params=params,
        )(*turns(parts, "freq", n_freq), *before)

    table, own_power = lax.optimization_barrier((table, own_power))
    white = whiten(copied, own_power)
    above = from_behind(white, "chan", 1)
    below = from_behind(white, "chan", -1)
    far = []
    for distance in range(2, reach):
        route = [(c + distance, c) for c in range(1, n_chan - distance)]
        far.append(lax.ppermute(white, "chan", route))
    own = kept(white)
    first = sum_bins(pairs(own, [white]))
    below, first = lax.optimization_barrier((below, first))
    base = kept(above)
    sums = split_windows(pairs(own, [below]), [first], [jnp.float32] + [jnp.bfloat16] * (n_win - 1))
    before = [sum_bins(pairs(base, [below]))]
    for block in far[:-1]:
        before.append(sum_bins(pairs(base, [block])))
    far, sums, before = lax.optimization_barrier((far[-1], sums, before))
    shipped = split_windows(pairs(base, [far]), before, [jnp.bfloat16] * n_win)
    received = turns(sums, "win", n_win)
    received.append(from_behind(shipped[0], "chan", -1))
    for turn in range(1, n_win):
        route = [
            (c * n_win + w, (c - 1) * n_win + (w + turn) % n_win) for c in range(1, n_chan) for w in range(n_win)
        ]
        received.append(lax.ppermute(shipped[turn], ("chan", "win"), route))
    scale = 1.0 / math.sqrt(w_dev * n_win * n_bins)
    factors = jnp.repeat(pair_mask.T.astype(jnp.float32) * scale, ch, axis=1)[..., None]
    return pl.pallas_call(
        functools.partial(combine_kernel, n_win, n_freq),
        out_shape=jax.ShapeDtypeStruct((ch, reach + 1, ch, width), jnp.float32),
        in_specs=[VMEM] * (1 + len(received)), out_specs=VMEM, compiler_params=params,
    )(factors, *received)


def solution(mesh):
    in_specs = (
        P("win", None, ("fibre", "chan"), "freq"),
        P(("fibre", "win")),
        P(("fibre", "chan"), None),
    )
    out_specs = P(("fibre", "chan"), None, None, ("win", "freq"))
    return jax.shard_map(local, mesh=mesh, in_specs=in_specs, out_specs=out_specs, check_vma=False)
```

```python
import functools
import math

import jax
import jax.numpy as jnp
import numpy as np
from jax import lax
from jax.experimental import pallas as pl
from jax.experimental.pallas import tpu as pltpu
from jax.sharding import PartitionSpec as P

LAGS = 1024
F_LO = 60
NSAMP = 15000
EPS = 1e-06
LANES = 128
SUBLANES = 8
FINE = 32
BLOCK = 256
VMEM_LIMIT = 16 * 1024 * 1024


def from_behind(block, axis, distance):
    devices = range(lax.axis_size(axis))
    route = [(i - distance, i) for i in devices if i - distance in devices]
    return lax.ppermute(block, axis, route)


def phases(bins, half_lags):
    turns = np.remainder(np.asarray(bins, np.int64)[:, None] * np.asarray(half_lags, np.int64)[None, :], 2 * NSAMP)
    angle = turns * (math.pi / NSAMP)
    return np.stack([np.cos(angle), np.sin(angle)]).astype(np.float32)


def split(value):
    high = value.astype(jnp.bfloat16)
    return high, (value - high.astype(jnp.float32)).astype(jnp.bfloat16)


def bin_power(x):
    x = x.astype(jnp.float32)
    return jnp.sum(x[0] * x[0] + x[1] * x[1], axis=-1, keepdims=True)


def power_kernel(x_ref, base_ref, power_ref, x_copy_ref, base_copy_ref):
    for w in range(x_ref.shape[0]):
        x = x_ref[w]
        power_ref[w] = bin_power(x)
        x_copy_ref[w] = x
    base_copy_ref[...] = base_ref[...]


def whiten_kernel(n_bins, x_ref, *refs):
    out_ref = refs[-1]
    for w in range(x_ref.shape[0]):
        power = bin_power(x_ref[w])
        for ref in refs[:-1]:
            power = power + ref[w]
        scale = lax.rsqrt(power / n_bins + EPS)
        for part in range(2):
            out_ref[w, part] = (x_ref[w, part].astype(jnp.float32) * scale).astype(jnp.bfloat16)


def keep_kernel(keep_ref, white_ref, out_ref):
    for w in range(white_ref.shape[0]):
        out_ref[w] = white_ref[w].astype(jnp.float32) * keep_ref[w, :, :, 0:1]


def table_kernel(base_ref, table_ref):
    f_dev, width = table_ref.shape[1:]
    coarse = base_ref.shape[1] - FINE
    start = lax.axis_index("freq") * (f_dev // FINE)
    for block in range(0, width, BLOCK):
        lags = slice(block, block + BLOCK)
        fine_cos = base_ref[0, coarse:, lags]
        fine_sin = base_ref[1, coarse:, lags]

        def body(step, carry):
            first = pl.multiple_of(start + step * SUBLANES, SUBLANES)
            coarse_cos = base_ref[0, pl.ds(first, SUBLANES), lags]
            coarse_sin = base_ref[1, pl.ds(first, SUBLANES), lags]
            for n in range(SUBLANES):
                cos_a, sin_a = coarse_cos[n:n + 1], coarse_sin[n:n + 1]
                rows = pl.ds(pl.multiple_of((step * SUBLANES + n) * FINE, FINE), FINE)
                table_ref[0, rows, lags], table_ref[1, rows, lags] = split(cos_a * fine_cos - sin_a * fine_sin)
                table_ref[2, rows, lags], table_ref[3, rows, lags] = split(cos_a * fine_sin + sin_a * fine_cos)
            return carry

        lax.fori_loop(0, f_dev // (FINE * SUBLANES), body, 0)


def cross_tile(base_ref, partner_ref, lanes):
    w_dev, _, ch, _ = base_ref.shape
    real = [None] * ch
    imag = [None] * ch
    for w in range(w_dev):
        partner_re = partner_ref[w, 0, :, lanes].astype(jnp.float32)
        partner_im = partner_ref[w, 1, :, lanes].astype(jnp.float32)
        for i in range(ch):
            base_re = base_ref[w, 0, i:i + 1, lanes]
            base_im = base_ref[w, 1, i:i + 1, lanes]
            re = base_re * partner_re + base_im * partner_im
            im = base_im * partner_re - base_re * partner_im
            real[i] = re if w == 0 else real[i] + re
            imag[i] = im if w == 0 else imag[i] + im
    return real, imag


def pairs_kernel(n_partners, n_win, n_freq, base_ref, *refs):
    partner_refs = refs[:n_partners]
    twist_ref, table_ref = refs[n_partners:n_partners + 2]
    before_refs = refs[n_partners + 2:-2 - n_freq]
    out_refs = refs[-2 - n_freq:-2]
    rows_ref, sums_ref = refs[-2:]
    done = out_refs[0].shape[0] - n_partners
    for before_ref, out_ref in zip(before_refs, out_refs):
        out_ref[:done] = before_ref[...]
    ch, f_dev = base_ref.shape[2:]
    pairs = ch * ch
    groups = n_win * n_freq
    width = out_refs[0].shape[-1]
    freq, win = lax.axis_index("freq"), lax.axis_index("win")
    dot = functools.partial(jnp.dot, preferred_element_type=jnp.float32)
    for k, partner_ref in enumerate(partner_refs):

        def body(tile, carry):
            lanes = pl.ds(pl.multiple_of(tile * LANES, LANES), LANES)
            real, imag = cross_tile(base_ref, partner_ref, lanes)
            cos = twist_ref[freq, 0:1, lanes]
            sin = twist_ref[freq, 1:2, lanes]
            for i in range(0, ch, 2):
                re = jnp.concatenate(real[i:i + 2], axis=0)
                im = jnp.concatenate(imag[i:i + 2], axis=0)
                for part, value in enumerate((re * cos + im * sin, im * cos - re * sin)):
                    high, low = split(value)
                    rows_ref[part, i * ch:(i + 2) * ch, lanes] = high
                    rows_ref[part, pairs + i * ch:pairs + (i + 2) * ch, lanes] = low
            return carry

        lax.fori_loop(0, f_dev // LANES, body, 0)
        for part in range(2):
            both = dot(rows_ref[part], table_ref[2 * part])
            sums_ref[part] = both[:pairs] + both[pairs:] + dot(rows_ref[part, :pairs], table_ref[2 * part + 1])
        for turn_freq, out_ref in enumerate(out_refs):
            for turn_win in range(n_win):
                owner = (win + turn_win) % n_win * n_freq + (freq + turn_freq) % n_freq
                upper = owner >= groups // 2
                block = jnp.where(upper, owner - groups // 2, groups // 2 - 1 - owner)
                sign = jnp.where(upper, -1.0, 1.0)
                lags = pl.ds(pl.multiple_of(block * width, LANES), width)
                out_ref[done + k, turn_win] = sums_ref[0, :, lags] + sign * sums_ref[1, :, lags]


def add_kernel(n_parts, n_before, *refs):
    parts, befores, out_refs = refs[:n_parts], refs[n_parts:n_parts + n_before], refs[n_parts + n_before:]
    for turn, out_ref in enumerate(out_refs):
        start = 0
        for before in befores:
            out_ref[start:start + before.shape[0]] = before[:, turn].astype(out_ref.dtype)
            start += before.shape[0]
        total = parts[0][:, turn]
        for ref in parts[1:]:
            total = total + ref[:, turn]
        out_ref[start:] = total.astype(out_ref.dtype)


def plain_add_kernel(*refs):
    total = refs[0][...]
    for ref in refs[1:-1]:
        total = total + ref[...]
    refs[-1][...] = total


def reverse_lanes(value):
    backward = LANES - 1 - lax.broadcasted_iota(jnp.int32, (value.shape[0], LANES), 1)
    pieces = [
        jnp.take_along_axis(value[:, start:start + LANES], backward, axis=1, mode="promise_in_bounds")
        for start in range(0, value.shape[1], LANES)
    ]
    return jnp.concatenate(pieces[::-1], axis=1)


def combine_kernel(n_win, n_freq, factor_ref, *refs):
    out_ref = refs[-1]
    ch = out_ref.shape[0]
    lower = lax.axis_index("win") * n_freq + lax.axis_index("freq") < n_win * n_freq // 2
    k = 0
    for first in range(0, len(refs) - 1, n_win):
        parts = refs[first:first + n_win]
        for n in range(parts[0].shape[0]):
            total = parts[0][n].astype(jnp.float32)
            for ref in parts[1:]:
                total = total + ref[n].astype(jnp.float32)
            total = jnp.where(lower, reverse_lanes(total), total) * factor_ref[k]
            for i in range(ch):
                out_ref[i, k] = total[i * ch:(i + 1) * ch]
            k += 1


VMEM = pl.BlockSpec(memory_space=pltpu.VMEM)


def local(spectra, keep, pair_mask):
    w_dev, _, ch, f_dev = spectra.shape
    reach = pair_mask.shape[1] - 1
    n_chan, n_win, n_freq = (lax.axis_size(a) for a in ("chan", "win", "freq"))
    width = LAGS // (n_win * n_freq)
    n_bins = f_dev * n_freq
    params = pltpu.CompilerParams(vmem_limit_bytes=VMEM_LIMIT)


    def cost(flops, size):
        return pl.CostEstimate(flops=flops, bytes_accessed=size, transcendentals=0)

    half_lags = 2 * np.arange(LAGS // 2) + 1
    coarse = phases(np.arange(0, n_bins, FINE), half_lags)
    fine = phases(F_LO + np.arange(FINE), half_lags)
    base = np.concatenate([coarse, fine], axis=1)
    power, copied, base = pl.pallas_call(
        power_kernel,
        out_shape=[
            jax.ShapeDtypeStruct((w_dev, ch, 1), jnp.float32),
            jax.ShapeDtypeStruct(spectra.shape, spectra.dtype),
            jax.ShapeDtypeStruct(base.shape, jnp.float32),
        ],
        in_specs=[VMEM] * 2, out_specs=[VMEM] * 3, compiler_params=params, cost_estimate=cost(ch, ch),
    )(spectra, jnp.asarray(base))
    own_power = []
    for turn in range(1, n_freq):
        route = [(f, (f + turn) % n_freq) for f in range(n_freq)]
        own_power.append(lax.ppermute(power, "freq", route))

    table = pl.pallas_call(
        table_kernel,
        out_shape=jax.ShapeDtypeStruct((4, f_dev, LAGS // 2), jnp.bfloat16),
        in_specs=[VMEM], out_specs=VMEM, compiler_params=params, cost_estimate=cost(ch, ch),
    )(base)
    twist = phases(F_LO + np.arange(n_bins), np.ones(1)).reshape(2, n_freq, f_dev)
    twist = jnp.asarray(np.moveaxis(twist, 0, 1))

    def whiten(block, others):
        return pl.pallas_call(
            functools.partial(whiten_kernel, n_bins),
            out_shape=jax.ShapeDtypeStruct(block.shape, jnp.bfloat16),
            in_specs=[VMEM] * (1 + len(others)), out_specs=VMEM, compiler_params=params,
        )(block, *others)

    kept_windows = jnp.broadcast_to(keep.astype(jnp.float32)[:, None, None, None], (w_dev, 1, 1, LANES))

    def kept(block):
        return pl.pallas_call(
            keep_kernel,
            out_shape=jax.ShapeDtypeStruct(block.shape, jnp.float32),
            in_specs=[VMEM] * 2, out_specs=VMEM, compiler_params=params,
        )(kept_windows, block)

    def pairs(base, partners, before=()):
        n = len(partners) + (before[0].shape[0] if before else 0)
        return pl.pallas_call(
            functools.partial(pairs_kernel, len(partners), n_win, n_freq),
            out_shape=[jax.ShapeDtypeStruct((n, n_win, ch * ch, width), jnp.float32)] * n_freq,
            in_specs=[VMEM] * (3 + len(partners) + len(before)), out_specs=[VMEM] * n_freq,
            scratch_shapes=[
                pltpu.VMEM((2, 2 * ch * ch, f_dev), jnp.bfloat16),
                pltpu.VMEM((2, ch * ch, LAGS // 2), jnp.float32),
            ],
            compiler_params=params,
            cost_estimate=cost(ch, ch),
        )(base, *partners, twist, table, *before)

    def turns(parts, axis, size):
        received = [parts[0]]
        for turn in range(1, size):
            route = [(g, (g + turn) % size) for g in range(size)]
            received.append(lax.ppermute(parts[turn], axis, route))
        return received

    def sum_bins(parts):
        return pl.pallas_call(
            plain_add_kernel,
            out_shape=jax.ShapeDtypeStruct(parts[0].shape, jnp.float32),
            in_specs=[VMEM] * n_freq, out_specs=VMEM, compiler_params=params,
        )(*turns(parts, "freq", n_freq))

    def split_windows(parts, before, kinds):
        n = sum(part.shape[0] for part in before) + parts[0].shape[0]
        return pl.pallas_call(
            functools.partial(add_kernel, n_freq, len(before)),
            out_shape=[jax.ShapeDtypeStruct((n, ch * ch, width), kind) for kind in kinds],
            in_specs=[VMEM] * (n_freq + len(before)), out_specs=[VMEM] * n_win, compiler_params=params,
        )(*turns(parts, "freq", n_freq), *before)

    table, own_power = lax.optimization_barrier((table, own_power))
    white = whiten(copied, own_power)
    above = from_behind(white, "chan", 1)
    below = from_behind(white, "chan", -1)
    far = []
    for distance in range(2, reach):
        route = [(c + distance, c) for c in range(1, n_chan - distance)]
        far.append(lax.ppermute(white, "chan", route))
    own = kept(white)
    first = pairs(own, [white])
    below, first = lax.optimization_barrier((below, first))
    base = kept(above)
    parts = pairs(own, [below], first)
    before = ()
    for block in [below] + far[:-1]:
        before = pairs(base, [block], before)
    far, parts, before = lax.optimization_barrier((far[-1], parts, before))
    sums = split_windows(parts, [], [jnp.float32] + [jnp.bfloat16] * (n_win - 1))
    shipped = split_windows(pairs(base, [far], before), [], [jnp.bfloat16] * n_win)
    received = turns(sums, "win", n_win)
    received.append(from_behind(shipped[0], "chan", -1))
    for turn in range(1, n_win):
        route = [
            (c * n_win + w, (c - 1) * n_win + (w + turn) % n_win) for c in range(1, n_chan) for w in range(n_win)
        ]
        received.append(lax.ppermute(shipped[turn], ("chan", "win"), route))
    scale = 1.0 / math.sqrt(w_dev * n_win * n_bins)
    factors = jnp.repeat(pair_mask.T.astype(jnp.float32) * scale, ch, axis=1)[..., None]
    return pl.pallas_call(
        functools.partial(combine_kernel, n_win, n_freq),
        out_shape=jax.ShapeDtypeStruct((ch, reach + 1, ch, width), jnp.float32),
        in_specs=[VMEM] * (1 + len(received)), out_specs=VMEM, compiler_params=params,
    )(factors, *received)


def solution(mesh):
    in_specs = (
        P("win", None, ("fibre", "chan"), "freq"),
        P(("fibre", "win")),
        P(("fibre", "chan"), None),
    )
    out_specs = P(("fibre", "chan"), None, None, ("win", "freq"))
    return jax.shard_map(local, mesh=mesh, in_specs=in_specs, out_specs=out_specs, check_vma=False)
```

```python
import functools
import math

import jax
import jax.numpy as jnp
import numpy as np
from jax import lax
from jax.experimental import pallas as pl
from jax.experimental.pallas import tpu as pltpu
from jax.sharding import PartitionSpec as P

LAGS = 1024
F_LO = 60
NSAMP = 15000
EPS = 1e-06
LANES = 128
SUBLANES = 8
FINE = 32
BLOCK = 256
VMEM_LIMIT = 16 * 1024 * 1024


def from_behind(block, axis, distance):
    devices = range(lax.axis_size(axis))
    route = [(i - distance, i) for i in devices if i - distance in devices]
    return lax.ppermute(block, axis, route)


def phases(bins, half_lags):
    turns = np.remainder(np.asarray(bins, np.int64)[:, None] * np.asarray(half_lags, np.int64)[None, :], 2 * NSAMP)
    angle = turns * (math.pi / NSAMP)
    return np.stack([np.cos(angle), np.sin(angle)]).astype(np.float32)


def split(value):
    high = value.astype(jnp.bfloat16)
    return high, (value - high.astype(jnp.float32)).astype(jnp.bfloat16)


def bin_power(x):
    x = x.astype(jnp.float32)
    return jnp.sum(x[0] * x[0] + x[1] * x[1], axis=-1, keepdims=True)


def power_kernel(x_ref, power_ref, copy_ref):
    for w in range(x_ref.shape[0]):
        x = x_ref[w]
        power_ref[w] = bin_power(x)
        copy_ref[w] = x


def whiten_kernel(n_bins, x_ref, *refs):
    out_ref = refs[-1]
    for w in range(x_ref.shape[0]):
        power = bin_power(x_ref[w])
        for ref in refs[:-1]:
            power = power + ref[w]
        scale = lax.rsqrt(power / n_bins + EPS)
        for part in range(2):
            out_ref[w, part] = (x_ref[w, part].astype(jnp.float32) * scale).astype(jnp.bfloat16)


def keep_kernel(keep_ref, white_ref, out_ref):
    for w in range(white_ref.shape[0]):
        out_ref[w] = white_ref[w].astype(jnp.float32) * keep_ref[w, :, :, 0:1]


def table_kernel(base_ref, table_ref):
    f_dev, width = table_ref.shape[1:]
    coarse = base_ref.shape[1] - FINE
    start = lax.axis_index("freq") * (f_dev // FINE)
    for block in range(0, width, BLOCK):
        lags = slice(block, block + BLOCK)
        fine_cos = base_ref[0, coarse:, lags]
        fine_sin = base_ref[1, coarse:, lags]

        def body(step, carry):
            first = pl.multiple_of(start + step * SUBLANES, SUBLANES)
            coarse_cos = base_ref[0, pl.ds(first, SUBLANES), lags]
            coarse_sin = base_ref[1, pl.ds(first, SUBLANES), lags]
            for n in range(SUBLANES):
                cos_a, sin_a = coarse_cos[n:n + 1], coarse_sin[n:n + 1]
                rows = pl.ds(pl.multiple_of((step * SUBLANES + n) * FINE, FINE), FINE)
                table_ref[0, rows, lags], table_ref[1, rows, lags] = split(cos_a * fine_cos - sin_a * fine_sin)
                table_ref[2, rows, lags], table_ref[3, rows, lags] = split(cos_a * fine_sin + sin_a * fine_cos)
            return carry

        lax.fori_loop(0, f_dev // (FINE * SUBLANES), body, 0)


def cross_tile(base_ref, partner_ref, lanes):
    w_dev, _, ch, _ = base_ref.shape
    real = [None] * ch
    imag = [None] * ch
    for w in range(w_dev):
        partner_re = partner_ref[w, 0, :, lanes].astype(jnp.float32)
        partner_im = partner_ref[w, 1, :, lanes].astype(jnp.float32)
        for i in range(ch):
            base_re = base_ref[w, 0, i:i + 1, lanes]
            base_im = base_ref[w, 1, i:i + 1, lanes]
            re = base_re * partner_re + base_im * partner_im
            im = base_im * partner_re - base_re * partner_im
            real[i] = re if w == 0 else real[i] + re
            imag[i] = im if w == 0 else imag[i] + im
    return real, imag


def pairs_kernel(n_partners, n_win, n_freq, base_ref, *refs):
    partner_refs = refs[:n_partners]
    twist_ref, table_ref = refs[n_partners:n_partners + 2]
    before_refs = refs[n_partners + 2:-2 - n_freq]
    out_refs = refs[-2 - n_freq:-2]
    rows_ref, sums_ref = refs[-2:]
    done = out_refs[0].shape[0] - n_partners
    for before_ref, out_ref in zip(before_refs, out_refs):
        out_ref[:done] = before_ref[...]
    ch, f_dev = base_ref.shape[2:]
    pairs = ch * ch
    groups = n_win * n_freq
    width = out_refs[0].shape[-1]
    freq, win = lax.axis_index("freq"), lax.axis_index("win")
    dot = functools.partial(jnp.dot, preferred_element_type=jnp.float32)
    for k, partner_ref in enumerate(partner_refs):

        def body(tile, carry):
            lanes = pl.ds(pl.multiple_of(tile * LANES, LANES), LANES)
            real, imag = cross_tile(base_ref, partner_ref, lanes)
            cos = twist_ref[freq, 0:1, lanes]
            sin = twist_ref[freq, 1:2, lanes]
            for i in range(0, ch, 2):
                re = jnp.concatenate(real[i:i + 2], axis=0)
                im = jnp.concatenate(imag[i:i + 2], axis=0)
                for part, value in enumerate((re * cos + im * sin, im * cos - re * sin)):
                    high, low = split(value)
                    rows_ref[part, i * ch:(i + 2) * ch, lanes] = high
                    rows_ref[part, pairs + i * ch:pairs + (i + 2) * ch, lanes] = low
            return carry

        lax.fori_loop(0, f_dev // LANES, body, 0)
        for part in range(2):
            both = dot(rows_ref[part], table_ref[2 * part])
            sums_ref[part] = both[:pairs] + both[pairs:] + dot(rows_ref[part, :pairs], table_ref[2 * part + 1])
        for turn_freq, out_ref in enumerate(out_refs):
            for turn_win in range(n_win):
                owner = (win + turn_win) % n_win * n_freq + (freq + turn_freq) % n_freq
                upper = owner >= groups // 2
                block = jnp.where(upper, owner - groups // 2, groups // 2 - 1 - owner)
                sign = jnp.where(upper, -1.0, 1.0)
                lags = pl.ds(pl.multiple_of(block * width, LANES), width)
                out_ref[done + k, turn_win] = sums_ref[0, :, lags] + sign * sums_ref[1, :, lags]


def add_kernel(n_parts, n_before, *refs):
    parts, befores, out_refs = refs[:n_parts], refs[n_parts:n_parts + n_before], refs[n_parts + n_before:]
    for turn, out_ref in enumerate(out_refs):
        start = 0
        for before in befores:
            out_ref[start:start + before.shape[0]] = before[:, turn].astype(out_ref.dtype)
            start += before.shape[0]
        total = parts[0][:, turn]
        for ref in parts[1:]:
            total = total + ref[:, turn]
        out_ref[start:] = total.astype(out_ref.dtype)


def plain_add_kernel(*refs):
    total = refs[0][...]
    for ref in refs[1:-1]:
        total = total + ref[...]
    refs[-1][...] = total


def reverse_lanes(value):
    backward = LANES - 1 - lax.broadcasted_iota(jnp.int32, (value.shape[0], LANES), 1)
    pieces = [
        jnp.take_along_axis(value[:, start:start + LANES], backward, axis=1, mode="promise_in_bounds")
        for start in range(0, value.shape[1], LANES)
    ]
    return jnp.concatenate(pieces[::-1], axis=1)


def combine_kernel(n_win, n_freq, factor_ref, *refs):
    out_ref = refs[-1]
    ch = out_ref.shape[0]
    lower = lax.axis_index("win") * n_freq + lax.axis_index("freq") < n_win * n_freq // 2
    k = 0
    for first in range(0, len(refs) - 1, n_win):
        parts = refs[first:first + n_win]
        for n in range(parts[0].shape[0]):
            total = parts[0][n].astype(jnp.float32)
            for ref in parts[1:]:
                total = total + ref[n].astype(jnp.float32)
            total = jnp.where(lower, reverse_lanes(total), total) * factor_ref[k]
            for i in range(ch):
                out_ref[i, k] = total[i * ch:(i + 1) * ch]
            k += 1


VMEM = pl.BlockSpec(memory_space=pltpu.VMEM)


def local(spectra, keep, pair_mask):
    w_dev, _, ch, f_dev = spectra.shape
    reach = pair_mask.shape[1] - 1
    n_chan, n_win, n_freq = (lax.axis_size(a) for a in ("chan", "win", "freq"))
    width = LAGS // (n_win * n_freq)
    n_bins = f_dev * n_freq
    params = pltpu.CompilerParams(vmem_limit_bytes=VMEM_LIMIT)


    def cost(flops, size):
        return pl.CostEstimate(flops=flops, bytes_accessed=size, transcendentals=0)

    power, copied = pl.pallas_call(
        power_kernel,
        out_shape=[
            jax.ShapeDtypeStruct((w_dev, ch, 1), jnp.float32),
            jax.ShapeDtypeStruct(spectra.shape, spectra.dtype),
        ],
        in_specs=[VMEM], out_specs=[VMEM] * 2, compiler_params=params, cost_estimate=cost(ch, ch),
    )(spectra)
    own_power = []
    for turn in range(1, n_freq):
        route = [(f, (f + turn) % n_freq) for f in range(n_freq)]
        own_power.append(lax.ppermute(power, "freq", route))

    twist = phases(F_LO + np.arange(n_bins), np.ones(1)).reshape(2, n_freq, f_dev)
    twist = jnp.asarray(np.moveaxis(twist, 0, 1))

    def whiten(block, others):
        return pl.pallas_call(
            functools.partial(whiten_kernel, n_bins),
            out_shape=jax.ShapeDtypeStruct(block.shape, jnp.bfloat16),
            in_specs=[VMEM] * (1 + len(others)), out_specs=VMEM, compiler_params=params,
        )(block, *others)

    kept_windows = jnp.broadcast_to(keep.astype(jnp.float32)[:, None, None, None], (w_dev, 1, 1, LANES))

    def kept(block):
        return pl.pallas_call(
            keep_kernel,
            out_shape=jax.ShapeDtypeStruct(block.shape, jnp.float32),
            in_specs=[VMEM] * 2, out_specs=VMEM, compiler_params=params,
        )(kept_windows, block)

    def pairs(base, partners, before=()):
        n = len(partners) + (before[0].shape[0] if before else 0)
        return pl.pallas_call(
            functools.partial(pairs_kernel, len(partners), n_win, n_freq),
            out_shape=[jax.ShapeDtypeStruct((n, n_win, ch * ch, width), jnp.float32)] * n_freq,
            in_specs=[VMEM] * (3 + len(partners) + len(before)), out_specs=[VMEM] * n_freq,
            scratch_shapes=[
                pltpu.VMEM((2, 2 * ch * ch, f_dev), jnp.bfloat16),
                pltpu.VMEM((2, ch * ch, LAGS // 2), jnp.float32),
            ],
            compiler_params=params,
            cost_estimate=cost(ch, ch),
        )(base, *partners, twist, table, *before)

    def turns(parts, axis, size):
        received = [parts[0]]
        for turn in range(1, size):
            route = [(g, (g + turn) % size) for g in range(size)]
            received.append(lax.ppermute(parts[turn], axis, route))
        return received

    def sum_bins(parts):
        return pl.pallas_call(
            plain_add_kernel,
            out_shape=jax.ShapeDtypeStruct(parts[0].shape, jnp.float32),
            in_specs=[VMEM] * n_freq, out_specs=VMEM, compiler_params=params,
        )(*turns(parts, "freq", n_freq))

    def split_windows(parts, before, kinds):
        n = sum(part.shape[0] for part in before) + parts[0].shape[0]
        return pl.pallas_call(
            functools.partial(add_kernel, n_freq, len(before)),
            out_shape=[jax.ShapeDtypeStruct((n, ch * ch, width), kind) for kind in kinds],
            in_specs=[VMEM] * (n_freq + len(before)), out_specs=[VMEM] * n_win, compiler_params=params,
        )(*turns(parts, "freq", n_freq), *before)

    white = whiten(copied, own_power)
    above = from_behind(white, "chan", 1)
    below = from_behind(white, "chan", -1)
    far = []
    for distance in range(2, reach):
        route = [(c + distance, c) for c in range(1, n_chan - distance)]
        far.append(lax.ppermute(white, "chan", route))
    half_lags = 2 * np.arange(LAGS // 2) + 1
    coarse = phases(np.arange(0, n_bins, FINE), half_lags)
    fine = phases(F_LO + np.arange(FINE), half_lags)
    white, ends = lax.optimization_barrier((white, jnp.asarray(np.concatenate([coarse, fine], axis=1))))
    table = pl.pallas_call(
        table_kernel,
        out_shape=jax.ShapeDtypeStruct((4, f_dev, LAGS // 2), jnp.bfloat16),
        in_specs=[VMEM], out_specs=VMEM, compiler_params=params, cost_estimate=cost(ch, ch),
    )(ends)
    own = kept(white)
    first = pairs(own, [white])
    above, first = lax.optimization_barrier((above, first))
    base = kept(above)
    below, base = lax.optimization_barrier((below, base))
    parts = pairs(own, [below], first)
    before = ()
    for block in [below] + far[:-1]:
        before = pairs(base, [block], before)
    far, parts, before = lax.optimization_barrier((far[-1], parts, before))
    sums = split_windows(parts, [], [jnp.float32] + [jnp.bfloat16] * (n_win - 1))
    shipped = split_windows(pairs(base, [far], before), [], [jnp.bfloat16] * n_win)
    received = turns(sums, "win", n_win)
    received.append(from_behind(shipped[0], "chan", -1))
    for turn in range(1, n_win):
        route = [
            (c * n_win + w, (c - 1) * n_win + (w + turn) % n_win) for c in range(1, n_chan) for w in range(n_win)
        ]
        received.append(lax.ppermute(shipped[turn], ("chan", "win"), route))
    scale = 1.0 / math.sqrt(w_dev * n_win * n_bins)
    factors = jnp.repeat(pair_mask.T.astype(jnp.float32) * scale, ch, axis=1)[..., None]
    return pl.pallas_call(
        functools.partial(combine_kernel, n_win, n_freq),
        out_shape=jax.ShapeDtypeStruct((ch, reach + 1, ch, width), jnp.float32),
        in_specs=[VMEM] * (1 + len(received)), out_specs=VMEM, compiler_params=params,
    )(factors, *received)


def solution(mesh):
    in_specs = (
        P("win", None, ("fibre", "chan"), "freq"),
        P(("fibre", "win")),
        P(("fibre", "chan"), None),
    )
    out_specs = P(("fibre", "chan"), None, None, ("win", "freq"))
    return jax.shard_map(local, mesh=mesh, in_specs=in_specs, out_specs=out_specs, check_vma=False)
```

```python
import functools
import math

import jax
import jax.numpy as jnp
import numpy as np
from jax import lax
from jax.experimental import pallas as pl
from jax.experimental.pallas import tpu as pltpu
from jax.sharding import PartitionSpec as P

LAGS = 1024
F_LO = 60
NSAMP = 15000
EPS = 1e-06
LANES = 128
SUBLANES = 8
FINE = 32
BLOCK = 256
VMEM_LIMIT = 16 * 1024 * 1024


def from_behind(block, axis, distance):
    devices = range(lax.axis_size(axis))
    route = [(i - distance, i) for i in devices if i - distance in devices]
    return lax.ppermute(block, axis, route)


def phases(bins, half_lags):
    turns = np.remainder(np.asarray(bins, np.int64)[:, None] * np.asarray(half_lags, np.int64)[None, :], 2 * NSAMP)
    angle = turns * (math.pi / NSAMP)
    return np.stack([np.cos(angle), np.sin(angle)]).astype(np.float32)


def split(value):
    high = value.astype(jnp.bfloat16)
    return high, (value - high.astype(jnp.float32)).astype(jnp.bfloat16)


def bin_power(x):
    x = x.astype(jnp.float32)
    return jnp.sum(x[0] * x[0] + x[1] * x[1], axis=-1, keepdims=True)


def power_kernel(x_ref, power_ref, copy_ref):
    for w in range(x_ref.shape[0]):
        x = x_ref[w]
        power_ref[w] = bin_power(x)
        copy_ref[w] = x


def partial_kernel(x_ref, power_ref):
    for w in range(x_ref.shape[0]):
        power_ref[w] = bin_power(x_ref[w])


def whiten_kernel(n_bins, x_ref, *refs):
    out_ref = refs[-1]
    for w in range(x_ref.shape[0]):
        power = bin_power(x_ref[w])
        for ref in refs[:-1]:
            power = power + ref[w]
        scale = lax.rsqrt(power / n_bins + EPS)
        for part in range(2):
            out_ref[w, part] = (x_ref[w, part].astype(jnp.float32) * scale).astype(jnp.bfloat16)


def keep_kernel(keep_ref, white_ref, out_ref):
    for w in range(white_ref.shape[0]):
        out_ref[w] = white_ref[w].astype(jnp.float32) * keep_ref[w, :, :, 0:1]


def table_kernel(base_ref, table_ref):
    f_dev, width = table_ref.shape[1:]
    coarse = base_ref.shape[1] - FINE
    start = lax.axis_index("freq") * (f_dev // FINE)
    for block in range(0, width, BLOCK):
        lags = slice(block, block + BLOCK)
        fine_cos = base_ref[0, coarse:, lags]
        fine_sin = base_ref[1, coarse:, lags]

        def body(step, carry):
            first = pl.multiple_of(start + step * SUBLANES, SUBLANES)
            coarse_cos = base_ref[0, pl.ds(first, SUBLANES), lags]
            coarse_sin = base_ref[1, pl.ds(first, SUBLANES), lags]
            for n in range(SUBLANES):
                cos_a, sin_a = coarse_cos[n:n + 1], coarse_sin[n:n + 1]
                rows = pl.ds(pl.multiple_of((step * SUBLANES + n) * FINE, FINE), FINE)
                table_ref[0, rows, lags], table_ref[1, rows, lags] = split(cos_a * fine_cos - sin_a * fine_sin)
                table_ref[2, rows, lags], table_ref[3, rows, lags] = split(cos_a * fine_sin + sin_a * fine_cos)
            return carry

        lax.fori_loop(0, f_dev // (FINE * SUBLANES), body, 0)


def cross_tile(base_ref, partner_ref, lanes):
    w_dev, _, ch, _ = base_ref.shape
    real = [None] * ch
    imag = [None] * ch
    for w in range(w_dev):
        partner_re = partner_ref[w, 0, :, lanes].astype(jnp.float32)
        partner_im = partner_ref[w, 1, :, lanes].astype(jnp.float32)
        for i in range(ch):
            base_re = base_ref[w, 0, i:i + 1, lanes]
            base_im = base_ref[w, 1, i:i + 1, lanes]
            re = base_re * partner_re + base_im * partner_im
            im = base_im * partner_re - base_re * partner_im
            real[i] = re if w == 0 else real[i] + re
            imag[i] = im if w == 0 else imag[i] + im
    return real, imag


def pairs_kernel(n_partners, n_win, n_freq, base_ref, *refs):
    partner_refs = refs[:n_partners]
    twist_ref, table_ref = refs[n_partners:n_partners + 2]
    before_refs = refs[n_partners + 2:-2 - n_freq]
    out_refs = refs[-2 - n_freq:-2]
    rows_ref, sums_ref = refs[-2:]
    done = out_refs[0].shape[0] - n_partners
    for before_ref, out_ref in zip(before_refs, out_refs):
        out_ref[:done] = before_ref[...]
    ch, f_dev = base_ref.shape[2:]
    pairs = ch * ch
    groups = n_win * n_freq
    width = out_refs[0].shape[-1]
    freq, win = lax.axis_index("freq"), lax.axis_index("win")
    dot = functools.partial(jnp.dot, preferred_element_type=jnp.float32)
    for k, partner_ref in enumerate(partner_refs):

        def body(tile, carry):
            lanes = pl.ds(pl.multiple_of(tile * LANES, LANES), LANES)
            real, imag = cross_tile(base_ref, partner_ref, lanes)
            cos = twist_ref[freq, 0:1, lanes]
            sin = twist_ref[freq, 1:2, lanes]
            for i in range(0, ch, 2):
                re = jnp.concatenate(real[i:i + 2], axis=0)
                im = jnp.concatenate(imag[i:i + 2], axis=0)
                for part, value in enumerate((re * cos + im * sin, im * cos - re * sin)):
                    high, low = split(value)
                    rows_ref[part, i * ch:(i + 2) * ch, lanes] = high
                    rows_ref[part, pairs + i * ch:pairs + (i + 2) * ch, lanes] = low
            return carry

        lax.fori_loop(0, f_dev // LANES, body, 0)
        for part in range(2):
            both = dot(rows_ref[part], table_ref[2 * part])
            sums_ref[part] = both[:pairs] + both[pairs:] + dot(rows_ref[part, :pairs], table_ref[2 * part + 1])
        for turn_freq, out_ref in enumerate(out_refs):
            for turn_win in range(n_win):
                owner = (win + turn_win) % n_win * n_freq + (freq + turn_freq) % n_freq
                upper = owner >= groups // 2
                block = jnp.where(upper, owner - groups // 2, groups // 2 - 1 - owner)
                sign = jnp.where(upper, -1.0, 1.0)
                lags = pl.ds(pl.multiple_of(block * width, LANES), width)
                out_ref[done + k, turn_win] = sums_ref[0, :, lags] + sign * sums_ref[1, :, lags]


def add_kernel(n_parts, n_before, *refs):
    parts, befores, out_refs = refs[:n_parts], refs[n_parts:n_parts + n_before], refs[n_parts + n_before:]
    for turn, out_ref in enumerate(out_refs):
        start = 0
        for before in befores:
            out_ref[start:start + before.shape[0]] = before[:, turn].astype(out_ref.dtype)
            start += before.shape[0]
        total = parts[0][:, turn]
        for ref in parts[1:]:
            total = total + ref[:, turn]
        out_ref[start:] = total.astype(out_ref.dtype)


def plain_add_kernel(*refs):
    total = refs[0][...]
    for ref in refs[1:-1]:
        total = total + ref[...]
    refs[-1][...] = total


def reverse_lanes(value):
    backward = LANES - 1 - lax.broadcasted_iota(jnp.int32, (value.shape[0], LANES), 1)
    pieces = [
        jnp.take_along_axis(value[:, start:start + LANES], backward, axis=1, mode="promise_in_bounds")
        for start in range(0, value.shape[1], LANES)
    ]
    return jnp.concatenate(pieces[::-1], axis=1)


def combine_kernel(n_win, n_freq, factor_ref, *refs):
    out_ref = refs[-1]
    ch = out_ref.shape[0]
    lower = lax.axis_index("win") * n_freq + lax.axis_index("freq") < n_win * n_freq // 2
    k = 0
    for first in range(0, len(refs) - 1, n_win):
        parts = refs[first:first + n_win]
        for n in range(parts[0].shape[0]):
            total = parts[0][n].astype(jnp.float32)
            for ref in parts[1:]:
                total = total + ref[n].astype(jnp.float32)
            total = jnp.where(lower, reverse_lanes(total), total) * factor_ref[k]
            for i in range(ch):
                out_ref[i, k] = total[i * ch:(i + 1) * ch]
            k += 1


VMEM = pl.BlockSpec(memory_space=pltpu.VMEM)


def local(spectra, keep, pair_mask):
    w_dev, _, ch, f_dev = spectra.shape
    reach = pair_mask.shape[1] - 1
    n_chan, n_win, n_freq = (lax.axis_size(a) for a in ("chan", "win", "freq"))
    width = LAGS // (n_win * n_freq)
    n_bins = f_dev * n_freq
    params = pltpu.CompilerParams(vmem_limit_bytes=VMEM_LIMIT)


    def cost(flops, size):
        return pl.CostEstimate(flops=flops, bytes_accessed=size, transcendentals=0)

    below = from_behind(spectra, "chan", -1)
    far = []
    for distance in range(2, reach):
        route = [(c + distance, c) for c in range(1, n_chan - distance)]
        far.append(lax.ppermute(spectra, "chan", route))
    power, copied = pl.pallas_call(
        power_kernel,
        out_shape=[
            jax.ShapeDtypeStruct((w_dev, ch, 1), jnp.float32),
            jax.ShapeDtypeStruct(spectra.shape, spectra.dtype),
        ],
        in_specs=[VMEM], out_specs=[VMEM] * 2, compiler_params=params, cost_estimate=cost(ch, ch),
    )(spectra)
    twist = phases(F_LO + np.arange(n_bins), np.ones(1)).reshape(2, n_freq, f_dev)
    twist = jnp.asarray(np.moveaxis(twist, 0, 1))

    def swap(power):
        routes = [[(f, (f + turn) % n_freq) for f in range(n_freq)] for turn in range(1, n_freq)]
        return [lax.ppermute(power, "freq", route) for route in routes]

    def half_power(block):
        return pl.pallas_call(
            partial_kernel,
            out_shape=jax.ShapeDtypeStruct(power.shape, jnp.float32),
            in_specs=[VMEM], out_specs=VMEM, compiler_params=params, cost_estimate=cost(ch, ch),
        )(block)

    def whiten(block, others):
        return pl.pallas_call(
            functools.partial(whiten_kernel, n_bins),
            out_shape=jax.ShapeDtypeStruct(block.shape, jnp.bfloat16),
            in_specs=[VMEM] * (1 + len(others)), out_specs=VMEM, compiler_params=params,
        )(block, *others)

    kept_windows = jnp.broadcast_to(keep.astype(jnp.float32)[:, None, None, None], (w_dev, 1, 1, LANES))

    def kept(block):
        return pl.pallas_call(
            keep_kernel,
            out_shape=jax.ShapeDtypeStruct(block.shape, jnp.float32),
            in_specs=[VMEM] * 2, out_specs=VMEM, compiler_params=params,
        )(kept_windows, block)

    def pairs(base, partners, before=()):
        n = len(partners) + (before[0].shape[0] if before else 0)
        return pl.pallas_call(
            functools.partial(pairs_kernel, len(partners), n_win, n_freq),
            out_shape=[jax.ShapeDtypeStruct((n, n_win, ch * ch, width), jnp.float32)] * n_freq,
            in_specs=[VMEM] * (3 + len(partners) + len(before)), out_specs=[VMEM] * n_freq,
            scratch_shapes=[
                pltpu.VMEM((2, 2 * ch * ch, f_dev), jnp.bfloat16),
                pltpu.VMEM((2, ch * ch, LAGS // 2), jnp.float32),
            ],
            compiler_params=params,
            cost_estimate=cost(ch, ch),
        )(base, *partners, twist, table, *before)

    def turns(parts, axis, size):
        received = [parts[0]]
        for turn in range(1, size):
            route = [(g, (g + turn) % size) for g in range(size)]
            received.append(lax.ppermute(parts[turn], axis, route))
        return received

    def sum_bins(parts):
        return pl.pallas_call(
            plain_add_kernel,
            out_shape=jax.ShapeDtypeStruct(parts[0].shape, jnp.float32),
            in_specs=[VMEM] * n_freq, out_specs=VMEM, compiler_params=params,
        )(*turns(parts, "freq", n_freq))

    def split_windows(parts, before, kinds):
        n = sum(part.shape[0] for part in before) + parts[0].shape[0]
        return pl.pallas_call(
            functools.partial(add_kernel, n_freq, len(before)),
            out_shape=[jax.ShapeDtypeStruct((n, ch * ch, width), kind) for kind in kinds],
            in_specs=[VMEM] * (n_freq + len(before)), out_specs=[VMEM] * n_win, compiler_params=params,
        )(*turns(parts, "freq", n_freq), *before)

    white = whiten(copied, swap(power))
    above = from_behind(white, "chan", 1)
    half_lags = 2 * np.arange(LAGS // 2) + 1
    coarse = phases(np.arange(0, n_bins, FINE), half_lags)
    fine = phases(F_LO + np.arange(FINE), half_lags)
    white, ends = lax.optimization_barrier((white, jnp.asarray(np.concatenate([coarse, fine], axis=1))))
    table = pl.pallas_call(
        table_kernel,
        out_shape=jax.ShapeDtypeStruct((4, f_dev, LAGS // 2), jnp.bfloat16),
        in_specs=[VMEM], out_specs=VMEM, compiler_params=params, cost_estimate=cost(ch, ch),
    )(ends)
    own = kept(white)
    first = pairs(own, [white])
    below, first = lax.optimization_barrier((below, first))
    below = whiten(below, swap(half_power(below)))
    parts = pairs(own, [below], first)
    far, parts = lax.optimization_barrier((far, parts))
    halves = [half_power(block) for block in far]
    above, halves = lax.optimization_barrier((above, halves))
    others = [swap(half) for half in halves]
    base = kept(above)
    before = pairs(base, [below])
    for block, power in zip(far[:-1], others[:-1]):
        before = pairs(base, [whiten(block, power)], before)
    others, before = lax.optimization_barrier((others, before))
    far = whiten(far[-1], others[-1])
    sums = split_windows(parts, [], [jnp.float32] + [jnp.bfloat16] * (n_win - 1))
    shipped = split_windows(pairs(base, [far], before), [], [jnp.bfloat16] * n_win)
    received = turns(sums, "win", n_win)
    received.append(from_behind(shipped[0], "chan", -1))
    for turn in range(1, n_win):
        route = [
            (c * n_win + w, (c - 1) * n_win + (w + turn) % n_win) for c in range(1, n_chan) for w in range(n_win)
        ]
        received.append(lax.ppermute(shipped[turn], ("chan", "win"), route))
    scale = 1.0 / math.sqrt(w_dev * n_win * n_bins)
    factors = jnp.repeat(pair_mask.T.astype(jnp.float32) * scale, ch, axis=1)[..., None]
    return pl.pallas_call(
        functools.partial(combine_kernel, n_win, n_freq),
        out_shape=jax.ShapeDtypeStruct((ch, reach + 1, ch, width), jnp.float32),
        in_specs=[VMEM] * (1 + len(received)), out_specs=VMEM, compiler_params=params,
    )(factors, *received)


def solution(mesh):
    in_specs = (
        P("win", None, ("fibre", "chan"), "freq"),
        P(("fibre", "win")),
        P(("fibre", "chan"), None),
    )
    out_specs = P(("fibre", "chan"), None, None, ("win", "freq"))
    return jax.shard_map(local, mesh=mesh, in_specs=in_specs, out_specs=out_specs, check_vma=False)
```

```python
import functools
import math

import jax
import jax.numpy as jnp
import numpy as np
from jax import lax
from jax.experimental import pallas as pl
from jax.experimental.pallas import tpu as pltpu
from jax.sharding import PartitionSpec as P

LAGS = 1024
F_LO = 60
NSAMP = 15000
EPS = 1e-06
LANES = 128
SUBLANES = 8
FINE = 32
BLOCK = 256
VMEM_LIMIT = 16 * 1024 * 1024


def from_behind(block, axis, distance):
    devices = range(lax.axis_size(axis))
    route = [(i - distance, i) for i in devices if i - distance in devices]
    return lax.ppermute(block, axis, route)


def phases(bins, half_lags):
    turns = np.remainder(np.asarray(bins, np.int64)[:, None] * np.asarray(half_lags, np.int64)[None, :], 2 * NSAMP)
    angle = turns * (math.pi / NSAMP)
    return np.stack([np.cos(angle), np.sin(angle)]).astype(np.float32)


def split(value):
    high = value.astype(jnp.bfloat16)
    return high, (value - high.astype(jnp.float32)).astype(jnp.bfloat16)


def bin_power(x):
    x = x.astype(jnp.float32)
    return jnp.sum(x[0] * x[0] + x[1] * x[1], axis=-1, keepdims=True)


def power_kernel(x_ref, power_ref, copy_ref):
    for w in range(x_ref.shape[0]):
        x = x_ref[w]
        power_ref[w] = bin_power(x)
        copy_ref[w] = x


def partial_kernel(x_ref, power_ref):
    for w in range(x_ref.shape[0]):
        power_ref[w] = bin_power(x_ref[w])


def own_kernel(n_bins, x_ref, *refs):
    power_ref = refs[-1]
    for w in range(x_ref.shape[0]):
        power = bin_power(x_ref[w])
        for ref in refs[:-2]:
            power = power + ref[w]
        power_ref[w] = power
    whiten_kernel(n_bins, False, x_ref, power_ref, refs[-2])


def whiten_kernel(n_bins, add_own, x_ref, *refs):
    out_ref = refs[-1]
    for w in range(x_ref.shape[0]):
        power = bin_power(x_ref[w]) if add_own else None
        for ref in refs[:-1]:
            power = ref[w] if power is None else power + ref[w]
        scale = lax.rsqrt(power / n_bins + EPS)
        for part in range(2):
            out_ref[w, part] = (x_ref[w, part].astype(jnp.float32) * scale).astype(jnp.bfloat16)


def keep_kernel(keep_ref, white_ref, out_ref):
    for w in range(white_ref.shape[0]):
        out_ref[w] = white_ref[w].astype(jnp.float32) * keep_ref[:, w:w + 1].astype(jnp.float32)[None]


def table_kernel(base_ref, table_ref):
    f_dev, width = table_ref.shape[1:]
    coarse = base_ref.shape[1] - FINE
    start = lax.axis_index("freq") * (f_dev // FINE)
    for block in range(0, width, BLOCK):
        lags = slice(block, block + BLOCK)
        fine_cos = base_ref[0, coarse:, lags]
        fine_sin = base_ref[1, coarse:, lags]

        def body(step, carry):
            first = pl.multiple_of(start + step * SUBLANES, SUBLANES)
            coarse_cos = base_ref[0, pl.ds(first, SUBLANES), lags]
            coarse_sin = base_ref[1, pl.ds(first, SUBLANES), lags]
            for n in range(SUBLANES):
                cos_a, sin_a = coarse_cos[n:n + 1], coarse_sin[n:n + 1]
                rows = pl.ds(pl.multiple_of((step * SUBLANES + n) * FINE, FINE), FINE)
                table_ref[0, rows, lags], table_ref[1, rows, lags] = split(cos_a * fine_cos - sin_a * fine_sin)
                table_ref[2, rows, lags], table_ref[3, rows, lags] = split(cos_a * fine_sin + sin_a * fine_cos)
            return carry

        lax.fori_loop(0, f_dev // (FINE * SUBLANES), body, 0)


def cross_tile(base_ref, partner_ref, lanes):
    w_dev, _, ch, _ = base_ref.shape
    real = [None] * ch
    imag = [None] * ch
    for w in range(w_dev):
        partner_re = partner_ref[w, 0, :, lanes].astype(jnp.float32)
        partner_im = partner_ref[w, 1, :, lanes].astype(jnp.float32)
        for i in range(ch):
            base_re = base_ref[w, 0, i:i + 1, lanes]
            base_im = base_ref[w, 1, i:i + 1, lanes]
            re = base_re * partner_re + base_im * partner_im
            im = base_im * partner_re - base_re * partner_im
            real[i] = re if w == 0 else real[i] + re
            imag[i] = im if w == 0 else imag[i] + im
    return real, imag


def pairs_kernel(n_partners, n_win, n_freq, base_ref, *refs):
    partner_refs = refs[:n_partners]
    twist_ref, table_ref = refs[n_partners:n_partners + 2]
    before_refs = refs[n_partners + 2:-2 - n_freq]
    out_refs = refs[-2 - n_freq:-2]
    rows_ref, sums_ref = refs[-2:]
    done = out_refs[0].shape[0] - n_partners
    for before_ref, out_ref in zip(before_refs, out_refs):
        out_ref[:done] = before_ref[...]
    ch, f_dev = base_ref.shape[2:]
    pairs = ch * ch
    groups = n_win * n_freq
    width = out_refs[0].shape[-1]
    freq, win = lax.axis_index("freq"), lax.axis_index("win")
    dot = functools.partial(jnp.dot, preferred_element_type=jnp.float32)
    count = n_partners * pairs

    def body(tile, carry):
        lanes = pl.ds(pl.multiple_of(tile * LANES, LANES), LANES)
        cos = twist_ref[freq, 0:1, lanes]
        sin = twist_ref[freq, 1:2, lanes]
        for k, partner_ref in enumerate(partner_refs):
            real, imag = cross_tile(base_ref, partner_ref, lanes)
            for i in range(0, ch, 2):
                rows = k * pairs + i * ch
                re = jnp.concatenate(real[i:i + 2], axis=0)
                im = jnp.concatenate(imag[i:i + 2], axis=0)
                for part, value in enumerate((re * cos + im * sin, im * cos - re * sin)):
                    high, low = split(value)
                    rows_ref[part, rows:rows + 2 * ch, lanes] = high
                    rows_ref[part, count + rows:count + rows + 2 * ch, lanes] = low
        return carry

    lax.fori_loop(0, f_dev // LANES, body, 0)
    for part in range(2):
        both = dot(rows_ref[part], table_ref[2 * part])
        sums_ref[part] = both[:count] + both[count:] + dot(rows_ref[part, :count], table_ref[2 * part + 1])
    for turn_freq, out_ref in enumerate(out_refs):
        for turn_win in range(n_win):
            owner = (win + turn_win) % n_win * n_freq + (freq + turn_freq) % n_freq
            upper = owner >= groups // 2
            block = jnp.where(upper, owner - groups // 2, groups // 2 - 1 - owner)
            sign = jnp.where(upper, -1.0, 1.0)
            lags = pl.ds(pl.multiple_of(block * width, LANES), width)
            for k in range(n_partners):
                rows = slice(k * pairs, (k + 1) * pairs)
                out_ref[done + k, turn_win] = sums_ref[0, rows, lags] + sign * sums_ref[1, rows, lags]


def add_kernel(n_parts, n_before, *refs):
    parts, befores, out_refs = refs[:n_parts], refs[n_parts:n_parts + n_before], refs[n_parts + n_before:]
    for turn, out_ref in enumerate(out_refs):
        start = 0
        for before in befores:
            out_ref[start:start + before.shape[0]] = before[:, turn].astype(out_ref.dtype)
            start += before.shape[0]
        total = parts[0][:, turn]
        for ref in parts[1:]:
            total = total + ref[:, turn]
        out_ref[start:] = total.astype(out_ref.dtype)


def plain_add_kernel(*refs):
    total = refs[0][...]
    for ref in refs[1:-1]:
        total = total + ref[...]
    refs[-1][...] = total


def reverse_lanes(value):
    backward = LANES - 1 - lax.broadcasted_iota(jnp.int32, (value.shape[0], LANES), 1)
    pieces = [
        jnp.take_along_axis(value[:, start:start + LANES], backward, axis=1, mode="promise_in_bounds")
        for start in range(0, value.shape[1], LANES)
    ]
    return jnp.concatenate(pieces[::-1], axis=1)


def combine_kernel(n_win, n_freq, factor_ref, *refs):
    out_ref = refs[-1]
    ch = out_ref.shape[0]
    lower = lax.axis_index("win") * n_freq + lax.axis_index("freq") < n_win * n_freq // 2
    k = 0
    for first in range(0, len(refs) - 1, n_win):
        parts = refs[first:first + n_win]
        for n in range(parts[0].shape[0]):
            total = parts[0][n].astype(jnp.float32)
            for ref in parts[1:]:
                total = total + ref[n].astype(jnp.float32)
            total = jnp.where(lower, reverse_lanes(total), total) * factor_ref[k]
            for i in range(ch):
                out_ref[i, k] = total[i * ch:(i + 1) * ch]
            k += 1


VMEM = pl.BlockSpec(memory_space=pltpu.VMEM)


def local(spectra, keep, pair_mask):
    w_dev, _, ch, f_dev = spectra.shape
    reach = pair_mask.shape[1] - 1
    n_chan, n_win, n_freq = (lax.axis_size(a) for a in ("chan", "win", "freq"))
    width = LAGS // (n_win * n_freq)
    n_bins = f_dev * n_freq
    params = pltpu.CompilerParams(vmem_limit_bytes=VMEM_LIMIT)


    def cost(flops, size):
        return pl.CostEstimate(flops=flops, bytes_accessed=size, transcendentals=0)

    below = from_behind(spectra, "chan", -1)
    far_routes = [[(c + away, c) for c in range(1, n_chan - away)] for away in range(2, reach)]
    far = [lax.ppermute(spectra, "chan", route) for route in far_routes]
    power, copied = pl.pallas_call(
        power_kernel,
        out_shape=[
            jax.ShapeDtypeStruct((w_dev, ch, 1), jnp.float32),
            jax.ShapeDtypeStruct(spectra.shape, spectra.dtype),
        ],
        in_specs=[VMEM], out_specs=[VMEM] * 2, compiler_params=params, cost_estimate=cost(ch, ch),
    )(spectra)
    twist = phases(F_LO + np.arange(n_bins), np.ones(1)).reshape(2, n_freq, f_dev)
    twist = jnp.asarray(np.moveaxis(twist, 0, 1))

    def swap(power):
        routes = [[(f, (f + turn) % n_freq) for f in range(n_freq)] for turn in range(1, n_freq)]
        return [lax.ppermute(power, "freq", route) for route in routes]

    def half_power(block):
        return pl.pallas_call(
            partial_kernel,
            out_shape=jax.ShapeDtypeStruct(power.shape, jnp.float32),
            in_specs=[VMEM], out_specs=VMEM, compiler_params=params, cost_estimate=cost(ch, ch),
        )(block)

    def whiten(block, others, add_own):
        return pl.pallas_call(
            functools.partial(whiten_kernel, n_bins, add_own),
            out_shape=jax.ShapeDtypeStruct(block.shape, jnp.bfloat16),
            in_specs=[VMEM] * (1 + len(others)), out_specs=VMEM, compiler_params=params,
        )(block, *others)

    def kept(block):
        return pl.pallas_call(
            keep_kernel,
            out_shape=jax.ShapeDtypeStruct(block.shape, jnp.float32),
            in_specs=[VMEM] * 2, out_specs=VMEM, compiler_params=params,
        )(keep.reshape(1, w_dev), block)

    def pairs(base, partners, before=()):
        n = len(partners) + (before[0].shape[0] if before else 0)
        return pl.pallas_call(
            functools.partial(pairs_kernel, len(partners), n_win, n_freq),
            out_shape=[jax.ShapeDtypeStruct((n, n_win, ch * ch, width), jnp.float32)] * n_freq,
            in_specs=[VMEM] * (3 + len(partners) + len(before)), out_specs=[VMEM] * n_freq,
            scratch_shapes=[
                pltpu.VMEM((2, 2 * len(partners) * ch * ch, f_dev), jnp.bfloat16),
                pltpu.VMEM((2, len(partners) * ch * ch, LAGS // 2), jnp.float32),
            ],
            compiler_params=params,
            cost_estimate=cost(ch, ch),
        )(base, *partners, twist, table, *before)

    def turns(parts, axis, size):
        received = [parts[0]]
        for turn in range(1, size):
            route = [(g, (g + turn) % size) for g in range(size)]
            received.append(lax.ppermute(parts[turn], axis, route))
        return received

    def sum_bins(parts):
        return pl.pallas_call(
            plain_add_kernel,
            out_shape=jax.ShapeDtypeStruct(parts[0].shape, jnp.float32),
            in_specs=[VMEM] * n_freq, out_specs=VMEM, compiler_params=params,
        )(*turns(parts, "freq", n_freq))

    def split_windows(parts, before, kinds):
        n = sum(part.shape[0] for part in before) + parts[0].shape[0]
        return pl.pallas_call(
            functools.partial(add_kernel, n_freq, len(before)),
            out_shape=[jax.ShapeDtypeStruct((n, ch * ch, width), kind) for kind in kinds],
            in_specs=[VMEM] * (n_freq + len(before)), out_specs=[VMEM] * n_win, compiler_params=params,
        )(*turns(parts, "freq", n_freq), *before)

    others = swap(power)
    white, power = pl.pallas_call(
        functools.partial(own_kernel, n_bins),
        out_shape=[
            jax.ShapeDtypeStruct(spectra.shape, jnp.bfloat16),
            jax.ShapeDtypeStruct(power.shape, jnp.float32),
        ],
        in_specs=[VMEM] * (1 + len(others)), out_specs=[VMEM] * 2, compiler_params=params,
    )(copied, *others)
    far_powers = [lax.ppermute(power, "chan", route) for route in far_routes]
    half_lags = 2 * np.arange(LAGS // 2) + 1
    coarse = phases(np.arange(0, n_bins, FINE), half_lags)
    fine = phases(F_LO + np.arange(FINE), half_lags)
    table = pl.pallas_call(
        table_kernel,
        out_shape=jax.ShapeDtypeStruct((4, f_dev, LAGS // 2), jnp.bfloat16),
        in_specs=[VMEM], out_specs=VMEM, compiler_params=params, cost_estimate=cost(ch, ch),
    )(jnp.asarray(np.concatenate([coarse, fine], axis=1)))
    own = kept(white)
    white, table, own = lax.optimization_barrier((white, table, own))
    above = from_behind(white, "chan", 1)
    first = pairs(own, [white])
    below, first = lax.optimization_barrier((below, first))
    below = whiten(below, swap(half_power(below)), True)
    parts = pairs(own, [below], first)
    far, parts = lax.optimization_barrier((far, parts))
    far = [whiten(block, [power], False) for block, power in zip(far, far_powers)]
    above, far = lax.optimization_barrier((above, far))
    base = kept(above)
    sums = split_windows(parts, [], [jnp.float32] + [jnp.bfloat16] * (n_win - 1))
    shipped = split_windows(pairs(base, [below] + far), [], [jnp.bfloat16] * n_win)
    received = turns(sums, "win", n_win)
    received.append(from_behind(shipped[0], "chan", -1))
    for turn in range(1, n_win):
        route = [
            (c * n_win + w, (c - 1) * n_win + (w + turn) % n_win) for c in range(1, n_chan) for w in range(n_win)
        ]
        received.append(lax.ppermute(shipped[turn], ("chan", "win"), route))
    scale = 1.0 / math.sqrt(w_dev * n_win * n_bins)
    factors = jnp.repeat(pair_mask.T.astype(jnp.float32) * scale, ch, axis=1)[..., None]
    return pl.pallas_call(
        functools.partial(combine_kernel, n_win, n_freq),
        out_shape=jax.ShapeDtypeStruct((ch, reach + 1, ch, width), jnp.float32),
        in_specs=[VMEM] * (1 + len(received)), out_specs=VMEM, compiler_params=params,
    )(factors, *received)


def solution(mesh):
    in_specs = (
        P("win", None, ("fibre", "chan"), "freq"),
        P(("fibre", "win")),
        P(("fibre", "chan"), None),
    )
    out_specs = P(("fibre", "chan"), None, None, ("win", "freq"))
    return jax.shard_map(local, mesh=mesh, in_specs=in_specs, out_specs=out_specs, check_vma=False)
```

```python
import functools
import math

import jax
import jax.numpy as jnp
import numpy as np
from jax import lax
from jax.experimental import pallas as pl
from jax.experimental.pallas import tpu as pltpu
from jax.sharding import PartitionSpec as P

LAGS = 1024
F_LO = 60
NSAMP = 15000
EPS = 1e-06
LANES = 128
SUBLANES = 8
FINE = 32
BLOCK = 256
VMEM_LIMIT = 16 * 1024 * 1024


def from_behind(block, axis, distance):
    devices = range(lax.axis_size(axis))
    route = [(i - distance, i) for i in devices if i - distance in devices]
    return lax.ppermute(block, axis, route)


def phases(bins, half_lags):
    turns = np.remainder(np.asarray(bins, np.int64)[:, None] * np.asarray(half_lags, np.int64)[None, :], 2 * NSAMP)
    angle = turns * (math.pi / NSAMP)
    return np.stack([np.cos(angle), np.sin(angle)]).astype(np.float32)


def split(value):
    high = value.astype(jnp.bfloat16)
    return high, (value - high.astype(jnp.float32)).astype(jnp.bfloat16)


def bin_power(x):
    x = x.astype(jnp.float32)
    return jnp.sum(x[0] * x[0] + x[1] * x[1], axis=-1, keepdims=True)


def power_kernel(x_ref, power_ref, copy_ref):
    for w in range(x_ref.shape[0]):
        x = x_ref[w]
        power_ref[w] = bin_power(x)
        copy_ref[w] = x


def partial_kernel(x_ref, power_ref):
    for w in range(x_ref.shape[0]):
        power_ref[w] = bin_power(x_ref[w])


def whiten_kernel(n_bins, x_ref, *refs):
    out_ref = refs[-1]
    for w in range(x_ref.shape[0]):
        power = bin_power(x_ref[w])
        for ref in refs[:-1]:
            power = power + ref[w]
        scale = lax.rsqrt(power / n_bins + EPS)
        for part in range(2):
            out_ref[w, part] = (x_ref[w, part].astype(jnp.float32) * scale).astype(jnp.bfloat16)


def keep_kernel(keep_ref, white_ref, out_ref):
    for w in range(white_ref.shape[0]):
        out_ref[w] = white_ref[w].astype(jnp.float32) * keep_ref[:, w:w + 1].astype(jnp.float32)[None]


def table_kernel(base_ref, table_ref):
    f_dev, width = table_ref.shape[1:]
    coarse = base_ref.shape[1] - FINE
    start = lax.axis_index("freq") * (f_dev // FINE)
    for block in range(0, width, BLOCK):
        lags = slice(block, block + BLOCK)
        fine_cos = base_ref[0, coarse:, lags]
        fine_sin = base_ref[1, coarse:, lags]

        def body(step, carry):
            first = pl.multiple_of(start + step * SUBLANES, SUBLANES)
            coarse_cos = base_ref[0, pl.ds(first, SUBLANES), lags]
            coarse_sin = base_ref[1, pl.ds(first, SUBLANES), lags]
            for n in range(SUBLANES):
                cos_a, sin_a = coarse_cos[n:n + 1], coarse_sin[n:n + 1]
                rows = pl.ds(pl.multiple_of((step * SUBLANES + n) * FINE, FINE), FINE)
                table_ref[0, rows, lags], table_ref[1, rows, lags] = split(cos_a * fine_cos - sin_a * fine_sin)
                table_ref[2, rows, lags], table_ref[3, rows, lags] = split(cos_a * fine_sin + sin_a * fine_cos)
            return carry

        lax.fori_loop(0, f_dev // (FINE * SUBLANES), body, 0)


def cross_tile(base_ref, partner_ref, lanes):
    w_dev, _, ch, _ = base_ref.shape
    real = [None] * ch
    imag = [None] * ch
    for w in range(w_dev):
        partner_re = partner_ref[w, 0, :, lanes].astype(jnp.float32)
        partner_im = partner_ref[w, 1, :, lanes].astype(jnp.float32)
        for i in range(ch):
            base_re = base_ref[w, 0, i:i + 1, lanes]
            base_im = base_ref[w, 1, i:i + 1, lanes]
            re = base_re * partner_re + base_im * partner_im
            im = base_im * partner_re - base_re * partner_im
            real[i] = re if w == 0 else real[i] + re
            imag[i] = im if w == 0 else imag[i] + im
    return real, imag


def pairs_kernel(n_partners, n_win, n_freq, base_ref, *refs):
    partner_refs = refs[:n_partners]
    twist_ref, table_ref = refs[n_partners:n_partners + 2]
    before_refs = refs[n_partners + 2:-2 - n_freq]
    out_refs = refs[-2 - n_freq:-2]
    rows_ref, sums_ref = refs[-2:]
    done = out_refs[0].shape[0] - n_partners
    for before_ref, out_ref in zip(before_refs, out_refs):
        out_ref[:done] = before_ref[...]
    ch, f_dev = base_ref.shape[2:]
    pairs = ch * ch
    groups = n_win * n_freq
    width = out_refs[0].shape[-1]
    freq, win = lax.axis_index("freq"), lax.axis_index("win")
    dot = functools.partial(jnp.dot, preferred_element_type=jnp.float32)
    count = n_partners * pairs

    def body(tile, carry):
        lanes = pl.ds(pl.multiple_of(tile * LANES, LANES), LANES)
        cos = twist_ref[freq, 0:1, lanes]
        sin = twist_ref[freq, 1:2, lanes]
        for k, partner_ref in enumerate(partner_refs):
            real, imag = cross_tile(base_ref, partner_ref, lanes)
            for i in range(0, ch, 2):
                rows = k * pairs + i * ch
                re = jnp.concatenate(real[i:i + 2], axis=0)
                im = jnp.concatenate(imag[i:i + 2], axis=0)
                for part, value in enumerate((re * cos + im * sin, im * cos - re * sin)):
                    high, low = split(value)
                    rows_ref[part, rows:rows + 2 * ch, lanes] = high
                    rows_ref[part, count + rows:count + rows + 2 * ch, lanes] = low
        return carry

    lax.fori_loop(0, f_dev // LANES, body, 0)
    for part in range(2):
        both = dot(rows_ref[part], table_ref[2 * part])
        sums_ref[part] = both[:count] + both[count:] + dot(rows_ref[part, :count], table_ref[2 * part + 1])
    for turn_freq, out_ref in enumerate(out_refs):
        for turn_win in range(n_win):
            owner = (win + turn_win) % n_win * n_freq + (freq + turn_freq) % n_freq
            upper = owner >= groups // 2
            block = jnp.where(upper, owner - groups // 2, groups // 2 - 1 - owner)
            sign = jnp.where(upper, -1.0, 1.0)
            lags = pl.ds(pl.multiple_of(block * width, LANES), width)
            for k in range(n_partners):
                rows = slice(k * pairs, (k + 1) * pairs)
                out_ref[done + k, turn_win] = sums_ref[0, rows, lags] + sign * sums_ref[1, rows, lags]


def add_kernel(n_parts, n_before, *refs):
    parts, befores, out_refs = refs[:n_parts], refs[n_parts:n_parts + n_before], refs[n_parts + n_before:]
    for turn, out_ref in enumerate(out_refs):
        start = 0
        for before in befores:
            out_ref[start:start + before.shape[0]] = before[:, turn].astype(out_ref.dtype)
            start += before.shape[0]
        total = parts[0][:, turn]
        for ref in parts[1:]:
            total = total + ref[:, turn]
        out_ref[start:] = total.astype(out_ref.dtype)


def plain_add_kernel(*refs):
    total = refs[0][...]
    for ref in refs[1:-1]:
        total = total + ref[...]
    refs[-1][...] = total


def reverse_lanes(value):
    backward = LANES - 1 - lax.broadcasted_iota(jnp.int32, (value.shape[0], LANES), 1)
    pieces = [
        jnp.take_along_axis(value[:, start:start + LANES], backward, axis=1, mode="promise_in_bounds")
        for start in range(0, value.shape[1], LANES)
    ]
    return jnp.concatenate(pieces[::-1], axis=1)


def combine_kernel(n_win, n_freq, factor_ref, *refs):
    out_ref = refs[-1]
    ch = out_ref.shape[0]
    lower = lax.axis_index("win") * n_freq + lax.axis_index("freq") < n_win * n_freq // 2
    k = 0
    for first in range(0, len(refs) - 1, n_win):
        parts = refs[first:first + n_win]
        for n in range(parts[0].shape[0]):
            total = parts[0][n].astype(jnp.float32)
            for ref in parts[1:]:
                total = total + ref[n].astype(jnp.float32)
            total = jnp.where(lower, reverse_lanes(total), total) * factor_ref[k]
            for i in range(ch):
                out_ref[i, k] = total[i * ch:(i + 1) * ch]
            k += 1


VMEM = pl.BlockSpec(memory_space=pltpu.VMEM)


def local(spectra, keep, pair_mask):
    w_dev, _, ch, f_dev = spectra.shape
    reach = pair_mask.shape[1] - 1
    n_chan, n_win, n_freq = (lax.axis_size(a) for a in ("chan", "win", "freq"))
    width = LAGS // (n_win * n_freq)
    n_bins = f_dev * n_freq
    params = pltpu.CompilerParams(vmem_limit_bytes=VMEM_LIMIT)


    def cost(flops, size):
        return pl.CostEstimate(flops=flops, bytes_accessed=size, transcendentals=0)

    below = from_behind(spectra, "chan", -1)
    far_routes = [[(c + away, c) for c in range(1, n_chan - away)] for away in range(2, reach)]
    power, copied = pl.pallas_call(
        power_kernel,
        out_shape=[
            jax.ShapeDtypeStruct((w_dev, ch, 1), jnp.float32),
            jax.ShapeDtypeStruct(spectra.shape, spectra.dtype),
        ],
        in_specs=[VMEM], out_specs=[VMEM] * 2, compiler_params=params, cost_estimate=cost(ch, ch),
    )(spectra)
    twist = phases(F_LO + np.arange(n_bins), np.ones(1)).reshape(2, n_freq, f_dev)
    twist = jnp.asarray(np.moveaxis(twist, 0, 1))

    def swap(power):
        routes = [[(f, (f + turn) % n_freq) for f in range(n_freq)] for turn in range(1, n_freq)]
        return [lax.ppermute(power, "freq", route) for route in routes]

    def half_power(block):
        return pl.pallas_call(
            partial_kernel,
            out_shape=jax.ShapeDtypeStruct(power.shape, jnp.float32),
            in_specs=[VMEM], out_specs=VMEM, compiler_params=params, cost_estimate=cost(ch, ch),
        )(block)

    def whiten(block, others):
        return pl.pallas_call(
            functools.partial(whiten_kernel, n_bins),
            out_shape=jax.ShapeDtypeStruct(block.shape, jnp.bfloat16),
            in_specs=[VMEM] * (1 + len(others)), out_specs=VMEM, compiler_params=params,
        )(block, *others)

    def kept(block):
        return pl.pallas_call(
            keep_kernel,
            out_shape=jax.ShapeDtypeStruct(block.shape, jnp.float32),
            in_specs=[VMEM] * 2, out_specs=VMEM, compiler_params=params,
        )(keep.reshape(1, w_dev), block)

    def pairs(base, partners, before=()):
        n = len(partners) + (before[0].shape[0] if before else 0)
        return pl.pallas_call(
            functools.partial(pairs_kernel, len(partners), n_win, n_freq),
            out_shape=[jax.ShapeDtypeStruct((n, n_win, ch * ch, width), jnp.float32)] * n_freq,
            in_specs=[VMEM] * (3 + len(partners) + len(before)), out_specs=[VMEM] * n_freq,
            scratch_shapes=[
                pltpu.VMEM((2, 2 * len(partners) * ch * ch, f_dev), jnp.bfloat16),
                pltpu.VMEM((2, len(partners) * ch * ch, LAGS // 2), jnp.float32),
            ],
            compiler_params=params,
            cost_estimate=cost(ch, ch),
        )(base, *partners, twist, table, *before)

    def turns(parts, axis, size):
        received = [parts[0]]
        for turn in range(1, size):
            route = [(g, (g + turn) % size) for g in range(size)]
            received.append(lax.ppermute(parts[turn], axis, route))
        return received

    def sum_bins(parts):
        return pl.pallas_call(
            plain_add_kernel,
            out_shape=jax.ShapeDtypeStruct(parts[0].shape, jnp.float32),
            in_specs=[VMEM] * n_freq, out_specs=VMEM, compiler_params=params,
        )(*turns(parts, "freq", n_freq))

    def split_windows(parts, before, kinds):
        n = sum(part.shape[0] for part in before) + parts[0].shape[0]
        return pl.pallas_call(
            functools.partial(add_kernel, n_freq, len(before)),
            out_shape=[jax.ShapeDtypeStruct((n, ch * ch, width), kind) for kind in kinds],
            in_specs=[VMEM] * (n_freq + len(before)), out_specs=[VMEM] * n_win, compiler_params=params,
        )(*turns(parts, "freq", n_freq), *before)

    white = whiten(copied, swap(power))
    far = [lax.ppermute(white, "chan", route) for route in far_routes]
    half_lags = 2 * np.arange(LAGS // 2) + 1
    coarse = phases(np.arange(0, n_bins, FINE), half_lags)
    fine = phases(F_LO + np.arange(FINE), half_lags)
    table = pl.pallas_call(
        table_kernel,
        out_shape=jax.ShapeDtypeStruct((4, f_dev, LAGS // 2), jnp.bfloat16),
        in_specs=[VMEM], out_specs=VMEM, compiler_params=params, cost_estimate=cost(ch, ch),
    )(jnp.asarray(np.concatenate([coarse, fine], axis=1)))
    own = kept(white)
    white, table, own = lax.optimization_barrier((white, table, own))
    above = from_behind(white, "chan", 1)
    first = pairs(own, [white])
    below, first = lax.optimization_barrier((below, first))
    below = whiten(below, swap(half_power(below)))
    parts = pairs(own, [below], first)
    far, parts = lax.optimization_barrier((far, parts))
    above, far = lax.optimization_barrier((above, far))
    base = kept(above)
    sums = split_windows(parts, [], [jnp.float32] + [jnp.bfloat16] * (n_win - 1))
    shipped = split_windows(pairs(base, [below] + far), [], [jnp.bfloat16] * n_win)
    received = turns(sums, "win", n_win)
    received.append(from_behind(shipped[0], "chan", -1))
    for turn in range(1, n_win):
        route = [
            (c * n_win + w, (c - 1) * n_win + (w + turn) % n_win) for c in range(1, n_chan) for w in range(n_win)
        ]
        received.append(lax.ppermute(shipped[turn], ("chan", "win"), route))
    scale = 1.0 / math.sqrt(w_dev * n_win * n_bins)
    factors = jnp.repeat(pair_mask.T.astype(jnp.float32) * scale, ch, axis=1)[..., None]
    return pl.pallas_call(
        functools.partial(combine_kernel, n_win, n_freq),
        out_shape=jax.ShapeDtypeStruct((ch, reach + 1, ch, width), jnp.float32),
        in_specs=[VMEM] * (1 + len(received)), out_specs=VMEM, compiler_params=params,
    )(factors, *received)


def solution(mesh):
    in_specs = (
        P("win", None, ("fibre", "chan"), "freq"),
        P(("fibre", "win")),
        P(("fibre", "chan"), None),
    )
    out_specs = P(("fibre", "chan"), None, None, ("win", "freq"))
    return jax.shard_map(local, mesh=mesh, in_specs=in_specs, out_specs=out_specs, check_vma=False)
```

```python
import functools
import math

import jax
import jax.numpy as jnp
import numpy as np
from jax import lax
from jax.experimental import pallas as pl
from jax.experimental.pallas import tpu as pltpu
from jax.sharding import PartitionSpec as P

LAGS = 1024
F_LO = 60
NSAMP = 15000
EPS = 1e-06
LANES = 128
SUBLANES = 8
FINE = 32
BLOCK = 256
VMEM_LIMIT = 16 * 1024 * 1024


def from_behind(block, axis, distance):
    devices = range(lax.axis_size(axis))
    route = [(i - distance, i) for i in devices if i - distance in devices]
    return lax.ppermute(block, axis, route)


def phases(bins, half_lags):
    turns = np.remainder(np.asarray(bins, np.int64)[:, None] * np.asarray(half_lags, np.int64)[None, :], 2 * NSAMP)
    angle = turns * (math.pi / NSAMP)
    return np.stack([np.cos(angle), np.sin(angle)]).astype(np.float32)


def split(value):
    high = value.astype(jnp.bfloat16)
    return high, (value - high.astype(jnp.float32)).astype(jnp.bfloat16)


def bin_power(x):
    x = x.astype(jnp.float32)
    return jnp.sum(x[0] * x[0] + x[1] * x[1], axis=-1, keepdims=True)


def power_kernel(x_ref, power_ref, copy_ref):
    for w in range(x_ref.shape[0]):
        x = x_ref[w]
        power_ref[w] = bin_power(x)
        copy_ref[w] = x


def partial_kernel(x_ref, power_ref):
    for w in range(x_ref.shape[0]):
        power_ref[w] = bin_power(x_ref[w])


def whiten_kernel(n_bins, x_ref, *refs):
    out_ref = refs[-1]
    for w in range(x_ref.shape[0]):
        power = bin_power(x_ref[w])
        for ref in refs[:-1]:
            power = power + ref[w]
        scale = lax.rsqrt(power / n_bins + EPS)
        for part in range(2):
            out_ref[w, part] = (x_ref[w, part].astype(jnp.float32) * scale).astype(jnp.bfloat16)


def keep_kernel(keep_ref, white_ref, out_ref):
    for w in range(white_ref.shape[0]):
        out_ref[w] = white_ref[w].astype(jnp.float32) * keep_ref[:, w:w + 1].astype(jnp.float32)[None]


def table_kernel(base_ref, table_ref):
    f_dev, width = table_ref.shape[1:]
    coarse = base_ref.shape[1] - FINE
    start = lax.axis_index("freq") * (f_dev // FINE)
    for block in range(0, width, BLOCK):
        lags = slice(block, block + BLOCK)
        fine_cos = base_ref[0, coarse:, lags]
        fine_sin = base_ref[1, coarse:, lags]

        def body(step, carry):
            first = pl.multiple_of(start + step * SUBLANES, SUBLANES)
            coarse_cos = base_ref[0, pl.ds(first, SUBLANES), lags]
            coarse_sin = base_ref[1, pl.ds(first, SUBLANES), lags]
            for n in range(SUBLANES):
                cos_a, sin_a = coarse_cos[n:n + 1], coarse_sin[n:n + 1]
                rows = pl.ds(pl.multiple_of((step * SUBLANES + n) * FINE, FINE), FINE)
                table_ref[0, rows, lags], table_ref[1, rows, lags] = split(cos_a * fine_cos - sin_a * fine_sin)
                table_ref[2, rows, lags], table_ref[3, rows, lags] = split(cos_a * fine_sin + sin_a * fine_cos)
            return carry

        lax.fori_loop(0, f_dev // (FINE * SUBLANES), body, 0)


def cross_tile(base_ref, partner_ref, lanes):
    w_dev, _, ch, _ = base_ref.shape
    real = [None] * ch
    imag = [None] * ch
    for w in range(w_dev):
        partner_re = partner_ref[w, 0, :, lanes].astype(jnp.float32)
        partner_im = partner_ref[w, 1, :, lanes].astype(jnp.float32)
        for i in range(ch):
            base_re = base_ref[w, 0, i:i + 1, lanes]
            base_im = base_ref[w, 1, i:i + 1, lanes]
            re = base_re * partner_re + base_im * partner_im
            im = base_im * partner_re - base_re * partner_im
            real[i] = re if w == 0 else real[i] + re
            imag[i] = im if w == 0 else imag[i] + im
    return real, imag


def pairs_kernel(n_partners, n_win, n_freq, base_ref, *refs):
    partner_refs = refs[:n_partners]
    twist_ref, table_ref = refs[n_partners:n_partners + 2]
    before_refs = refs[n_partners + 2:-2 - n_freq]
    out_refs = refs[-2 - n_freq:-2]
    rows_ref, sums_ref = refs[-2:]
    done = out_refs[0].shape[0] - n_partners
    for before_ref, out_ref in zip(before_refs, out_refs):
        out_ref[:done] = before_ref[...]
    ch, f_dev = base_ref.shape[2:]
    pairs = ch * ch
    groups = n_win * n_freq
    width = out_refs[0].shape[-1]
    freq, win = lax.axis_index("freq"), lax.axis_index("win")
    dot = functools.partial(jnp.dot, preferred_element_type=jnp.float32)
    count = n_partners * pairs

    def body(tile, carry):
        lanes = pl.ds(pl.multiple_of(tile * LANES, LANES), LANES)
        cos = twist_ref[freq, 0:1, lanes]
        sin = twist_ref[freq, 1:2, lanes]
        for k, partner_ref in enumerate(partner_refs):
            real, imag = cross_tile(base_ref, partner_ref, lanes)
            for i in range(0, ch, 2):
                rows = k * pairs + i * ch
                re = jnp.concatenate(real[i:i + 2], axis=0)
                im = jnp.concatenate(imag[i:i + 2], axis=0)
                for part, value in enumerate((re * cos + im * sin, im * cos - re * sin)):
                    high, low = split(value)
                    rows_ref[part, rows:rows + 2 * ch, lanes] = high
                    rows_ref[part, count + rows:count + rows + 2 * ch, lanes] = low
        return carry

    lax.fori_loop(0, f_dev // LANES, body, 0)
    for part in range(2):
        both = dot(rows_ref[part], table_ref[2 * part])
        sums_ref[part] = both[:count] + both[count:] + dot(rows_ref[part, :count], table_ref[2 * part + 1])
    for turn_freq, out_ref in enumerate(out_refs):
        for turn_win in range(n_win):
            owner = (win + turn_win) % n_win * n_freq + (freq + turn_freq) % n_freq
            upper = owner >= groups // 2
            block = jnp.where(upper, owner - groups // 2, groups // 2 - 1 - owner)
            sign = jnp.where(upper, -1.0, 1.0)
            lags = pl.ds(pl.multiple_of(block * width, LANES), width)
            for k in range(n_partners):
                rows = slice(k * pairs, (k + 1) * pairs)
                out_ref[done + k, turn_win] = sums_ref[0, rows, lags] + sign * sums_ref[1, rows, lags]


def add_kernel(n_parts, n_before, *refs):
    parts, befores, out_refs = refs[:n_parts], refs[n_parts:n_parts + n_before], refs[n_parts + n_before:]
    for turn, out_ref in enumerate(out_refs):
        start = 0
        for before in befores:
            out_ref[start:start + before.shape[0]] = before[:, turn].astype(out_ref.dtype)
            start += before.shape[0]
        total = parts[0][:, turn]
        for ref in parts[1:]:
            total = total + ref[:, turn]
        out_ref[start:] = total.astype(out_ref.dtype)


def plain_add_kernel(*refs):
    total = refs[0][...]
    for ref in refs[1:-1]:
        total = total + ref[...]
    refs[-1][...] = total


def reverse_lanes(value):
    backward = LANES - 1 - lax.broadcasted_iota(jnp.int32, (value.shape[0], LANES), 1)
    pieces = [
        jnp.take_along_axis(value[:, start:start + LANES], backward, axis=1, mode="promise_in_bounds")
        for start in range(0, value.shape[1], LANES)
    ]
    return jnp.concatenate(pieces[::-1], axis=1)


def combine_kernel(n_win, n_freq, factor_ref, *refs):
    out_ref = refs[-1]
    ch = out_ref.shape[0]
    lower = lax.axis_index("win") * n_freq + lax.axis_index("freq") < n_win * n_freq // 2
    k = 0
    for first in range(0, len(refs) - 1, n_win):
        parts = refs[first:first + n_win]
        for n in range(parts[0].shape[0]):
            total = parts[0][n].astype(jnp.float32)
            for ref in parts[1:]:
                total = total + ref[n].astype(jnp.float32)
            total = jnp.where(lower, reverse_lanes(total), total) * factor_ref[k]
            for i in range(ch):
                out_ref[i, k] = total[i * ch:(i + 1) * ch]
            k += 1


VMEM = pl.BlockSpec(memory_space=pltpu.VMEM)


def local(spectra, keep, pair_mask):
    w_dev, _, ch, f_dev = spectra.shape
    reach = pair_mask.shape[1] - 1
    n_chan, n_win, n_freq = (lax.axis_size(a) for a in ("chan", "win", "freq"))
    width = LAGS // (n_win * n_freq)
    n_bins = f_dev * n_freq
    params = pltpu.CompilerParams(vmem_limit_bytes=VMEM_LIMIT)


    def cost(flops, size):
        return pl.CostEstimate(flops=flops, bytes_accessed=size, transcendentals=0)

    below = from_behind(spectra, "chan", -1)
    far_routes = [[(c + away, c) for c in range(1, n_chan - away)] for away in range(2, reach)]
    power, copied = pl.pallas_call(
        power_kernel,
        out_shape=[
            jax.ShapeDtypeStruct((w_dev, ch, 1), jnp.float32),
            jax.ShapeDtypeStruct(spectra.shape, spectra.dtype),
        ],
        in_specs=[VMEM], out_specs=[VMEM] * 2, compiler_params=params, cost_estimate=cost(ch, ch),
    )(spectra)
    twist = phases(F_LO + np.arange(n_bins), np.ones(1)).reshape(2, n_freq, f_dev)
    twist = jnp.asarray(np.moveaxis(twist, 0, 1))

    def swap(power):
        routes = [[(f, (f + turn) % n_freq) for f in range(n_freq)] for turn in range(1, n_freq)]
        return [lax.ppermute(power, "freq", route) for route in routes]

    def half_power(block):
        return pl.pallas_call(
            partial_kernel,
            out_shape=jax.ShapeDtypeStruct(power.shape, jnp.float32),
            in_specs=[VMEM], out_specs=VMEM, compiler_params=params, cost_estimate=cost(ch, ch),
        )(block)

    def whiten(block, others):
        return pl.pallas_call(
            functools.partial(whiten_kernel, n_bins),
            out_shape=jax.ShapeDtypeStruct(block.shape, jnp.bfloat16),
            in_specs=[VMEM] * (1 + len(others)), out_specs=VMEM, compiler_params=params,
        )(block, *others)

    def kept(block):
        return pl.pallas_call(
            keep_kernel,
            out_shape=jax.ShapeDtypeStruct(block.shape, jnp.float32),
            in_specs=[VMEM] * 2, out_specs=VMEM, compiler_params=params,
        )(keep.reshape(1, w_dev), block)

    def pairs(base, partners, before=()):
        n = len(partners) + (before[0].shape[0] if before else 0)
        return pl.pallas_call(
            functools.partial(pairs_kernel, len(partners), n_win, n_freq),
            out_shape=[jax.ShapeDtypeStruct((n, n_win, ch * ch, width), jnp.float32)] * n_freq,
            in_specs=[VMEM] * (3 + len(partners) + len(before)), out_specs=[VMEM] * n_freq,
            scratch_shapes=[
                pltpu.VMEM((2, 2 * len(partners) * ch * ch, f_dev), jnp.bfloat16),
                pltpu.VMEM((2, len(partners) * ch * ch, LAGS // 2), jnp.float32),
            ],
            compiler_params=params,
            cost_estimate=cost(ch, ch),
        )(base, *partners, twist, table, *before)

    def turns(parts, axis, size):
        received = [parts[0]]
        for turn in range(1, size):
            route = [(g, (g + turn) % size) for g in range(size)]
            received.append(lax.ppermute(parts[turn], axis, route))
        return received

    def sum_bins(parts):
        return pl.pallas_call(
            plain_add_kernel,
            out_shape=jax.ShapeDtypeStruct(parts[0].shape, jnp.float32),
            in_specs=[VMEM] * n_freq, out_specs=VMEM, compiler_params=params,
        )(*turns(parts, "freq", n_freq))

    def split_windows(parts, before, kinds):
        n = sum(part.shape[0] for part in before) + parts[0].shape[0]
        return pl.pallas_call(
            functools.partial(add_kernel, n_freq, len(before)),
            out_shape=[jax.ShapeDtypeStruct((n, ch * ch, width), kind) for kind in kinds],
            in_specs=[VMEM] * (n_freq + len(before)), out_specs=[VMEM] * n_win, compiler_params=params,
        )(*turns(parts, "freq", n_freq), *before)

    white = whiten(copied, swap(power))
    far = [lax.ppermute(white, "chan", route) for route in far_routes]
    above = lax.ppermute(white, "chan", [(c - 1, c) for c in range(1, n_chan - 1)])
    half_lags = 2 * np.arange(LAGS // 2) + 1
    coarse = phases(np.arange(0, n_bins, FINE), half_lags)
    fine = phases(F_LO + np.arange(FINE), half_lags)
    white, ends = lax.optimization_barrier((white, jnp.asarray(np.concatenate([coarse, fine], axis=1))))
    table = pl.pallas_call(
        table_kernel,
        out_shape=jax.ShapeDtypeStruct((4, f_dev, LAGS // 2), jnp.bfloat16),
        in_specs=[VMEM], out_specs=VMEM, compiler_params=params, cost_estimate=cost(ch, ch),
    )(ends)
    own = kept(white)
    first = pairs(own, [white])
    below, first = lax.optimization_barrier((below, first))
    below = whiten(below, swap(half_power(below)))
    parts = pairs(own, [below], first)
    far, parts = lax.optimization_barrier((far, parts))
    above, far = lax.optimization_barrier((above, far))
    base = kept(above)
    sums = split_windows(parts, [], [jnp.float32] + [jnp.bfloat16] * (n_win - 1))
    shipped = split_windows(pairs(base, [below] + far), [], [jnp.bfloat16] * n_win)
    received = turns(sums, "win", n_win)
    received.append(lax.ppermute(shipped[0], "chan", [(c, c - 1) for c in range(1, n_chan - 1)]))
    for turn in range(1, n_win):
        route = [
            (c * n_win + w, (c - 1) * n_win + (w + turn) % n_win) for c in range(1, n_chan - 1) for w in range(n_win)
        ]
        received.append(lax.ppermute(shipped[turn], ("chan", "win"), route))
    scale = 1.0 / math.sqrt(w_dev * n_win * n_bins)
    factors = jnp.repeat(pair_mask.T.astype(jnp.float32) * scale, ch, axis=1)[..., None]
    return pl.pallas_call(
        functools.partial(combine_kernel, n_win, n_freq),
        out_shape=jax.ShapeDtypeStruct((ch, reach + 1, ch, width), jnp.float32),
        in_specs=[VMEM] * (1 + len(received)), out_specs=VMEM, compiler_params=params,
    )(factors, *received)


def solution(mesh):
    in_specs = (
        P("win", None, ("fibre", "chan"), "freq"),
        P(("fibre", "win")),
        P(("fibre", "chan"), None),
    )
    out_specs = P(("fibre", "chan"), None, None, ("win", "freq"))
    return jax.shard_map(local, mesh=mesh, in_specs=in_specs, out_specs=out_specs, check_vma=False)
```

```python
import functools
import math

import jax
import jax.numpy as jnp
import numpy as np
from jax import lax
from jax.experimental import pallas as pl
from jax.experimental.pallas import tpu as pltpu
from jax.sharding import PartitionSpec as P

LAGS = 1024
F_LO = 60
NSAMP = 15000
EPS = 1e-06
LANES = 128
SUBLANES = 8
FINE = 32
BLOCK = 256
VMEM_LIMIT = 16 * 1024 * 1024


def from_behind(block, axis, distance):
    devices = range(lax.axis_size(axis))
    route = [(i - distance, i) for i in devices if i - distance in devices]
    return lax.ppermute(block, axis, route)


def phases(bins, half_lags):
    turns = np.remainder(np.asarray(bins, np.int64)[:, None] * np.asarray(half_lags, np.int64)[None, :], 2 * NSAMP)
    angle = turns * (math.pi / NSAMP)
    return np.stack([np.cos(angle), np.sin(angle)]).astype(np.float32)


def split(value):
    high = value.astype(jnp.bfloat16)
    return high, (value - high.astype(jnp.float32)).astype(jnp.bfloat16)


def bin_power(x):
    x = x.astype(jnp.float32)
    return jnp.sum(x[0] * x[0] + x[1] * x[1], axis=-1, keepdims=True)


def power_kernel(x_ref, power_ref, copy_ref):
    for w in range(x_ref.shape[0]):
        x = x_ref[w]
        power_ref[w] = bin_power(x)
        copy_ref[w] = x


def partial_kernel(x_ref, power_ref):
    for w in range(x_ref.shape[0]):
        power_ref[w] = bin_power(x_ref[w])


def whiten_kernel(n_bins, x_ref, *refs):
    out_ref = refs[-1]
    for w in range(x_ref.shape[0]):
        power = bin_power(x_ref[w])
        for ref in refs[:-1]:
            power = power + ref[w]
        scale = lax.rsqrt(power / n_bins + EPS)
        for part in range(2):
            out_ref[w, part] = (x_ref[w, part].astype(jnp.float32) * scale).astype(jnp.bfloat16)


def keep_kernel(keep_ref, white_ref, out_ref):
    for w in range(white_ref.shape[0]):
        out_ref[w] = white_ref[w].astype(jnp.float32) * keep_ref[:, w:w + 1].astype(jnp.float32)[None]


def table_kernel(base_ref, table_ref):
    f_dev, width = table_ref.shape[1:]
    coarse = base_ref.shape[1] - FINE
    start = lax.axis_index("freq") * (f_dev // FINE)
    for block in range(0, width, BLOCK):
        lags = slice(block, block + BLOCK)
        fine_cos = base_ref[0, coarse:, lags]
        fine_sin = base_ref[1, coarse:, lags]

        def body(step, carry):
            first = pl.multiple_of(start + step * SUBLANES, SUBLANES)
            coarse_cos = base_ref[0, pl.ds(first, SUBLANES), lags]
            coarse_sin = base_ref[1, pl.ds(first, SUBLANES), lags]
            for n in range(SUBLANES):
                cos_a, sin_a = coarse_cos[n:n + 1], coarse_sin[n:n + 1]
                rows = pl.ds(pl.multiple_of((step * SUBLANES + n) * FINE, FINE), FINE)
                table_ref[0, rows, lags], table_ref[1, rows, lags] = split(cos_a * fine_cos - sin_a * fine_sin)
                table_ref[2, rows, lags], table_ref[3, rows, lags] = split(cos_a * fine_sin + sin_a * fine_cos)
            return carry

        lax.fori_loop(0, f_dev // (FINE * SUBLANES), body, 0)


def cross_tile(base_ref, partner_ref, lanes):
    w_dev, _, ch, _ = base_ref.shape
    real = [None] * ch
    imag = [None] * ch
    for w in range(w_dev):
        partner_re = partner_ref[w, 0, :, lanes].astype(jnp.float32)
        partner_im = partner_ref[w, 1, :, lanes].astype(jnp.float32)
        for i in range(ch):
            base_re = base_ref[w, 0, i:i + 1, lanes]
            base_im = base_ref[w, 1, i:i + 1, lanes]
            re = base_re * partner_re + base_im * partner_im
            im = base_im * partner_re - base_re * partner_im
            real[i] = re if w == 0 else real[i] + re
            imag[i] = im if w == 0 else imag[i] + im
    return real, imag


def pairs_kernel(n_partners, n_win, n_freq, base_ref, *refs):
    partner_refs = refs[:n_partners]
    twist_ref, table_ref = refs[n_partners:n_partners + 2]
    out_refs = refs[-2 - n_freq:-2]
    rows_ref, sums_ref = refs[-2:]
    ch, f_dev = base_ref.shape[2:]
    pairs = ch * ch
    groups = n_win * n_freq
    width = out_refs[0].shape[-1]
    freq, win = lax.axis_index("freq"), lax.axis_index("win")
    dot = functools.partial(jnp.dot, preferred_element_type=jnp.float32)
    count = n_partners * pairs

    def body(tile, carry):
        lanes = pl.ds(pl.multiple_of(tile * LANES, LANES), LANES)
        cos = twist_ref[freq, 0:1, lanes]
        sin = twist_ref[freq, 1:2, lanes]
        for k, partner_ref in enumerate(partner_refs):
            real, imag = cross_tile(base_ref, partner_ref, lanes)
            for i in range(0, ch, 2):
                rows = k * pairs + i * ch
                re = jnp.concatenate(real[i:i + 2], axis=0)
                im = jnp.concatenate(imag[i:i + 2], axis=0)
                for part, value in enumerate((re * cos + im * sin, im * cos - re * sin)):
                    high, low = split(value)
                    rows_ref[part, rows:rows + 2 * ch, lanes] = high
                    rows_ref[part, count + rows:count + rows + 2 * ch, lanes] = low
        return carry

    lax.fori_loop(0, f_dev // LANES, body, 0)
    for part in range(2):
        both = dot(rows_ref[part], table_ref[2 * part])
        sums_ref[part] = both[:count] + both[count:] + dot(rows_ref[part, :count], table_ref[2 * part + 1])
    for turn_freq, out_ref in enumerate(out_refs):
        for turn_win in range(n_win):
            owner = (win + turn_win) % n_win * n_freq + (freq + turn_freq) % n_freq
            upper = owner >= groups // 2
            block = jnp.where(upper, owner - groups // 2, groups // 2 - 1 - owner)
            sign = jnp.where(upper, -1.0, 1.0)
            lags = pl.ds(pl.multiple_of(block * width, LANES), width)
            for k in range(n_partners):
                rows = slice(k * pairs, (k + 1) * pairs)
                out_ref[k, turn_win] = sums_ref[0, rows, lags] + sign * sums_ref[1, rows, lags]


def add_kernel(n_parts, *refs):
    for turn, out_ref in enumerate(refs[n_parts:]):
        total = refs[0][:, turn]
        for ref in refs[1:n_parts]:
            total = total + ref[:, turn]
        out_ref[...] = total.astype(out_ref.dtype)


def total_kernel(*refs):
    total = refs[0][...]
    for ref in refs[1:-1]:
        total = total + ref[...].astype(jnp.float32)
    refs[-1][...] = total.astype(refs[-1].dtype)


def reverse_lanes(value):
    backward = LANES - 1 - lax.broadcasted_iota(jnp.int32, (value.shape[0], LANES), 1)
    pieces = [
        jnp.take_along_axis(value[:, start:start + LANES], backward, axis=1, mode="promise_in_bounds")
        for start in range(0, value.shape[1], LANES)
    ]
    return jnp.concatenate(pieces[::-1], axis=1)


def combine_kernel(n_win, n_freq, factor_ref, *refs):
    out_ref = refs[-1]
    ch = out_ref.shape[0]
    lower = lax.axis_index("win") * n_freq + lax.axis_index("freq") < n_win * n_freq // 2
    k = 0
    for parts in (refs[:n_win], refs[n_win:-1]):
        for n in range(parts[0].shape[0]):
            total = parts[0][n].astype(jnp.float32)
            for ref in parts[1:]:
                total = total + ref[n].astype(jnp.float32)
            total = jnp.where(lower, reverse_lanes(total), total) * factor_ref[k]
            for i in range(ch):
                out_ref[i, k] = total[i * ch:(i + 1) * ch]
            k += 1


VMEM = pl.BlockSpec(memory_space=pltpu.VMEM)


def local(spectra, keep, pair_mask):
    w_dev, _, ch, f_dev = spectra.shape
    reach = pair_mask.shape[1] - 1
    n_chan, n_win, n_freq = (lax.axis_size(a) for a in ("chan", "win", "freq"))
    width = LAGS // (n_win * n_freq)
    n_bins = f_dev * n_freq
    params = pltpu.CompilerParams(vmem_limit_bytes=VMEM_LIMIT)


    def cost(flops, size):
        return pl.CostEstimate(flops=flops, bytes_accessed=size, transcendentals=0)

    below = from_behind(spectra, "chan", -1)
    far_routes = [[(c + away, c) for c in range(1, n_chan - away)] for away in range(2, reach)]
    power, copied = pl.pallas_call(
        power_kernel,
        out_shape=[
            jax.ShapeDtypeStruct((w_dev, ch, 1), jnp.float32),
            jax.ShapeDtypeStruct(spectra.shape, spectra.dtype),
        ],
        in_specs=[VMEM], out_specs=[VMEM] * 2, compiler_params=params, cost_estimate=cost(ch, ch),
    )(spectra)
    twist = phases(F_LO + np.arange(n_bins), np.ones(1)).reshape(2, n_freq, f_dev)
    twist = jnp.asarray(np.moveaxis(twist, 0, 1))

    def swap(power):
        routes = [[(f, (f + turn) % n_freq) for f in range(n_freq)] for turn in range(1, n_freq)]
        return [lax.ppermute(power, "freq", route) for route in routes]

    def half_power(block):
        return pl.pallas_call(
            partial_kernel,
            out_shape=jax.ShapeDtypeStruct(power.shape, jnp.float32),
            in_specs=[VMEM], out_specs=VMEM, compiler_params=params, cost_estimate=cost(ch, ch),
        )(block)

    def whiten(block, others):
        return pl.pallas_call(
            functools.partial(whiten_kernel, n_bins),
            out_shape=jax.ShapeDtypeStruct(block.shape, jnp.bfloat16),
            in_specs=[VMEM] * (1 + len(others)), out_specs=VMEM, compiler_params=params,
        )(block, *others)

    def kept(block):
        return pl.pallas_call(
            keep_kernel,
            out_shape=jax.ShapeDtypeStruct(block.shape, jnp.float32),
            in_specs=[VMEM] * 2, out_specs=VMEM, compiler_params=params,
        )(keep.reshape(1, w_dev), block)

    def pairs(base, partners):
        n = len(partners)
        return pl.pallas_call(
            functools.partial(pairs_kernel, n, n_win, n_freq),
            out_shape=[jax.ShapeDtypeStruct((n, n_win, ch * ch, width), jnp.float32)] * n_freq,
            in_specs=[VMEM] * (3 + n), out_specs=[VMEM] * n_freq,
            scratch_shapes=[
                pltpu.VMEM((2, 2 * n * ch * ch, f_dev), jnp.bfloat16),
                pltpu.VMEM((2, n * ch * ch, LAGS // 2), jnp.float32),
            ],
            compiler_params=params,
            cost_estimate=cost(ch, ch),
        )(base, *partners, twist, table)

    def turns(parts, axis, size):
        received = [parts[0]]
        for turn in range(1, size):
            route = [(g, (g + turn) % size) for g in range(size)]
            received.append(lax.ppermute(parts[turn], axis, route))
        return received

    def split_windows(parts, kinds):
        n = parts[0].shape[0]
        return pl.pallas_call(
            functools.partial(add_kernel, n_freq),
            out_shape=[jax.ShapeDtypeStruct((n, ch * ch, width), kind) for kind in kinds],
            in_specs=[VMEM] * n_freq, out_specs=[VMEM] * n_win, compiler_params=params,
        )(*turns(parts, "freq", n_freq))

    white = whiten(copied, swap(power))
    far = [lax.ppermute(white, "chan", route) for route in far_routes]
    above = lax.ppermute(white, "chan", [(c - 1, c) for c in range(1, n_chan - 1)])
    half_lags = 2 * np.arange(LAGS // 2) + 1
    coarse = phases(np.arange(0, n_bins, FINE), half_lags)
    fine = phases(F_LO + np.arange(FINE), half_lags)
    white, ends = lax.optimization_barrier((white, jnp.asarray(np.concatenate([coarse, fine], axis=1))))
    table = pl.pallas_call(
        table_kernel,
        out_shape=jax.ShapeDtypeStruct((4, f_dev, LAGS // 2), jnp.bfloat16),
        in_specs=[VMEM], out_specs=VMEM, compiler_params=params, cost_estimate=cost(ch, ch),
    )(ends)
    own = kept(white)
    below = whiten(below, swap(half_power(below)))
    parts = pairs(own, [white, below])
    far, parts = lax.optimization_barrier((far, parts))
    above, far = lax.optimization_barrier((above, far))
    kinds = [jnp.float32] + [jnp.bfloat16] * (n_win - 1)
    near = turns(split_windows(parts, kinds), "win", n_win)
    remote = turns(split_windows(pairs(kept(above), [below] + far), kinds), "win", n_win)
    shipped = pl.pallas_call(
        total_kernel,
        out_shape=jax.ShapeDtypeStruct(remote[0].shape, jnp.bfloat16),
        in_specs=[VMEM] * n_win, out_specs=VMEM, compiler_params=params,
    )(*remote)
    shipped = lax.ppermute(shipped, "chan", [(c, c - 1) for c in range(1, n_chan - 1)])
    scale = 1.0 / math.sqrt(w_dev * n_win * n_bins)
    factors = jnp.repeat(pair_mask.T.astype(jnp.float32) * scale, ch, axis=1)[..., None]
    return pl.pallas_call(
        functools.partial(combine_kernel, n_win, n_freq),
        out_shape=jax.ShapeDtypeStruct((ch, reach + 1, ch, width), jnp.float32),
        in_specs=[VMEM] * (2 + n_win), out_specs=VMEM, compiler_params=params,
    )(factors, *near, shipped)


def solution(mesh):
    in_specs = (
        P("win", None, ("fibre", "chan"), "freq"),
        P(("fibre", "win")),
        P(("fibre", "chan"), None),
    )
    out_specs = P(("fibre", "chan"), None, None, ("win", "freq"))
    return jax.shard_map(local, mesh=mesh, in_specs=in_specs, out_specs=out_specs, check_vma=False)
```

```python
import functools
import math

import jax
import jax.numpy as jnp
import numpy as np
from jax import lax
from jax.experimental import pallas as pl
from jax.experimental.pallas import tpu as pltpu
from jax.sharding import PartitionSpec as P

LAGS = 1024
F_LO = 60
NSAMP = 15000
EPS = 1e-06
LANES = 128
SUBLANES = 8
FINE = 32
BLOCK = 256
VMEM_LIMIT = 16 * 1024 * 1024


def from_behind(block, axis, distance):
    devices = range(lax.axis_size(axis))
    route = [(i - distance, i) for i in devices if i - distance in devices]
    return lax.ppermute(block, axis, route)


def phases(bins, half_lags):
    turns = np.remainder(np.asarray(bins, np.int64)[:, None] * np.asarray(half_lags, np.int64)[None, :], 2 * NSAMP)
    angle = turns * (math.pi / NSAMP)
    return np.stack([np.cos(angle), np.sin(angle)]).astype(np.float32)


def split(value):
    high = value.astype(jnp.bfloat16)
    return high, (value - high.astype(jnp.float32)).astype(jnp.bfloat16)


def bin_power(x):
    x = x.astype(jnp.float32)
    return jnp.sum(x[0] * x[0] + x[1] * x[1], axis=-1, keepdims=True)


def power_kernel(x_ref, power_ref, copy_ref):
    for w in range(x_ref.shape[0]):
        x = x_ref[w]
        power_ref[w] = bin_power(x)
        copy_ref[w] = x


def partial_kernel(x_ref, power_ref):
    for w in range(x_ref.shape[0]):
        power_ref[w] = bin_power(x_ref[w])


def whiten_kernel(n_bins, x_ref, *refs):
    out_ref = refs[-1]
    for w in range(x_ref.shape[0]):
        power = bin_power(x_ref[w])
        for ref in refs[:-1]:
            power = power + ref[w]
        scale = lax.rsqrt(power / n_bins + EPS)
        for part in range(2):
            out_ref[w, part] = (x_ref[w, part].astype(jnp.float32) * scale).astype(jnp.bfloat16)


def keep_kernel(keep_ref, white_ref, out_ref):
    for w in range(white_ref.shape[0]):
        out_ref[w] = white_ref[w].astype(jnp.float32) * keep_ref[:, w:w + 1].astype(jnp.float32)[None]


def table_kernel(base_ref, table_ref):
    f_dev, width = table_ref.shape[1:]
    coarse = base_ref.shape[1] - FINE
    start = lax.axis_index("freq") * (f_dev // FINE)
    for block in range(0, width, BLOCK):
        lags = slice(block, block + BLOCK)
        fine_cos = base_ref[0, coarse:, lags]
        fine_sin = base_ref[1, coarse:, lags]

        def body(step, carry):
            first = pl.multiple_of(start + step * SUBLANES, SUBLANES)
            coarse_cos = base_ref[0, pl.ds(first, SUBLANES), lags]
            coarse_sin = base_ref[1, pl.ds(first, SUBLANES), lags]
            for n in range(SUBLANES):
                cos_a, sin_a = coarse_cos[n:n + 1], coarse_sin[n:n + 1]
                rows = pl.ds(pl.multiple_of((step * SUBLANES + n) * FINE, FINE), FINE)
                table_ref[0, rows, lags], table_ref[1, rows, lags] = split(cos_a * fine_cos - sin_a * fine_sin)
                table_ref[2, rows, lags], table_ref[3, rows, lags] = split(cos_a * fine_sin + sin_a * fine_cos)
            return carry

        lax.fori_loop(0, f_dev // (FINE * SUBLANES), body, 0)


def cross_tile(base_ref, partner_ref, lanes):
    w_dev, _, ch, _ = base_ref.shape
    real = [None] * ch
    imag = [None] * ch
    for w in range(w_dev):
        partner_re = partner_ref[w, 0, :, lanes].astype(jnp.float32)
        partner_im = partner_ref[w, 1, :, lanes].astype(jnp.float32)
        for i in range(ch):
            base_re = base_ref[w, 0, i:i + 1, lanes]
            base_im = base_ref[w, 1, i:i + 1, lanes]
            re = base_re * partner_re + base_im * partner_im
            im = base_im * partner_re - base_re * partner_im
            real[i] = re if w == 0 else real[i] + re
            imag[i] = im if w == 0 else imag[i] + im
    return real, imag


def pairs_kernel(n_partners, n_win, n_freq, by_window, base_ref, *refs):
    partner_refs = refs[:n_partners]
    twist_ref, table_ref = refs[n_partners:n_partners + 2]
    out_refs = refs[-2 - n_freq:-2]
    rows_ref, sums_ref = refs[-2:]
    ch, f_dev = base_ref.shape[2:]
    pairs = ch * ch
    groups = n_win * n_freq
    width = out_refs[0].shape[-1]
    freq, win = lax.axis_index("freq"), lax.axis_index("win")
    dot = functools.partial(jnp.dot, preferred_element_type=jnp.float32)
    count = n_partners * pairs

    def body(tile, carry):
        lanes = pl.ds(pl.multiple_of(tile * LANES, LANES), LANES)
        cos = twist_ref[freq, 0:1, lanes]
        sin = twist_ref[freq, 1:2, lanes]
        for k, partner_ref in enumerate(partner_refs):
            real, imag = cross_tile(base_ref, partner_ref, lanes)
            for i in range(0, ch, 2):
                rows = k * pairs + i * ch
                re = jnp.concatenate(real[i:i + 2], axis=0)
                im = jnp.concatenate(imag[i:i + 2], axis=0)
                for part, value in enumerate((re * cos + im * sin, im * cos - re * sin)):
                    high, low = split(value)
                    rows_ref[part, rows:rows + 2 * ch, lanes] = high
                    rows_ref[part, count + rows:count + rows + 2 * ch, lanes] = low
        return carry

    lax.fori_loop(0, f_dev // LANES, body, 0)
    for part in range(2):
        both = dot(rows_ref[part], table_ref[2 * part])
        sums_ref[part] = both[:count] + both[count:] + dot(rows_ref[part, :count], table_ref[2 * part + 1])
    for turn_freq, out_ref in enumerate(out_refs):
        core = (freq + turn_freq) % n_freq
        for turn_win in range(n_win):
            if by_window:
                away = turn_win // n_freq * n_freq + core
                owner = (win + away) % n_win * n_freq + (core + turn_win) % n_freq
            else:
                owner = (win + turn_win) % n_win * n_freq + core
            upper = owner >= groups // 2
            block = jnp.where(upper, owner - groups // 2, groups // 2 - 1 - owner)
            sign = jnp.where(upper, -1.0, 1.0)
            lags = pl.ds(pl.multiple_of(block * width, LANES), width)
            for k in range(n_partners):
                rows = slice(k * pairs, (k + 1) * pairs)
                out_ref[k, turn_win] = sums_ref[0, rows, lags] + sign * sums_ref[1, rows, lags]


def add_kernel(n_parts, *refs):
    for turn, out_ref in enumerate(refs[n_parts:]):
        total = refs[0][:, turn]
        for ref in refs[1:n_parts]:
            total = total + ref[:, turn]
        out_ref[...] = total.astype(out_ref.dtype)


def group_kernel(n_parts, *refs):
    out_refs = refs[n_parts:]
    per_ship = refs[0].shape[1] // len(out_refs)
    for ship, out_ref in enumerate(out_refs):
        for turn in range(per_ship):
            total = refs[0][:, ship * per_ship + turn]
            for ref in refs[1:n_parts]:
                total = total + ref[:, ship * per_ship + turn]
            out_ref[turn] = total.astype(out_ref.dtype)


def ungroup_kernel(n_ships, *refs):
    for turn, out_ref in enumerate(refs[n_ships:]):
        total = refs[0][turn].astype(jnp.float32)
        for ref in refs[1:n_ships]:
            total = total + ref[turn].astype(jnp.float32)
        out_ref[...] = total


def reverse_lanes(value):
    backward = LANES - 1 - lax.broadcasted_iota(jnp.int32, (value.shape[0], LANES), 1)
    pieces = [
        jnp.take_along_axis(value[:, start:start + LANES], backward, axis=1, mode="promise_in_bounds")
        for start in range(0, value.shape[1], LANES)
    ]
    return jnp.concatenate(pieces[::-1], axis=1)


def combine_kernel(n_win, n_freq, factor_ref, *refs):
    out_ref = refs[-1]
    ch = out_ref.shape[0]
    lower = lax.axis_index("win") * n_freq + lax.axis_index("freq") < n_win * n_freq // 2
    k = 0
    for parts in (refs[:n_win], refs[n_win:-1]):
        for n in range(parts[0].shape[0]):
            total = parts[0][n].astype(jnp.float32)
            for ref in parts[1:]:
                total = total + ref[n].astype(jnp.float32)
            total = jnp.where(lower, reverse_lanes(total), total) * factor_ref[k]
            for i in range(ch):
                out_ref[i, k] = total[i * ch:(i + 1) * ch]
            k += 1


VMEM = pl.BlockSpec(memory_space=pltpu.VMEM)


def local(spectra, keep, pair_mask):
    w_dev, _, ch, f_dev = spectra.shape
    reach = pair_mask.shape[1] - 1
    n_chan, n_win, n_freq = (lax.axis_size(a) for a in ("chan", "win", "freq"))
    width = LAGS // (n_win * n_freq)
    n_bins = f_dev * n_freq
    params = pltpu.CompilerParams(vmem_limit_bytes=VMEM_LIMIT)


    def cost(flops, size):
        return pl.CostEstimate(flops=flops, bytes_accessed=size, transcendentals=0)

    below = from_behind(spectra, "chan", -1)
    far_routes = [[(c + away, c) for c in range(1, n_chan - away)] for away in range(2, reach)]
    power, copied = pl.pallas_call(
        power_kernel,
        out_shape=[
            jax.ShapeDtypeStruct((w_dev, ch, 1), jnp.float32),
            jax.ShapeDtypeStruct(spectra.shape, spectra.dtype),
        ],
        in_specs=[VMEM], out_specs=[VMEM] * 2, compiler_params=params, cost_estimate=cost(ch, ch),
    )(spectra)
    twist = phases(F_LO + np.arange(n_bins), np.ones(1)).reshape(2, n_freq, f_dev)
    twist = jnp.asarray(np.moveaxis(twist, 0, 1))

    def swap(power):
        routes = [[(f, (f + turn) % n_freq) for f in range(n_freq)] for turn in range(1, n_freq)]
        return [lax.ppermute(power, "freq", route) for route in routes]

    def half_power(block):
        return pl.pallas_call(
            partial_kernel,
            out_shape=jax.ShapeDtypeStruct(power.shape, jnp.float32),
            in_specs=[VMEM], out_specs=VMEM, compiler_params=params, cost_estimate=cost(ch, ch),
        )(block)

    def whiten(block, others):
        return pl.pallas_call(
            functools.partial(whiten_kernel, n_bins),
            out_shape=jax.ShapeDtypeStruct(block.shape, jnp.bfloat16),
            in_specs=[VMEM] * (1 + len(others)), out_specs=VMEM, compiler_params=params,
        )(block, *others)

    def kept(block):
        return pl.pallas_call(
            keep_kernel,
            out_shape=jax.ShapeDtypeStruct(block.shape, jnp.float32),
            in_specs=[VMEM] * 2, out_specs=VMEM, compiler_params=params,
        )(keep.reshape(1, w_dev), block)

    def pairs(base, partners, by_window):
        n = len(partners)
        return pl.pallas_call(
            functools.partial(pairs_kernel, n, n_win, n_freq, by_window),
            out_shape=[jax.ShapeDtypeStruct((n, n_win, ch * ch, width), jnp.float32)] * n_freq,
            in_specs=[VMEM] * (3 + n), out_specs=[VMEM] * n_freq,
            scratch_shapes=[
                pltpu.VMEM((2, 2 * n * ch * ch, f_dev), jnp.bfloat16),
                pltpu.VMEM((2, n * ch * ch, LAGS // 2), jnp.float32),
            ],
            compiler_params=params,
            cost_estimate=cost(ch, ch),
        )(base, *partners, twist, table)

    def turns(parts, axis, size):
        received = [parts[0]]
        for turn in range(1, size):
            route = [(g, (g + turn) % size) for g in range(size)]
            received.append(lax.ppermute(parts[turn], axis, route))
        return received

    def split_windows(parts, kinds):
        n = parts[0].shape[0]
        return pl.pallas_call(
            functools.partial(add_kernel, n_freq),
            out_shape=[jax.ShapeDtypeStruct((n, ch * ch, width), kind) for kind in kinds],
            in_specs=[VMEM] * n_freq, out_specs=[VMEM] * n_win, compiler_params=params,
        )(*turns(parts, "freq", n_freq))

    white = whiten(copied, swap(power))
    far = [lax.ppermute(white, "chan", route) for route in far_routes]
    above = lax.ppermute(white, "chan", [(c - 1, c) for c in range(1, n_chan - 1)])
    half_lags = 2 * np.arange(LAGS // 2) + 1
    coarse = phases(np.arange(0, n_bins, FINE), half_lags)
    fine = phases(F_LO + np.arange(FINE), half_lags)
    white, ends = lax.optimization_barrier((white, jnp.asarray(np.concatenate([coarse, fine], axis=1))))
    table = pl.pallas_call(
        table_kernel,
        out_shape=jax.ShapeDtypeStruct((4, f_dev, LAGS // 2), jnp.bfloat16),
        in_specs=[VMEM], out_specs=VMEM, compiler_params=params, cost_estimate=cost(ch, ch),
    )(ends)
    own = kept(white)
    below = whiten(below, swap(half_power(below)))
    parts = pairs(own, [white, below], False)
    far, parts = lax.optimization_barrier((far, parts))
    above, far = lax.optimization_barrier((above, far))
    kinds = [jnp.float32] + [jnp.bfloat16] * (n_win - 1)
    near = turns(split_windows(parts, kinds), "win", n_win)
    remote = turns(pairs(kept(above), [below] + far, True), "freq", n_freq)
    shape = (remote[0].shape[0], ch * ch, width)
    n_ships = n_win // n_freq
    shipped = pl.pallas_call(
        functools.partial(group_kernel, n_freq),
        out_shape=[jax.ShapeDtypeStruct((n_freq,) + shape, jnp.bfloat16)] * n_ships,
        in_specs=[VMEM] * n_freq, out_specs=[VMEM] * n_ships, compiler_params=params,
    )(*remote)
    arrived = []
    for ship, block in enumerate(shipped):
        route = [
            ((c * n_win + w) * n_freq + f, ((c - 1) * n_win + (w + ship * n_freq + f) % n_win) * n_freq + f)
            for c in range(1, n_chan - 1) for w in range(n_win) for f in range(n_freq)
        ]
        arrived.append(lax.ppermute(block, ("chan", "win", "freq"), route))
    arrived = pl.pallas_call(
        functools.partial(ungroup_kernel, n_ships),
        out_shape=[jax.ShapeDtypeStruct(shape, jnp.float32)] * n_freq,
        in_specs=[VMEM] * n_ships, out_specs=[VMEM] * n_freq, compiler_params=params,
    )(*arrived)
    arrived = turns(arrived, "freq", n_freq)
    scale = 1.0 / math.sqrt(w_dev * n_win * n_bins)
    factors = jnp.repeat(pair_mask.T.astype(jnp.float32) * scale, ch, axis=1)[..., None]
    return pl.pallas_call(
        functools.partial(combine_kernel, n_win, n_freq),
        out_shape=jax.ShapeDtypeStruct((ch, reach + 1, ch, width), jnp.float32),
        in_specs=[VMEM] * (1 + n_win + n_freq), out_specs=VMEM, compiler_params=params,
    )(factors, *near, *arrived)


def solution(mesh):
    in_specs = (
        P("win", None, ("fibre", "chan"), "freq"),
        P(("fibre", "win")),
        P(("fibre", "chan"), None),
    )
    out_specs = P(("fibre", "chan"), None, None, ("win", "freq"))
    return jax.shard_map(local, mesh=mesh, in_specs=in_specs, out_specs=out_specs, check_vma=False)
```

```python
import functools
import math

import jax
import jax.numpy as jnp
import numpy as np
from jax import lax
from jax.experimental import pallas as pl
from jax.experimental.pallas import tpu as pltpu
from jax.sharding import PartitionSpec as P

LAGS = 1024
F_LO = 60
NSAMP = 15000
EPS = 1e-06
LANES = 128
SUBLANES = 8
FINE = 32
BLOCK = 256
VMEM_LIMIT = 16 * 1024 * 1024


def from_behind(block, axis, distance):
    devices = range(lax.axis_size(axis))
    route = [(i - distance, i) for i in devices if i - distance in devices]
    return lax.ppermute(block, axis, route)


def phases(bins, half_lags):
    turns = np.remainder(np.asarray(bins, np.int64)[:, None] * np.asarray(half_lags, np.int64)[None, :], 2 * NSAMP)
    angle = turns * (math.pi / NSAMP)
    return np.stack([np.cos(angle), np.sin(angle)]).astype(np.float32)


def split(value):
    high = value.astype(jnp.bfloat16)
    return high, (value - high.astype(jnp.float32)).astype(jnp.bfloat16)


def bin_power(x):
    x = x.astype(jnp.float32)
    return jnp.sum(x[0] * x[0] + x[1] * x[1], axis=-1, keepdims=True)


def power_kernel(x_ref, power_ref, copy_ref):
    for w in range(x_ref.shape[0]):
        x = x_ref[w]
        power_ref[w] = bin_power(x)
        copy_ref[w] = x


def partial_kernel(x_ref, power_ref):
    for w in range(x_ref.shape[0]):
        power_ref[w] = bin_power(x_ref[w])


def whiten_kernel(n_bins, x_ref, *refs):
    out_ref = refs[-1]
    for w in range(x_ref.shape[0]):
        power = bin_power(x_ref[w])
        for ref in refs[:-1]:
            power = power + ref[w]
        scale = lax.rsqrt(power / n_bins + EPS)
        for part in range(2):
            out_ref[w, part] = (x_ref[w, part].astype(jnp.float32) * scale).astype(jnp.bfloat16)


def keep_kernel(keep_ref, white_ref, out_ref):
    for w in range(white_ref.shape[0]):
        out_ref[w] = white_ref[w].astype(jnp.float32) * keep_ref[:, w:w + 1].astype(jnp.float32)[None]


def table_kernel(base_ref, table_ref):
    f_dev, width = table_ref.shape[1:]
    coarse = base_ref.shape[1] - FINE
    start = lax.axis_index("freq") * (f_dev // FINE)
    for block in range(0, width, BLOCK):
        lags = slice(block, block + BLOCK)
        fine_cos = base_ref[0, coarse:, lags]
        fine_sin = base_ref[1, coarse:, lags]

        def body(step, carry):
            first = pl.multiple_of(start + step * SUBLANES, SUBLANES)
            coarse_cos = base_ref[0, pl.ds(first, SUBLANES), lags]
            coarse_sin = base_ref[1, pl.ds(first, SUBLANES), lags]
            for n in range(SUBLANES):
                cos_a, sin_a = coarse_cos[n:n + 1], coarse_sin[n:n + 1]
                rows = pl.ds(pl.multiple_of((step * SUBLANES + n) * FINE, FINE), FINE)
                table_ref[0, rows, lags], table_ref[1, rows, lags] = split(cos_a * fine_cos - sin_a * fine_sin)
                table_ref[2, rows, lags], table_ref[3, rows, lags] = split(cos_a * fine_sin + sin_a * fine_cos)
            return carry

        lax.fori_loop(0, f_dev // (FINE * SUBLANES), body, 0)


def cross_tile(base_ref, partner_ref, lanes):
    w_dev, _, ch, _ = base_ref.shape
    real = [None] * ch
    imag = [None] * ch
    for w in range(w_dev):
        partner_re = partner_ref[w, 0, :, lanes].astype(jnp.float32)
        partner_im = partner_ref[w, 1, :, lanes].astype(jnp.float32)
        for i in range(ch):
            base_re = base_ref[w, 0, i:i + 1, lanes]
            base_im = base_ref[w, 1, i:i + 1, lanes]
            re = base_re * partner_re + base_im * partner_im
            im = base_im * partner_re - base_re * partner_im
            real[i] = re if w == 0 else real[i] + re
            imag[i] = im if w == 0 else imag[i] + im
    return real, imag


def pairs_kernel(n_partners, n_win, n_freq, by_window, base_ref, *refs):
    partner_refs = refs[:n_partners]
    twist_ref, table_ref = refs[n_partners:n_partners + 2]
    before_refs = refs[n_partners + 2:-2 - n_freq]
    out_refs = refs[-2 - n_freq:-2]
    rows_ref, sums_ref = refs[-2:]
    done = out_refs[0].shape[0] - n_partners
    for before_ref, out_ref in zip(before_refs, out_refs):
        out_ref[:done] = before_ref[...]
    ch, f_dev = base_ref.shape[2:]
    pairs = ch * ch
    groups = n_win * n_freq
    width = out_refs[0].shape[-1]
    freq, win = lax.axis_index("freq"), lax.axis_index("win")
    dot = functools.partial(jnp.dot, preferred_element_type=jnp.float32)
    count = n_partners * pairs

    def body(tile, carry):
        lanes = pl.ds(pl.multiple_of(tile * LANES, LANES), LANES)
        cos = twist_ref[freq, 0:1, lanes]
        sin = twist_ref[freq, 1:2, lanes]
        for k, partner_ref in enumerate(partner_refs):
            real, imag = cross_tile(base_ref, partner_ref, lanes)
            for i in range(0, ch, 2):
                rows = k * pairs + i * ch
                re = jnp.concatenate(real[i:i + 2], axis=0)
                im = jnp.concatenate(imag[i:i + 2], axis=0)
                for part, value in enumerate((re * cos + im * sin, im * cos - re * sin)):
                    high, low = split(value)
                    rows_ref[part, rows:rows + 2 * ch, lanes] = high
                    rows_ref[part, count + rows:count + rows + 2 * ch, lanes] = low
        return carry

    lax.fori_loop(0, f_dev // LANES, body, 0)
    for part in range(2):
        both = dot(rows_ref[part], table_ref[2 * part])
        sums_ref[part] = both[:count] + both[count:] + dot(rows_ref[part, :count], table_ref[2 * part + 1])
    for turn_freq, out_ref in enumerate(out_refs):
        core = (freq + turn_freq) % n_freq
        for turn_win in range(n_win):
            if by_window:
                away = turn_win // n_freq * n_freq + core
                owner = (win + away) % n_win * n_freq + (core + turn_win) % n_freq
            else:
                owner = (win + turn_win) % n_win * n_freq + core
            upper = owner >= groups // 2
            block = jnp.where(upper, owner - groups // 2, groups // 2 - 1 - owner)
            sign = jnp.where(upper, -1.0, 1.0)
            lags = pl.ds(pl.multiple_of(block * width, LANES), width)
            for k in range(n_partners):
                rows = slice(k * pairs, (k + 1) * pairs)
                out_ref[done + k, turn_win] = sums_ref[0, rows, lags] + sign * sums_ref[1, rows, lags]


def add_kernel(n_parts, *refs):
    for turn, out_ref in enumerate(refs[n_parts:]):
        total = refs[0][:, turn]
        for ref in refs[1:n_parts]:
            total = total + ref[:, turn]
        out_ref[...] = total.astype(out_ref.dtype)


def group_kernel(n_parts, *refs):
    out_refs = refs[n_parts:]
    per_ship = refs[0].shape[1] // len(out_refs)
    for ship, out_ref in enumerate(out_refs):
        for turn in range(per_ship):
            total = refs[0][:, ship * per_ship + turn]
            for ref in refs[1:n_parts]:
                total = total + ref[:, ship * per_ship + turn]
            out_ref[turn] = total.astype(out_ref.dtype)


def ungroup_kernel(n_ships, *refs):
    for turn, out_ref in enumerate(refs[n_ships:]):
        total = refs[0][turn].astype(jnp.float32)
        for ref in refs[1:n_ships]:
            total = total + ref[turn].astype(jnp.float32)
        out_ref[...] = total


def reverse_lanes(value):
    backward = LANES - 1 - lax.broadcasted_iota(jnp.int32, (value.shape[0], LANES), 1)
    pieces = [
        jnp.take_along_axis(value[:, start:start + LANES], backward, axis=1, mode="promise_in_bounds")
        for start in range(0, value.shape[1], LANES)
    ]
    return jnp.concatenate(pieces[::-1], axis=1)


def combine_kernel(n_win, n_freq, factor_ref, *refs):
    out_ref = refs[-1]
    ch = out_ref.shape[0]
    lower = lax.axis_index("win") * n_freq + lax.axis_index("freq") < n_win * n_freq // 2
    k = 0
    for parts in (refs[:n_win], refs[n_win:-1]):
        for n in range(parts[0].shape[0]):
            total = parts[0][n].astype(jnp.float32)
            for ref in parts[1:]:
                total = total + ref[n].astype(jnp.float32)
            total = jnp.where(lower, reverse_lanes(total), total) * factor_ref[k]
            for i in range(ch):
                out_ref[i, k] = total[i * ch:(i + 1) * ch]
            k += 1


VMEM = pl.BlockSpec(memory_space=pltpu.VMEM)


def local(spectra, keep, pair_mask):
    w_dev, _, ch, f_dev = spectra.shape
    reach = pair_mask.shape[1] - 1
    n_chan, n_win, n_freq = (lax.axis_size(a) for a in ("chan", "win", "freq"))
    width = LAGS // (n_win * n_freq)
    n_bins = f_dev * n_freq
    params = pltpu.CompilerParams(vmem_limit_bytes=VMEM_LIMIT)


    def cost(flops, size):
        return pl.CostEstimate(flops=flops, bytes_accessed=size, transcendentals=0)

    far_routes = [[(c + away, c) for c in range(1, n_chan - away)] for away in range(2, reach)]
    far = [lax.ppermute(spectra, "chan", route) for route in far_routes]
    power, copied = pl.pallas_call(
        power_kernel,
        out_shape=[
            jax.ShapeDtypeStruct((w_dev, ch, 1), jnp.float32),
            jax.ShapeDtypeStruct(spectra.shape, spectra.dtype),
        ],
        in_specs=[VMEM], out_specs=[VMEM] * 2, compiler_params=params, cost_estimate=cost(ch, ch),
    )(spectra)
    twist = phases(F_LO + np.arange(n_bins), np.ones(1)).reshape(2, n_freq, f_dev)
    twist = jnp.asarray(np.moveaxis(twist, 0, 1))

    def swap(power):
        routes = [[(f, (f + turn) % n_freq) for f in range(n_freq)] for turn in range(1, n_freq)]
        return [lax.ppermute(power, "freq", route) for route in routes]

    def half_power(block):
        return pl.pallas_call(
            partial_kernel,
            out_shape=jax.ShapeDtypeStruct(power.shape, jnp.float32),
            in_specs=[VMEM], out_specs=VMEM, compiler_params=params, cost_estimate=cost(ch, ch),
        )(block)

    def whiten(block, others):
        return pl.pallas_call(
            functools.partial(whiten_kernel, n_bins),
            out_shape=jax.ShapeDtypeStruct(block.shape, jnp.bfloat16),
            in_specs=[VMEM] * (1 + len(others)), out_specs=VMEM, compiler_params=params,
        )(block, *others)

    def kept(block):
        return pl.pallas_call(
            keep_kernel,
            out_shape=jax.ShapeDtypeStruct(block.shape, jnp.float32),
            in_specs=[VMEM] * 2, out_specs=VMEM, compiler_params=params,
        )(keep.reshape(1, w_dev), block)

    def pairs(base, partners, by_window, before=()):
        n = len(partners)
        total = n + (before[0].shape[0] if before else 0)
        return pl.pallas_call(
            functools.partial(pairs_kernel, n, n_win, n_freq, by_window),
            out_shape=[jax.ShapeDtypeStruct((total, n_win, ch * ch, width), jnp.float32)] * n_freq,
            in_specs=[VMEM] * (3 + n + len(before)), out_specs=[VMEM] * n_freq,
            scratch_shapes=[
                pltpu.VMEM((2, 2 * n * ch * ch, f_dev), jnp.bfloat16),
                pltpu.VMEM((2, n * ch * ch, LAGS // 2), jnp.float32),
            ],
            compiler_params=params,
            cost_estimate=cost(ch, ch),
        )(base, *partners, twist, table, *before)

    def turns(parts, axis, size):
        received = [parts[0]]
        for turn in range(1, size):
            route = [(g, (g + turn) % size) for g in range(size)]
            received.append(lax.ppermute(parts[turn], axis, route))
        return received

    def split_windows(parts, kinds):
        n = parts[0].shape[0]
        return pl.pallas_call(
            functools.partial(add_kernel, n_freq),
            out_shape=[jax.ShapeDtypeStruct((n, ch * ch, width), kind) for kind in kinds],
            in_specs=[VMEM] * n_freq, out_specs=[VMEM] * n_win, compiler_params=params,
        )(*turns(parts, "freq", n_freq))

    white = whiten(copied, swap(power))
    below = from_behind(white, "chan", -1)
    above = lax.ppermute(white, "chan", [(c - 1, c) for c in range(1, n_chan - 1)])
    half_lags = 2 * np.arange(LAGS // 2) + 1
    coarse = phases(np.arange(0, n_bins, FINE), half_lags)
    fine = phases(F_LO + np.arange(FINE), half_lags)
    white, ends = lax.optimization_barrier((white, jnp.asarray(np.concatenate([coarse, fine], axis=1))))
    table = pl.pallas_call(
        table_kernel,
        out_shape=jax.ShapeDtypeStruct((4, f_dev, LAGS // 2), jnp.bfloat16),
        in_specs=[VMEM], out_specs=VMEM, compiler_params=params, cost_estimate=cost(ch, ch),
    )(ends)
    own = kept(white)
    far = [whiten(block, swap(half_power(block))) for block in far]
    first = pairs(own, [white], False)
    below, above, far, first = lax.optimization_barrier((below, above, far, first))
    remote = pairs(kept(above), [below] + far, True)
    remote, first = lax.optimization_barrier((remote, first))
    kinds = [jnp.float32] + [jnp.bfloat16] * (n_win - 1)
    near = turns(split_windows(pairs(own, [below], False, first), kinds), "win", n_win)
    remote = turns(remote, "freq", n_freq)
    shape = (remote[0].shape[0], ch * ch, width)
    n_ships = n_win // n_freq
    shipped = pl.pallas_call(
        functools.partial(group_kernel, n_freq),
        out_shape=[jax.ShapeDtypeStruct((n_freq,) + shape, jnp.bfloat16)] * n_ships,
        in_specs=[VMEM] * n_freq, out_specs=[VMEM] * n_ships, compiler_params=params,
    )(*remote)
    arrived = []
    for ship, block in enumerate(shipped):
        route = [
            ((c * n_win + w) * n_freq + f, ((c - 1) * n_win + (w + ship * n_freq + f) % n_win) * n_freq + f)
            for c in range(1, n_chan - 1) for w in range(n_win) for f in range(n_freq)
        ]
        arrived.append(lax.ppermute(block, ("chan", "win", "freq"), route))
    arrived = pl.pallas_call(
        functools.partial(ungroup_kernel, n_ships),
        out_shape=[jax.ShapeDtypeStruct(shape, jnp.float32)] * n_freq,
        in_specs=[VMEM] * n_ships, out_specs=[VMEM] * n_freq, compiler_params=params,
    )(*arrived)
    arrived = turns(arrived, "freq", n_freq)
    scale = 1.0 / math.sqrt(w_dev * n_win * n_bins)
    factors = jnp.repeat(pair_mask.T.astype(jnp.float32) * scale, ch, axis=1)[..., None]
    return pl.pallas_call(
        functools.partial(combine_kernel, n_win, n_freq),
        out_shape=jax.ShapeDtypeStruct((ch, reach + 1, ch, width), jnp.float32),
        in_specs=[VMEM] * (1 + n_win + n_freq), out_specs=VMEM, compiler_params=params,
    )(factors, *near, *arrived)


def solution(mesh):
    in_specs = (
        P("win", None, ("fibre", "chan"), "freq"),
        P(("fibre", "win")),
        P(("fibre", "chan"), None),
    )
    out_specs = P(("fibre", "chan"), None, None, ("win", "freq"))
    return jax.shard_map(local, mesh=mesh, in_specs=in_specs, out_specs=out_specs, check_vma=False)
```

```python
import functools
import math

import jax
import jax.numpy as jnp
import numpy as np
from jax import lax
from jax.experimental import pallas as pl
from jax.experimental.pallas import tpu as pltpu
from jax.sharding import PartitionSpec as P

LAGS = 1024
F_LO = 60
NSAMP = 15000
EPS = 1e-06
LANES = 128
SUBLANES = 8
FINE = 32
BLOCK = 256
VMEM_LIMIT = 16 * 1024 * 1024


def from_behind(block, axis, distance):
    devices = range(lax.axis_size(axis))
    route = [(i - distance, i) for i in devices if i - distance in devices]
    return lax.ppermute(block, axis, route)


def phases(bins, half_lags):
    turns = np.remainder(np.asarray(bins, np.int64)[:, None] * np.asarray(half_lags, np.int64)[None, :], 2 * NSAMP)
    angle = turns * (math.pi / NSAMP)
    return np.stack([np.cos(angle), np.sin(angle)]).astype(np.float32)


def split(value):
    high = value.astype(jnp.bfloat16)
    return high, (value - high.astype(jnp.float32)).astype(jnp.bfloat16)


def bin_power(x):
    x = x.astype(jnp.float32)
    return jnp.sum(x[0] * x[0] + x[1] * x[1], axis=-1, keepdims=True)


def power_kernel(x_ref, power_ref, copy_ref):
    for w in range(x_ref.shape[0]):
        x = x_ref[w]
        power_ref[w] = bin_power(x)
        copy_ref[w] = x


def partial_kernel(x_ref, power_ref):
    for w in range(x_ref.shape[0]):
        power_ref[w] = bin_power(x_ref[w])


def own_kernel(n_bins, x_ref, *refs):
    white_ref, power_ref = refs[-2:]
    for w in range(x_ref.shape[0]):
        power = bin_power(x_ref[w])
        for ref in refs[:-2]:
            power = power + ref[w]
        power_ref[w] = jnp.broadcast_to(power, power_ref.shape[1:])
    whiten_kernel(n_bins, False, x_ref, power_ref, white_ref)


def whiten_kernel(n_bins, add_own, x_ref, *refs):
    out_ref = refs[-1]
    for w in range(x_ref.shape[0]):
        power = bin_power(x_ref[w]) if add_own else None
        for ref in refs[:-1]:
            other = ref[w][:, 0:1]
            power = other if power is None else power + other
        scale = lax.rsqrt(power / n_bins + EPS)
        for part in range(2):
            out_ref[w, part] = (x_ref[w, part].astype(jnp.float32) * scale).astype(jnp.bfloat16)


def keep_kernel(keep_ref, white_ref, out_ref):
    for w in range(white_ref.shape[0]):
        out_ref[w] = white_ref[w].astype(jnp.float32) * keep_ref[:, w:w + 1].astype(jnp.float32)[None]


def table_kernel(base_ref, table_ref):
    f_dev, width = table_ref.shape[1:]
    coarse = base_ref.shape[1] - FINE
    start = lax.axis_index("freq") * (f_dev // FINE)
    for block in range(0, width, BLOCK):
        lags = slice(block, block + BLOCK)
        fine_cos = base_ref[0, coarse:, lags]
        fine_sin = base_ref[1, coarse:, lags]

        def body(step, carry):
            first = pl.multiple_of(start + step * SUBLANES, SUBLANES)
            coarse_cos = base_ref[0, pl.ds(first, SUBLANES), lags]
            coarse_sin = base_ref[1, pl.ds(first, SUBLANES), lags]
            for n in range(SUBLANES):
                cos_a, sin_a = coarse_cos[n:n + 1], coarse_sin[n:n + 1]
                rows = pl.ds(pl.multiple_of((step * SUBLANES + n) * FINE, FINE), FINE)
                table_ref[0, rows, lags], table_ref[1, rows, lags] = split(cos_a * fine_cos - sin_a * fine_sin)
                table_ref[2, rows, lags], table_ref[3, rows, lags] = split(cos_a * fine_sin + sin_a * fine_cos)
            return carry

        lax.fori_loop(0, f_dev // (FINE * SUBLANES), body, 0)


def cross_tile(base_ref, partner_ref, lanes):
    w_dev, _, ch, _ = base_ref.shape
    real = [None] * ch
    imag = [None] * ch
    for w in range(w_dev):
        partner_re = partner_ref[w, 0, :, lanes].astype(jnp.float32)
        partner_im = partner_ref[w, 1, :, lanes].astype(jnp.float32)
        for i in range(ch):
            base_re = base_ref[w, 0, i:i + 1, lanes]
            base_im = base_ref[w, 1, i:i + 1, lanes]
            re = base_re * partner_re + base_im * partner_im
            im = base_im * partner_re - base_re * partner_im
            real[i] = re if w == 0 else real[i] + re
            imag[i] = im if w == 0 else imag[i] + im
    return real, imag


def pairs_kernel(n_partners, n_win, n_freq, by_window, base_ref, *refs):
    partner_refs = refs[:n_partners]
    twist_ref, table_ref = refs[n_partners:n_partners + 2]
    out_refs = refs[-2 - n_freq:-2]
    rows_ref, sums_ref = refs[-2:]
    ch, f_dev = base_ref.shape[2:]
    pairs = ch * ch
    groups = n_win * n_freq
    width = out_refs[0].shape[-1]
    freq, win = lax.axis_index("freq"), lax.axis_index("win")
    dot = functools.partial(jnp.dot, preferred_element_type=jnp.float32)
    count = n_partners * pairs

    def body(tile, carry):
        lanes = pl.ds(pl.multiple_of(tile * LANES, LANES), LANES)
        cos = twist_ref[freq, 0:1, lanes]
        sin = twist_ref[freq, 1:2, lanes]
        for k, partner_ref in enumerate(partner_refs):
            real, imag = cross_tile(base_ref, partner_ref, lanes)
            for i in range(0, ch, 2):
                rows = k * pairs + i * ch
                re = jnp.concatenate(real[i:i + 2], axis=0)
                im = jnp.concatenate(imag[i:i + 2], axis=0)
                for part, value in enumerate((re * cos + im * sin, im * cos - re * sin)):
                    high, low = split(value)
                    rows_ref[part, rows:rows + 2 * ch, lanes] = high
                    rows_ref[part, count + rows:count + rows + 2 * ch, lanes] = low
        return carry

    lax.fori_loop(0, f_dev // LANES, body, 0)
    for part in range(2):
        both = dot(rows_ref[part], table_ref[2 * part])
        sums_ref[part] = both[:count] + both[count:] + dot(rows_ref[part, :count], table_ref[2 * part + 1])
    for turn_freq, out_ref in enumerate(out_refs):
        core = (freq + turn_freq) % n_freq
        for turn_win in range(n_win):
            if by_window:
                away = turn_win // n_freq * n_freq + core
                owner = (win + away) % n_win * n_freq + (core + turn_win) % n_freq
            else:
                owner = (win + turn_win) % n_win * n_freq + core
            upper = owner >= groups // 2
            block = jnp.where(upper, owner - groups // 2, groups // 2 - 1 - owner)
            sign = jnp.where(upper, -1.0, 1.0)
            lags = pl.ds(pl.multiple_of(block * width, LANES), width)
            for k in range(n_partners):
                rows = slice(k * pairs, (k + 1) * pairs)
                out_ref[k, turn_win] = sums_ref[0, rows, lags] + sign * sums_ref[1, rows, lags]


def add_kernel(n_parts, *refs):
    for turn, out_ref in enumerate(refs[n_parts:]):
        total = refs[0][:, turn]
        for ref in refs[1:n_parts]:
            total = total + ref[:, turn]
        out_ref[...] = total.astype(out_ref.dtype)


def group_kernel(n_parts, *refs):
    out_refs = refs[n_parts:]
    per_ship = refs[0].shape[1] // len(out_refs)
    for ship, out_ref in enumerate(out_refs):
        for turn in range(per_ship):
            total = refs[0][:, ship * per_ship + turn]
            for ref in refs[1:n_parts]:
                total = total + ref[:, ship * per_ship + turn]
            out_ref[turn] = total.astype(out_ref.dtype)


def ungroup_kernel(n_ships, *refs):
    for turn, out_ref in enumerate(refs[n_ships:]):
        total = refs[0][turn].astype(jnp.float32)
        for ref in refs[1:n_ships]:
            total = total + ref[turn].astype(jnp.float32)
        out_ref[...] = total


def reverse_lanes(value):
    backward = LANES - 1 - lax.broadcasted_iota(jnp.int32, (value.shape[0], LANES), 1)
    pieces = [
        jnp.take_along_axis(value[:, start:start + LANES], backward, axis=1, mode="promise_in_bounds")
        for start in range(0, value.shape[1], LANES)
    ]
    return jnp.concatenate(pieces[::-1], axis=1)


def combine_kernel(n_win, n_freq, factor_ref, *refs):
    out_ref = refs[-1]
    ch = out_ref.shape[0]
    lower = lax.axis_index("win") * n_freq + lax.axis_index("freq") < n_win * n_freq // 2
    k = 0
    for parts in (refs[:n_win], refs[n_win:-1]):
        for n in range(parts[0].shape[0]):
            total = parts[0][n].astype(jnp.float32)
            for ref in parts[1:]:
                total = total + ref[n].astype(jnp.float32)
            total = jnp.where(lower, reverse_lanes(total), total) * factor_ref[k]
            for i in range(ch):
                out_ref[i, k] = total[i * ch:(i + 1) * ch]
            k += 1


VMEM = pl.BlockSpec(memory_space=pltpu.VMEM)


def local(spectra, keep, pair_mask):
    w_dev, _, ch, f_dev = spectra.shape
    reach = pair_mask.shape[1] - 1
    n_chan, n_win, n_freq = (lax.axis_size(a) for a in ("chan", "win", "freq"))
    width = LAGS // (n_win * n_freq)
    n_bins = f_dev * n_freq
    params = pltpu.CompilerParams(vmem_limit_bytes=VMEM_LIMIT)


    def cost(flops, size):
        return pl.CostEstimate(flops=flops, bytes_accessed=size, transcendentals=0)

    below = from_behind(spectra, "chan", -1)
    far_routes = [[(c + away, c) for c in range(1, n_chan - away)] for away in range(2, reach)]
    far = [lax.ppermute(spectra, "chan", route) for route in far_routes]
    power, copied = pl.pallas_call(
        power_kernel,
        out_shape=[
            jax.ShapeDtypeStruct((w_dev, ch, 1), jnp.float32),
            jax.ShapeDtypeStruct(spectra.shape, spectra.dtype),
        ],
        in_specs=[VMEM], out_specs=[VMEM] * 2, compiler_params=params, cost_estimate=cost(ch, ch),
    )(spectra)
    twist = phases(F_LO + np.arange(n_bins), np.ones(1)).reshape(2, n_freq, f_dev)
    twist = jnp.asarray(np.moveaxis(twist, 0, 1))

    def swap(power):
        routes = [[(f, (f + turn) % n_freq) for f in range(n_freq)] for turn in range(1, n_freq)]
        return [lax.ppermute(power, "freq", route) for route in routes]

    def half_power(block):
        return pl.pallas_call(
            partial_kernel,
            out_shape=jax.ShapeDtypeStruct(power.shape, jnp.float32),
            in_specs=[VMEM], out_specs=VMEM, compiler_params=params, cost_estimate=cost(ch, ch),
        )(block)

    def whiten(block, others, add_own):
        return pl.pallas_call(
            functools.partial(whiten_kernel, n_bins, add_own),
            out_shape=jax.ShapeDtypeStruct(block.shape, jnp.bfloat16),
            in_specs=[VMEM] * (1 + len(others)), out_specs=VMEM, compiler_params=params,
        )(block, *others)

    def kept(block):
        return pl.pallas_call(
            keep_kernel,
            out_shape=jax.ShapeDtypeStruct(block.shape, jnp.float32),
            in_specs=[VMEM] * 2, out_specs=VMEM, compiler_params=params,
        )(keep.reshape(1, w_dev), block)

    def pairs(base, partners, by_window):
        n = len(partners)
        return pl.pallas_call(
            functools.partial(pairs_kernel, n, n_win, n_freq, by_window),
            out_shape=[jax.ShapeDtypeStruct((n, n_win, ch * ch, width), jnp.float32)] * n_freq,
            in_specs=[VMEM] * (3 + n), out_specs=[VMEM] * n_freq,
            scratch_shapes=[
                pltpu.VMEM((2, 2 * n * ch * ch, f_dev), jnp.bfloat16),
                pltpu.VMEM((2, n * ch * ch, LAGS // 2), jnp.float32),
            ],
            compiler_params=params,
            cost_estimate=cost(ch, ch),
        )(base, *partners, twist, table)

    def turns(parts, axis, size):
        received = [parts[0]]
        for turn in range(1, size):
            route = [(g, (g + turn) % size) for g in range(size)]
            received.append(lax.ppermute(parts[turn], axis, route))
        return received

    def split_windows(parts, kinds):
        n = parts[0].shape[0]
        return pl.pallas_call(
            functools.partial(add_kernel, n_freq),
            out_shape=[jax.ShapeDtypeStruct((n, ch * ch, width), kind) for kind in kinds],
            in_specs=[VMEM] * n_freq, out_specs=[VMEM] * n_win, compiler_params=params,
        )(*turns(parts, "freq", n_freq))

    others = swap(power)
    white, whole_power = pl.pallas_call(
        functools.partial(own_kernel, n_bins),
        out_shape=[
            jax.ShapeDtypeStruct(spectra.shape, jnp.bfloat16),
            jax.ShapeDtypeStruct((w_dev, ch, LANES), jnp.float32),
        ],
        in_specs=[VMEM] * (1 + len(others)), out_specs=[VMEM] * 2, compiler_params=params,
    )(copied, *others)
    far_powers = [lax.ppermute(whole_power, "chan", route) for route in far_routes]
    above = lax.ppermute(white, "chan", [(c - 1, c) for c in range(1, n_chan - 1)])
    half_lags = 2 * np.arange(LAGS // 2) + 1
    coarse = phases(np.arange(0, n_bins, FINE), half_lags)
    fine = phases(F_LO + np.arange(FINE), half_lags)
    white, ends = lax.optimization_barrier((white, jnp.asarray(np.concatenate([coarse, fine], axis=1))))
    table = pl.pallas_call(
        table_kernel,
        out_shape=jax.ShapeDtypeStruct((4, f_dev, LAGS // 2), jnp.bfloat16),
        in_specs=[VMEM], out_specs=VMEM, compiler_params=params, cost_estimate=cost(ch, ch),
    )(ends)
    own = kept(white)
    below = whiten(below, swap(half_power(below)), True)
    parts = pairs(own, [white, below], False)
    far, far_powers, parts = lax.optimization_barrier((far, far_powers, parts))
    far = [whiten(block, [power], False) for block, power in zip(far, far_powers)]
    above, far = lax.optimization_barrier((above, far))
    kinds = [jnp.float32] + [jnp.bfloat16] * (n_win - 1)
    near = turns(split_windows(parts, kinds), "win", n_win)
    remote = turns(pairs(kept(above), [below] + far, True), "freq", n_freq)
    shape = (remote[0].shape[0], ch * ch, width)
    n_ships = n_win // n_freq
    shipped = pl.pallas_call(
        functools.partial(group_kernel, n_freq),
        out_shape=[jax.ShapeDtypeStruct((n_freq,) + shape, jnp.bfloat16)] * n_ships,
        in_specs=[VMEM] * n_freq, out_specs=[VMEM] * n_ships, compiler_params=params,
    )(*remote)
    arrived = []
    for ship, block in enumerate(shipped):
        route = [
            ((c * n_win + w) * n_freq + f, ((c - 1) * n_win + (w + ship * n_freq + f) % n_win) * n_freq + f)
            for c in range(1, n_chan - 1) for w in range(n_win) for f in range(n_freq)
        ]
        arrived.append(lax.ppermute(block, ("chan", "win", "freq"), route))
    arrived = pl.pallas_call(
        functools.partial(ungroup_kernel, n_ships),
        out_shape=[jax.ShapeDtypeStruct(shape, jnp.float32)] * n_freq,
        in_specs=[VMEM] * n_ships, out_specs=[VMEM] * n_freq, compiler_params=params,
    )(*arrived)
    arrived = turns(arrived, "freq", n_freq)
    scale = 1.0 / math.sqrt(w_dev * n_win * n_bins)
    factors = jnp.repeat(pair_mask.T.astype(jnp.float32) * scale, ch, axis=1)[..., None]
    return pl.pallas_call(
        functools.partial(combine_kernel, n_win, n_freq),
        out_shape=jax.ShapeDtypeStruct((ch, reach + 1, ch, width), jnp.float32),
        in_specs=[VMEM] * (1 + n_win + n_freq), out_specs=VMEM, compiler_params=params,
    )(factors, *near, *arrived)


def solution(mesh):
    in_specs = (
        P("win", None, ("fibre", "chan"), "freq"),
        P(("fibre", "win")),
        P(("fibre", "chan"), None),
    )
    out_specs = P(("fibre", "chan"), None, None, ("win", "freq"))
    return jax.shard_map(local, mesh=mesh, in_specs=in_specs, out_specs=out_specs, check_vma=False)
```

```python
import functools
import math

import jax
import jax.numpy as jnp
import numpy as np
from jax import lax
from jax.experimental import pallas as pl
from jax.experimental.pallas import tpu as pltpu
from jax.sharding import PartitionSpec as P

LAGS = 1024
F_LO = 60
NSAMP = 15000
EPS = 1e-06
LANES = 128
SUBLANES = 8
FINE = 32
BLOCK = 256
VMEM_LIMIT = 16 * 1024 * 1024


def from_behind(block, axis, distance):
    devices = range(lax.axis_size(axis))
    route = [(i - distance, i) for i in devices if i - distance in devices]
    return lax.ppermute(block, axis, route)


def phases(bins, half_lags):
    turns = np.remainder(np.asarray(bins, np.int64)[:, None] * np.asarray(half_lags, np.int64)[None, :], 2 * NSAMP)
    angle = turns * (math.pi / NSAMP)
    return np.stack([np.cos(angle), np.sin(angle)]).astype(np.float32)


def split(value):
    high = value.astype(jnp.bfloat16)
    return high, (value - high.astype(jnp.float32)).astype(jnp.bfloat16)


def bin_power(x):
    x = x.astype(jnp.float32)
    return jnp.sum(x[0] * x[0] + x[1] * x[1], axis=-1, keepdims=True)


def power_kernel(x_ref, power_ref, copy_ref):
    for w in range(x_ref.shape[0]):
        x = x_ref[w]
        power_ref[w] = bin_power(x)
        copy_ref[w] = x


def partial_kernel(x_ref, power_ref):
    for w in range(x_ref.shape[0]):
        power_ref[w] = bin_power(x_ref[w])


def whiten_kernel(n_bins, x_ref, *refs):
    out_ref = refs[-1]
    for w in range(x_ref.shape[0]):
        power = bin_power(x_ref[w])
        for ref in refs[:-1]:
            power = power + ref[w]
        scale = lax.rsqrt(power / n_bins + EPS)
        for part in range(2):
            out_ref[w, part] = (x_ref[w, part].astype(jnp.float32) * scale).astype(jnp.bfloat16)


def keep_kernel(keep_ref, white_ref, out_ref):
    for w in range(white_ref.shape[0]):
        out_ref[w] = white_ref[w].astype(jnp.float32) * keep_ref[:, w:w + 1].astype(jnp.float32)[None]


def table_kernel(base_ref, table_ref):
    f_dev, width = table_ref.shape[1:]
    coarse = base_ref.shape[1] - FINE
    start = lax.axis_index("freq") * (f_dev // FINE)
    for block in range(0, width, BLOCK):
        lags = slice(block, block + BLOCK)
        fine_cos = base_ref[0, coarse:, lags]
        fine_sin = base_ref[1, coarse:, lags]

        def body(step, carry):
            first = pl.multiple_of(start + step * SUBLANES, SUBLANES)
            coarse_cos = base_ref[0, pl.ds(first, SUBLANES), lags]
            coarse_sin = base_ref[1, pl.ds(first, SUBLANES), lags]
            for n in range(SUBLANES):
                cos_a, sin_a = coarse_cos[n:n + 1], coarse_sin[n:n + 1]
                rows = pl.ds(pl.multiple_of((step * SUBLANES + n) * FINE, FINE), FINE)
                table_ref[0, rows, lags], table_ref[1, rows, lags] = split(cos_a * fine_cos - sin_a * fine_sin)
                table_ref[2, rows, lags], table_ref[3, rows, lags] = split(cos_a * fine_sin + sin_a * fine_cos)
            return carry

        lax.fori_loop(0, f_dev // (FINE * SUBLANES), body, 0)


def cross_tile(base_ref, partner_ref, lanes):
    w_dev, _, ch, _ = base_ref.shape
    real = [None] * ch
    imag = [None] * ch
    for w in range(w_dev):
        partner_re = partner_ref[w, 0, :, lanes].astype(jnp.float32)
        partner_im = partner_ref[w, 1, :, lanes].astype(jnp.float32)
        for i in range(ch):
            base_re = base_ref[w, 0, i:i + 1, lanes]
            base_im = base_ref[w, 1, i:i + 1, lanes]
            re = base_re * partner_re + base_im * partner_im
            im = base_im * partner_re - base_re * partner_im
            real[i] = re if w == 0 else real[i] + re
            imag[i] = im if w == 0 else imag[i] + im
    return real, imag


def pairs_kernel(n_partners, n_win, n_freq, by_window, base_ref, *refs):
    partner_refs = refs[:n_partners]
    twist_ref, table_ref = refs[n_partners:n_partners + 2]
    out_refs = refs[-2 - n_freq:-2]
    rows_ref, sums_ref = refs[-2:]
    ch, f_dev = base_ref.shape[2:]
    pairs = ch * ch
    groups = n_win * n_freq
    width = out_refs[0].shape[-1]
    freq, win = lax.axis_index("freq"), lax.axis_index("win")
    dot = functools.partial(jnp.dot, preferred_element_type=jnp.float32)
    count = n_partners * pairs

    def body(tile, carry):
        lanes = pl.ds(pl.multiple_of(tile * LANES, LANES), LANES)
        cos = twist_ref[freq, 0:1, lanes]
        sin = twist_ref[freq, 1:2, lanes]
        for k, partner_ref in enumerate(partner_refs):
            real, imag = cross_tile(base_ref, partner_ref, lanes)
            for i in range(0, ch, 2):
                rows = k * pairs + i * ch
                re = jnp.concatenate(real[i:i + 2], axis=0)
                im = jnp.concatenate(imag[i:i + 2], axis=0)
                for part, value in enumerate((re * cos + im * sin, im * cos - re * sin)):
                    high, low = split(value)
                    rows_ref[part, rows:rows + 2 * ch, lanes] = high
                    rows_ref[part, count + rows:count + rows + 2 * ch, lanes] = low
        return carry

    lax.fori_loop(0, f_dev // LANES, body, 0)

    def transform(part, carry):
        both = dot(rows_ref[part], table_ref[2 * part])
        sums_ref[part] = both[:count] + both[count:] + dot(rows_ref[part, :count], table_ref[2 * part + 1])
        return carry

    lax.fori_loop(0, 2, transform, 0)
    for turn_freq, out_ref in enumerate(out_refs):
        core = (freq + turn_freq) % n_freq
        for turn_win in range(n_win):
            if by_window:
                away = turn_win // n_freq * n_freq + core
                owner = (win + away) % n_win * n_freq + (core + turn_win) % n_freq
            else:
                owner = (win + turn_win) % n_win * n_freq + core
            upper = owner >= groups // 2
            block = jnp.where(upper, owner - groups // 2, groups // 2 - 1 - owner)
            sign = jnp.where(upper, -1.0, 1.0)
            lags = pl.ds(pl.multiple_of(block * width, LANES), width)
            for k in range(n_partners):
                rows = slice(k * pairs, (k + 1) * pairs)
                out_ref[k, turn_win] = sums_ref[0, rows, lags] + sign * sums_ref[1, rows, lags]


def add_kernel(n_parts, *refs):
    for turn, out_ref in enumerate(refs[n_parts:]):
        total = refs[0][:, turn]
        for ref in refs[1:n_parts]:
            total = total + ref[:, turn]
        out_ref[...] = total.astype(out_ref.dtype)


def group_kernel(n_parts, *refs):
    out_refs = refs[n_parts:]
    per_ship = refs[0].shape[1] // len(out_refs)
    for ship, out_ref in enumerate(out_refs):
        for turn in range(per_ship):
            total = refs[0][:, ship * per_ship + turn]
            for ref in refs[1:n_parts]:
                total = total + ref[:, ship * per_ship + turn]
            out_ref[turn] = total.astype(out_ref.dtype)


def ungroup_kernel(n_ships, *refs):
    for turn, out_ref in enumerate(refs[n_ships:]):
        total = refs[0][turn].astype(jnp.float32)
        for ref in refs[1:n_ships]:
            total = total + ref[turn].astype(jnp.float32)
        out_ref[...] = total


def reverse_lanes(value):
    backward = LANES - 1 - lax.broadcasted_iota(jnp.int32, (value.shape[0], LANES), 1)
    pieces = [
        jnp.take_along_axis(value[:, start:start + LANES], backward, axis=1, mode="promise_in_bounds")
        for start in range(0, value.shape[1], LANES)
    ]
    return jnp.concatenate(pieces[::-1], axis=1)


def combine_kernel(n_win, n_freq, factor_ref, *refs):
    out_ref = refs[-1]
    ch = out_ref.shape[0]
    lower = lax.axis_index("win") * n_freq + lax.axis_index("freq") < n_win * n_freq // 2
    k = 0
    for parts in (refs[:n_win], refs[n_win:-1]):
        for n in range(parts[0].shape[0]):
            total = parts[0][n].astype(jnp.float32)
            for ref in parts[1:]:
                total = total + ref[n].astype(jnp.float32)
            total = jnp.where(lower, reverse_lanes(total), total) * factor_ref[k]
            for i in range(ch):
                out_ref[i, k] = total[i * ch:(i + 1) * ch]
            k += 1


VMEM = pl.BlockSpec(memory_space=pltpu.VMEM)


def local(spectra, keep, pair_mask):
    w_dev, _, ch, f_dev = spectra.shape
    reach = pair_mask.shape[1] - 1
    n_chan, n_win, n_freq = (lax.axis_size(a) for a in ("chan", "win", "freq"))
    width = LAGS // (n_win * n_freq)
    n_bins = f_dev * n_freq
    params = pltpu.CompilerParams(vmem_limit_bytes=VMEM_LIMIT)


    def cost(flops, size):
        return pl.CostEstimate(flops=flops, bytes_accessed=size, transcendentals=0)

    below = from_behind(spectra, "chan", -1)
    far_routes = [[(c + away, c) for c in range(1, n_chan - away)] for away in range(2, reach)]
    power, copied = pl.pallas_call(
        power_kernel,
        out_shape=[
            jax.ShapeDtypeStruct((w_dev, ch, 1), jnp.float32),
            jax.ShapeDtypeStruct(spectra.shape, spectra.dtype),
        ],
        in_specs=[VMEM], out_specs=[VMEM] * 2, compiler_params=params, cost_estimate=cost(ch, ch),
    )(spectra)
    twist = phases(F_LO + np.arange(n_bins), np.ones(1)).reshape(2, n_freq, f_dev)
    twist = jnp.asarray(np.moveaxis(twist, 0, 1))

    def swap(power):
        routes = [[(f, (f + turn) % n_freq) for f in range(n_freq)] for turn in range(1, n_freq)]
        return [lax.ppermute(power, "freq", route) for route in routes]

    def half_power(block):
        return pl.pallas_call(
            partial_kernel,
            out_shape=jax.ShapeDtypeStruct(power.shape, jnp.float32),
            in_specs=[VMEM], out_specs=VMEM, compiler_params=params, cost_estimate=cost(ch, ch),
        )(block)

    def whiten(block, others):
        return pl.pallas_call(
            functools.partial(whiten_kernel, n_bins),
            out_shape=jax.ShapeDtypeStruct(block.shape, jnp.bfloat16),
            in_specs=[VMEM] * (1 + len(others)), out_specs=VMEM, compiler_params=params,
        )(block, *others)

    def kept(block):
        return pl.pallas_call(
            keep_kernel,
            out_shape=jax.ShapeDtypeStruct(block.shape, jnp.float32),
            in_specs=[VMEM] * 2, out_specs=VMEM, compiler_params=params,
        )(keep.reshape(1, w_dev), block)

    def pairs(base, partners, by_window):
        n = len(partners)
        return pl.pallas_call(
            functools.partial(pairs_kernel, n, n_win, n_freq, by_window),
            out_shape=[jax.ShapeDtypeStruct((n, n_win, ch * ch, width), jnp.float32)] * n_freq,
            in_specs=[VMEM] * (3 + n), out_specs=[VMEM] * n_freq,
            scratch_shapes=[
                pltpu.VMEM((2, 2 * n * ch * ch, f_dev), jnp.bfloat16),
                pltpu.VMEM((2, n * ch * ch, LAGS // 2), jnp.float32),
            ],
            compiler_params=params,
            cost_estimate=cost(ch, ch),
        )(base, *partners, twist, table)

    def turns(parts, axis, size):
        received = [parts[0]]
        for turn in range(1, size):
            route = [(g, (g + turn) % size) for g in range(size)]
            received.append(lax.ppermute(parts[turn], axis, route))
        return received

    def split_windows(parts, kinds):
        n = parts[0].shape[0]
        return pl.pallas_call(
            functools.partial(add_kernel, n_freq),
            out_shape=[jax.ShapeDtypeStruct((n, ch * ch, width), kind) for kind in kinds],
            in_specs=[VMEM] * n_freq, out_specs=[VMEM] * n_win, compiler_params=params,
        )(*turns(parts, "freq", n_freq))

    white = whiten(copied, swap(power))
    far = [lax.ppermute(white, "chan", route) for route in far_routes]
    above = lax.ppermute(white, "chan", [(c - 1, c) for c in range(1, n_chan - 1)])
    half_lags = 2 * np.arange(LAGS // 2) + 1
    coarse = phases(np.arange(0, n_bins, FINE), half_lags)
    fine = phases(F_LO + np.arange(FINE), half_lags)
    white, ends = lax.optimization_barrier((white, jnp.asarray(np.concatenate([coarse, fine], axis=1))))
    table = pl.pallas_call(
        table_kernel,
        out_shape=jax.ShapeDtypeStruct((4, f_dev, LAGS // 2), jnp.bfloat16),
        in_specs=[VMEM], out_specs=VMEM, compiler_params=params, cost_estimate=cost(ch, ch),
    )(ends)
    own = kept(white)
    below = whiten(below, swap(half_power(below)))
    parts = pairs(own, [white, below], False)
    far, parts = lax.optimization_barrier((far, parts))
    above, far = lax.optimization_barrier((above, far))
    kinds = [jnp.float32] + [jnp.bfloat16] * (n_win - 1)
    near = turns(split_windows(parts, kinds), "win", n_win)
    remote = turns(pairs(kept(above), [below] + far, True), "freq", n_freq)
    shape = (remote[0].shape[0], ch * ch, width)
    n_ships = n_win // n_freq
    shipped = pl.pallas_call(
        functools.partial(group_kernel, n_freq),
        out_shape=[jax.ShapeDtypeStruct((n_freq,) + shape, jnp.bfloat16)] * n_ships,
        in_specs=[VMEM] * n_freq, out_specs=[VMEM] * n_ships, compiler_params=params,
    )(*remote)
    arrived = []
    for ship, block in enumerate(shipped):
        route = [
            ((c * n_win + w) * n_freq + f, ((c - 1) * n_win + (w + ship * n_freq + f) % n_win) * n_freq + f)
            for c in range(1, n_chan - 1) for w in range(n_win) for f in range(n_freq)
        ]
        arrived.append(lax.ppermute(block, ("chan", "win", "freq"), route))
    arrived = pl.pallas_call(
        functools.partial(ungroup_kernel, n_ships),
        out_shape=[jax.ShapeDtypeStruct(shape, jnp.float32)] * n_freq,
        in_specs=[VMEM] * n_ships, out_specs=[VMEM] * n_freq, compiler_params=params,
    )(*arrived)
    arrived = turns(arrived, "freq", n_freq)
    scale = 1.0 / math.sqrt(w_dev * n_win * n_bins)
    factors = jnp.repeat(pair_mask.T.astype(jnp.float32) * scale, ch, axis=1)[..., None]
    return pl.pallas_call(
        functools.partial(combine_kernel, n_win, n_freq),
        out_shape=jax.ShapeDtypeStruct((ch, reach + 1, ch, width), jnp.float32),
        in_specs=[VMEM] * (1 + n_win + n_freq), out_specs=VMEM, compiler_params=params,
    )(factors, *near, *arrived)


def solution(mesh):
    in_specs = (
        P("win", None, ("fibre", "chan"), "freq"),
        P(("fibre", "win")),
        P(("fibre", "chan"), None),
    )
    out_specs = P(("fibre", "chan"), None, None, ("win", "freq"))
    return jax.shard_map(local, mesh=mesh, in_specs=in_specs, out_specs=out_specs, check_vma=False)
```

```python
import functools
import math

import jax
import jax.numpy as jnp
import numpy as np
from jax import lax
from jax.experimental import pallas as pl
from jax.experimental.pallas import tpu as pltpu
from jax.sharding import PartitionSpec as P

LAGS = 1024
F_LO = 60
NSAMP = 15000
EPS = 1e-06
LANES = 128
SUBLANES = 8
FINE = 32
BLOCK = 256
VMEM_LIMIT = 16 * 1024 * 1024


def from_behind(block, axis, distance):
    devices = range(lax.axis_size(axis))
    route = [(i - distance, i) for i in devices if i - distance in devices]
    return lax.ppermute(block, axis, route)


def phases(bins, half_lags):
    turns = np.remainder(np.asarray(bins, np.int64)[:, None] * np.asarray(half_lags, np.int64)[None, :], 2 * NSAMP)
    angle = turns * (math.pi / NSAMP)
    return np.stack([np.cos(angle), np.sin(angle)]).astype(np.float32)


def split(value):
    high = value.astype(jnp.bfloat16)
    return high, (value - high.astype(jnp.float32)).astype(jnp.bfloat16)


def bin_power(x):
    x = x.astype(jnp.float32)
    return jnp.sum(x[0] * x[0] + x[1] * x[1], axis=-1, keepdims=True)


def power_kernel(x_ref, power_ref, copy_ref):
    for w in range(x_ref.shape[0]):
        x = x_ref[w]
        power_ref[w] = bin_power(x)
        copy_ref[w] = x


def partial_kernel(x_ref, power_ref):
    for w in range(x_ref.shape[0]):
        power_ref[w] = bin_power(x_ref[w])


def whiten_kernel(n_bins, x_ref, *refs):
    out_ref = refs[-1]
    for w in range(x_ref.shape[0]):
        power = bin_power(x_ref[w])
        for ref in refs[:-1]:
            power = power + ref[w]
        scale = lax.rsqrt(power / n_bins + EPS)
        for part in range(2):
            out_ref[w, part] = (x_ref[w, part].astype(jnp.float32) * scale).astype(jnp.bfloat16)


def keep_kernel(keep_ref, white_ref, out_ref):
    for w in range(white_ref.shape[0]):
        out_ref[w] = white_ref[w].astype(jnp.float32) * keep_ref[:, w:w + 1].astype(jnp.float32)[None]


def table_kernel(base_ref, table_ref):
    f_dev, width = table_ref.shape[1:]
    coarse = base_ref.shape[1] - FINE
    start = lax.axis_index("freq") * (f_dev // FINE)
    for block in range(0, width, BLOCK):
        lags = slice(block, block + BLOCK)
        fine_cos = base_ref[0, coarse:, lags]
        fine_sin = base_ref[1, coarse:, lags]

        def body(step, carry):
            first = pl.multiple_of(start + step * SUBLANES, SUBLANES)
            coarse_cos = base_ref[0, pl.ds(first, SUBLANES), lags]
            coarse_sin = base_ref[1, pl.ds(first, SUBLANES), lags]
            for n in range(SUBLANES):
                cos_a, sin_a = coarse_cos[n:n + 1], coarse_sin[n:n + 1]
                rows = pl.ds(pl.multiple_of((step * SUBLANES + n) * FINE, FINE), FINE)
                table_ref[0, rows, lags], table_ref[1, rows, lags] = split(cos_a * fine_cos - sin_a * fine_sin)
                table_ref[2, rows, lags], table_ref[3, rows, lags] = split(cos_a * fine_sin + sin_a * fine_cos)
            return carry

        lax.fori_loop(0, f_dev // (FINE * SUBLANES), body, 0)


def cross_tile(base_ref, partner_ref, lanes):
    w_dev, _, ch, _ = base_ref.shape
    real = [None] * ch
    imag = [None] * ch
    for w in range(w_dev):
        partner_re = partner_ref[w, 0, :, lanes].astype(jnp.float32)
        partner_im = partner_ref[w, 1, :, lanes].astype(jnp.float32)
        for i in range(ch):
            base_re = base_ref[w, 0, i:i + 1, lanes]
            base_im = base_ref[w, 1, i:i + 1, lanes]
            re = base_re * partner_re + base_im * partner_im
            im = base_im * partner_re - base_re * partner_im
            real[i] = re if w == 0 else real[i] + re
            imag[i] = im if w == 0 else imag[i] + im
    return real, imag


def pairs_kernel(n_partners, n_win, n_freq, by_window, base_ref, *refs):
    partner_refs = refs[:n_partners]
    twist_ref, table_ref = refs[n_partners:n_partners + 2]
    out_refs = refs[-2 - n_freq:-2]
    rows_ref, sums_ref = refs[-2:]
    ch, f_dev = base_ref.shape[2:]
    pairs = ch * ch
    groups = n_win * n_freq
    width = out_refs[0].shape[-1]
    freq, win = lax.axis_index("freq"), lax.axis_index("win")
    dot = functools.partial(jnp.dot, preferred_element_type=jnp.float32)
    count = n_partners * pairs

    def body(tile, carry):
        lanes = pl.ds(pl.multiple_of(tile * LANES, LANES), LANES)
        cos = twist_ref[freq, 0:1, lanes]
        sin = twist_ref[freq, 1:2, lanes]
        for k, partner_ref in enumerate(partner_refs):
            real, imag = cross_tile(base_ref, partner_ref, lanes)
            for i in range(0, ch, 2):
                rows = k * pairs + i * ch
                re = jnp.concatenate(real[i:i + 2], axis=0)
                im = jnp.concatenate(imag[i:i + 2], axis=0)
                for part, value in enumerate((re * cos + im * sin, im * cos - re * sin)):
                    high, low = split(value)
                    rows_ref[part, rows:rows + 2 * ch, lanes] = high
                    rows_ref[part, count + rows:count + rows + 2 * ch, lanes] = low
        return carry

    lax.fori_loop(0, f_dev // LANES, body, 0)

    def transform(step, carry):
        part = step % 2
        lags = pl.ds(pl.multiple_of(step // 2 * BLOCK, BLOCK), BLOCK)
        both = dot(rows_ref[part], table_ref[2 * part, :, lags])
        low = dot(rows_ref[part, :count], table_ref[2 * part + 1, :, lags])
        sums_ref[part, :, lags] = both[:count] + both[count:] + low
        return carry

    lax.fori_loop(0, 2 * (table_ref.shape[-1] // BLOCK), transform, 0)
    for turn_freq, out_ref in enumerate(out_refs):
        core = (freq + turn_freq) % n_freq
        for turn_win in range(n_win):
            if by_window:
                away = turn_win // n_freq * n_freq + core
                owner = (win + away) % n_win * n_freq + (core + turn_win) % n_freq
            else:
                owner = (win + turn_win) % n_win * n_freq + core
            upper = owner >= groups // 2
            block = jnp.where(upper, owner - groups // 2, groups // 2 - 1 - owner)
            sign = jnp.where(upper, -1.0, 1.0)
            lags = pl.ds(pl.multiple_of(block * width, LANES), width)
            for k in range(n_partners):
                rows = slice(k * pairs, (k + 1) * pairs)
                out_ref[k, turn_win] = sums_ref[0, rows, lags] + sign * sums_ref[1, rows, lags]


def add_kernel(n_parts, *refs):
    for turn, out_ref in enumerate(refs[n_parts:]):
        total = refs[0][:, turn]
        for ref in refs[1:n_parts]:
            total = total + ref[:, turn]
        out_ref[...] = total.astype(out_ref.dtype)


def group_kernel(n_parts, *refs):
    out_refs = refs[n_parts:]
    per_ship = refs[0].shape[1] // len(out_refs)
    for ship, out_ref in enumerate(out_refs):
        for turn in range(per_ship):
            total = refs[0][:, ship * per_ship + turn]
            for ref in refs[1:n_parts]:
                total = total + ref[:, ship * per_ship + turn]
            out_ref[turn] = total.astype(out_ref.dtype)


def ungroup_kernel(n_ships, *refs):
    for turn, out_ref in enumerate(refs[n_ships:]):
        total = refs[0][turn].astype(jnp.float32)
        for ref in refs[1:n_ships]:
            total = total + ref[turn].astype(jnp.float32)
        out_ref[...] = total


def reverse_lanes(value):
    backward = LANES - 1 - lax.broadcasted_iota(jnp.int32, (value.shape[0], LANES), 1)
    pieces = [
        jnp.take_along_axis(value[:, start:start + LANES], backward, axis=1, mode="promise_in_bounds")
        for start in range(0, value.shape[1], LANES)
    ]
    return jnp.concatenate(pieces[::-1], axis=1)


def combine_kernel(n_win, n_freq, factor_ref, *refs):
    out_ref = refs[-1]
    ch = out_ref.shape[0]
    lower = lax.axis_index("win") * n_freq + lax.axis_index("freq") < n_win * n_freq // 2
    k = 0
    for parts in (refs[:n_win], refs[n_win:-1]):
        for n in range(parts[0].shape[0]):
            total = parts[0][n].astype(jnp.float32)
            for ref in parts[1:]:
                total = total + ref[n].astype(jnp.float32)
            total = jnp.where(lower, reverse_lanes(total), total) * factor_ref[k]
            for i in range(ch):
                out_ref[i, k] = total[i * ch:(i + 1) * ch]
            k += 1


VMEM = pl.BlockSpec(memory_space=pltpu.VMEM)


def local(spectra, keep, pair_mask):
    w_dev, _, ch, f_dev = spectra.shape
    reach = pair_mask.shape[1] - 1
    n_chan, n_win, n_freq = (lax.axis_size(a) for a in ("chan", "win", "freq"))
    width = LAGS // (n_win * n_freq)
    n_bins = f_dev * n_freq
    params = pltpu.CompilerParams(vmem_limit_bytes=VMEM_LIMIT)


    def cost(flops, size):
        return pl.CostEstimate(flops=flops, bytes_accessed=size, transcendentals=0)

    below = from_behind(spectra, "chan", -1)
    far_routes = [[(c + away, c) for c in range(1, n_chan - away)] for away in range(2, reach)]
    power, copied = pl.pallas_call(
        power_kernel,
        out_shape=[
            jax.ShapeDtypeStruct((w_dev, ch, 1), jnp.float32),
            jax.ShapeDtypeStruct(spectra.shape, spectra.dtype),
        ],
        in_specs=[VMEM], out_specs=[VMEM] * 2, compiler_params=params, cost_estimate=cost(ch, ch),
    )(spectra)
    twist = phases(F_LO + np.arange(n_bins), np.ones(1)).reshape(2, n_freq, f_dev)
    twist = jnp.asarray(np.moveaxis(twist, 0, 1))

    def swap(power):
        routes = [[(f, (f + turn) % n_freq) for f in range(n_freq)] for turn in range(1, n_freq)]
        return [lax.ppermute(power, "freq", route) for route in routes]

    def half_power(block):
        return pl.pallas_call(
            partial_kernel,
            out_shape=jax.ShapeDtypeStruct(power.shape, jnp.float32),
            in_specs=[VMEM], out_specs=VMEM, compiler_params=params, cost_estimate=cost(ch, ch),
        )(block)

    def whiten(block, others):
        return pl.pallas_call(
            functools.partial(whiten_kernel, n_bins),
            out_shape=jax.ShapeDtypeStruct(block.shape, jnp.bfloat16),
            in_specs=[VMEM] * (1 + len(others)), out_specs=VMEM, compiler_params=params,
        )(block, *others)

    def kept(block):
        return pl.pallas_call(
            keep_kernel,
            out_shape=jax.ShapeDtypeStruct(block.shape, jnp.float32),
            in_specs=[VMEM] * 2, out_specs=VMEM, compiler_params=params,
        )(keep.reshape(1, w_dev), block)

    def pairs(base, partners, by_window):
        n = len(partners)
        return pl.pallas_call(
            functools.partial(pairs_kernel, n, n_win, n_freq, by_window),
            out_shape=[jax.ShapeDtypeStruct((n, n_win, ch * ch, width), jnp.float32)] * n_freq,
            in_specs=[VMEM] * (3 + n), out_specs=[VMEM] * n_freq,
            scratch_shapes=[
                pltpu.VMEM((2, 2 * n * ch * ch, f_dev), jnp.bfloat16),
                pltpu.VMEM((2, n * ch * ch, LAGS // 2), jnp.float32),
            ],
            compiler_params=params,
            cost_estimate=cost(ch, ch),
        )(base, *partners, twist, table)

    def turns(parts, axis, size):
        received = [parts[0]]
        for turn in range(1, size):
            route = [(g, (g + turn) % size) for g in range(size)]
            received.append(lax.ppermute(parts[turn], axis, route))
        return received

    def split_windows(parts, kinds):
        n = parts[0].shape[0]
        return pl.pallas_call(
            functools.partial(add_kernel, n_freq),
            out_shape=[jax.ShapeDtypeStruct((n, ch * ch, width), kind) for kind in kinds],
            in_specs=[VMEM] * n_freq, out_specs=[VMEM] * n_win, compiler_params=params,
        )(*turns(parts, "freq", n_freq))

    white = whiten(copied, swap(power))
    far = [lax.ppermute(white, "chan", route) for route in far_routes]
    above = lax.ppermute(white, "chan", [(c - 1, c) for c in range(1, n_chan - 1)])
    half_lags = 2 * np.arange(LAGS // 2) + 1
    coarse = phases(np.arange(0, n_bins, FINE), half_lags)
    fine = phases(F_LO + np.arange(FINE), half_lags)
    white, ends = lax.optimization_barrier((white, jnp.asarray(np.concatenate([coarse, fine], axis=1))))
    table = pl.pallas_call(
        table_kernel,
        out_shape=jax.ShapeDtypeStruct((4, f_dev, LAGS // 2), jnp.bfloat16),
        in_specs=[VMEM], out_specs=VMEM, compiler_params=params, cost_estimate=cost(ch, ch),
    )(ends)
    own = kept(white)
    below = whiten(below, swap(half_power(below)))
    parts = pairs(own, [white, below], False)
    far, parts = lax.optimization_barrier((far, parts))
    above, far = lax.optimization_barrier((above, far))
    kinds = [jnp.float32] + [jnp.bfloat16] * (n_win - 1)
    near = turns(split_windows(parts, kinds), "win", n_win)
    remote = turns(pairs(kept(above), [below] + far, True), "freq", n_freq)
    shape = (remote[0].shape[0], ch * ch, width)
    n_ships = n_win // n_freq
    shipped = pl.pallas_call(
        functools.partial(group_kernel, n_freq),
        out_shape=[jax.ShapeDtypeStruct((n_freq,) + shape, jnp.bfloat16)] * n_ships,
        in_specs=[VMEM] * n_freq, out_specs=[VMEM] * n_ships, compiler_params=params,
    )(*remote)
    arrived = []
    for ship, block in enumerate(shipped):
        route = [
            ((c * n_win + w) * n_freq + f, ((c - 1) * n_win + (w + ship * n_freq + f) % n_win) * n_freq + f)
            for c in range(1, n_chan - 1) for w in range(n_win) for f in range(n_freq)
        ]
        arrived.append(lax.ppermute(block, ("chan", "win", "freq"), route))
    arrived = pl.pallas_call(
        functools.partial(ungroup_kernel, n_ships),
        out_shape=[jax.ShapeDtypeStruct(shape, jnp.float32)] * n_freq,
        in_specs=[VMEM] * n_ships, out_specs=[VMEM] * n_freq, compiler_params=params,
    )(*arrived)
    arrived = turns(arrived, "freq", n_freq)
    scale = 1.0 / math.sqrt(w_dev * n_win * n_bins)
    factors = jnp.repeat(pair_mask.T.astype(jnp.float32) * scale, ch, axis=1)[..., None]
    return pl.pallas_call(
        functools.partial(combine_kernel, n_win, n_freq),
        out_shape=jax.ShapeDtypeStruct((ch, reach + 1, ch, width), jnp.float32),
        in_specs=[VMEM] * (1 + n_win + n_freq), out_specs=VMEM, compiler_params=params,
    )(factors, *near, *arrived)


def solution(mesh):
    in_specs = (
        P("win", None, ("fibre", "chan"), "freq"),
        P(("fibre", "win")),
        P(("fibre", "chan"), None),
    )
    out_specs = P(("fibre", "chan"), None, None, ("win", "freq"))
    return jax.shard_map(local, mesh=mesh, in_specs=in_specs, out_specs=out_specs, check_vma=False)
```

```python
import functools
import math

import jax
import jax.numpy as jnp
import numpy as np
from jax import lax
from jax.experimental import pallas as pl
from jax.experimental.pallas import tpu as pltpu
from jax.sharding import PartitionSpec as P

LAGS = 1024
F_LO = 60
NSAMP = 15000
EPS = 1e-06
LANES = 128
SUBLANES = 8
FINE = 32
BLOCK = 256
VMEM_LIMIT = 16 * 1024 * 1024


def from_behind(block, axis, distance):
    devices = range(lax.axis_size(axis))
    route = [(i - distance, i) for i in devices if i - distance in devices]
    return lax.ppermute(block, axis, route)


def phases(bins, half_lags):
    turns = np.remainder(np.asarray(bins, np.int64)[:, None] * np.asarray(half_lags, np.int64)[None, :], 2 * NSAMP)
    angle = turns * (math.pi / NSAMP)
    return np.stack([np.cos(angle), np.sin(angle)]).astype(np.float32)


def split(value):
    high = value.astype(jnp.bfloat16)
    return high, (value - high.astype(jnp.float32)).astype(jnp.bfloat16)


def bin_power(x):
    x = x.astype(jnp.float32)
    return jnp.sum(x[0] * x[0] + x[1] * x[1], axis=-1, keepdims=True)


def power_kernel(x_ref, power_ref, copy_ref):
    for w in range(x_ref.shape[0]):
        x = x_ref[w]
        power_ref[w] = bin_power(x)
        copy_ref[w] = x


def partial_kernel(x_ref, power_ref):
    for w in range(x_ref.shape[0]):
        power_ref[w] = bin_power(x_ref[w])


def whiten_kernel(n_bins, x_ref, *refs):
    out_ref = refs[-1]
    for w in range(x_ref.shape[0]):
        power = bin_power(x_ref[w])
        for ref in refs[:-1]:
            power = power + ref[w]
        scale = lax.rsqrt(power / n_bins + EPS)
        for part in range(2):
            out_ref[w, part] = (x_ref[w, part].astype(jnp.float32) * scale).astype(jnp.bfloat16)


def keep_kernel(keep_ref, white_ref, out_ref):
    for w in range(white_ref.shape[0]):
        value = white_ref[w].astype(jnp.float32) * keep_ref[:, w:w + 1].astype(jnp.float32)[None]
        out_ref[w, 0] = value[0]
        out_ref[w, 1] = value[1]
        out_ref[w, 2] = value[0] + value[1]


def table_kernel(base_ref, table_ref):
    f_dev, width = table_ref.shape[1:]
    coarse = base_ref.shape[1] - FINE
    start = lax.axis_index("freq") * (f_dev // FINE)
    for block in range(0, width, BLOCK):
        lags = slice(block, block + BLOCK)
        fine_cos = base_ref[0, coarse:, lags]
        fine_sin = base_ref[1, coarse:, lags]

        def body(step, carry):
            first = pl.multiple_of(start + step * SUBLANES, SUBLANES)
            coarse_cos = base_ref[0, pl.ds(first, SUBLANES), lags]
            coarse_sin = base_ref[1, pl.ds(first, SUBLANES), lags]
            for n in range(SUBLANES):
                cos_a, sin_a = coarse_cos[n:n + 1], coarse_sin[n:n + 1]
                rows = pl.ds(pl.multiple_of((step * SUBLANES + n) * FINE, FINE), FINE)
                table_ref[0, rows, lags], table_ref[1, rows, lags] = split(cos_a * fine_cos - sin_a * fine_sin)
                table_ref[2, rows, lags], table_ref[3, rows, lags] = split(cos_a * fine_sin + sin_a * fine_cos)
            return carry

        lax.fori_loop(0, f_dev // (FINE * SUBLANES), body, 0)


def cross_tile(base_ref, partner_ref, lanes):
    w_dev, _, ch, _ = base_ref.shape
    sums = [[None] * ch for _ in range(3)]
    for w in range(w_dev):
        partner_re = partner_ref[w, 0, :, lanes].astype(jnp.float32)
        partner_im = partner_ref[w, 1, :, lanes].astype(jnp.float32)
        factors = (partner_re + partner_im, partner_re - partner_im, partner_re)
        for i in range(ch):
            for n, factor in enumerate(factors):
                product = base_ref[w, n, i:i + 1, lanes] * factor
                sums[n][i] = product if w == 0 else sums[n][i] + product
    real = [both - im for im, both in zip(sums[1], sums[2])]
    imag = [both - re for re, both in zip(sums[0], sums[2])]
    return real, imag


def pairs_kernel(n_partners, n_win, n_freq, by_window, base_ref, *refs):
    partner_refs = refs[:n_partners]
    twist_ref, table_ref = refs[n_partners:n_partners + 2]
    out_refs = refs[-2 - n_freq:-2]
    rows_ref, sums_ref = refs[-2:]
    ch, f_dev = base_ref.shape[2:]
    pairs = ch * ch
    groups = n_win * n_freq
    width = out_refs[0].shape[-1]
    freq, win = lax.axis_index("freq"), lax.axis_index("win")
    dot = functools.partial(jnp.dot, preferred_element_type=jnp.float32)
    count = n_partners * pairs

    def body(tile, carry):
        lanes = pl.ds(pl.multiple_of(tile * LANES, LANES), LANES)
        cos = twist_ref[freq, 0:1, lanes]
        sin = twist_ref[freq, 1:2, lanes]
        for k, partner_ref in enumerate(partner_refs):
            real, imag = cross_tile(base_ref, partner_ref, lanes)
            for i in range(0, ch, 2):
                rows = k * pairs + i * ch
                re = jnp.concatenate(real[i:i + 2], axis=0)
                im = jnp.concatenate(imag[i:i + 2], axis=0)
                for part, value in enumerate((re * cos + im * sin, im * cos - re * sin)):
                    high, low = split(value)
                    rows_ref[part, rows:rows + 2 * ch, lanes] = high
                    rows_ref[part, count + rows:count + rows + 2 * ch, lanes] = low
        return carry

    lax.fori_loop(0, f_dev // LANES, body, 0)
    for part in range(2):
        both = dot(rows_ref[part], table_ref[2 * part])
        sums_ref[part] = both[:count] + both[count:] + dot(rows_ref[part, :count], table_ref[2 * part + 1])
    for turn_freq, out_ref in enumerate(out_refs):
        core = (freq + turn_freq) % n_freq
        for turn_win in range(n_win):
            if by_window:
                away = turn_win // n_freq * n_freq + core
                owner = (win + away) % n_win * n_freq + (core + turn_win) % n_freq
            else:
                owner = (win + turn_win) % n_win * n_freq + core
            upper = owner >= groups // 2
            block = jnp.where(upper, owner - groups // 2, groups // 2 - 1 - owner)
            sign = jnp.where(upper, -1.0, 1.0)
            lags = pl.ds(pl.multiple_of(block * width, LANES), width)
            for k in range(n_partners):
                rows = slice(k * pairs, (k + 1) * pairs)
                out_ref[k, turn_win] = sums_ref[0, rows, lags] + sign * sums_ref[1, rows, lags]


def add_kernel(n_parts, *refs):
    for turn, out_ref in enumerate(refs[n_parts:]):
        total = refs[0][:, turn]
        for ref in refs[1:n_parts]:
            total = total + ref[:, turn]
        out_ref[...] = total.astype(out_ref.dtype)


def group_kernel(n_parts, *refs):
    out_refs = refs[n_parts:]
    per_ship = refs[0].shape[1] // len(out_refs)
    for ship, out_ref in enumerate(out_refs):
        for turn in range(per_ship):
            total = refs[0][:, ship * per_ship + turn]
            for ref in refs[1:n_parts]:
                total = total + ref[:, ship * per_ship + turn]
            out_ref[turn] = total.astype(out_ref.dtype)


def ungroup_kernel(n_ships, *refs):
    for turn, out_ref in enumerate(refs[n_ships:]):
        total = refs[0][turn].astype(jnp.float32)
        for ref in refs[1:n_ships]:
            total = total + ref[turn].astype(jnp.float32)
        out_ref[...] = total.astype(out_ref.dtype)


def reverse_lanes(value):
    backward = LANES - 1 - lax.broadcasted_iota(jnp.int32, (value.shape[0], LANES), 1)
    pieces = [
        jnp.take_along_axis(value[:, start:start + LANES], backward, axis=1, mode="promise_in_bounds")
        for start in range(0, value.shape[1], LANES)
    ]
    return jnp.concatenate(pieces[::-1], axis=1)


def combine_kernel(n_win, n_freq, factor_ref, *refs):
    out_ref = refs[-1]
    ch = out_ref.shape[0]
    lower = lax.axis_index("win") * n_freq + lax.axis_index("freq") < n_win * n_freq // 2
    k = 0
    for parts in (refs[:n_win], refs[n_win:-1]):
        for n in range(parts[0].shape[0]):
            total = parts[0][n].astype(jnp.float32)
            for ref in parts[1:]:
                total = total + ref[n].astype(jnp.float32)
            total = jnp.where(lower, reverse_lanes(total), total) * factor_ref[k]
            for i in range(ch):
                out_ref[i, k] = total[i * ch:(i + 1) * ch]
            k += 1


VMEM = pl.BlockSpec(memory_space=pltpu.VMEM)


def local(spectra, keep, pair_mask):
    w_dev, _, ch, f_dev = spectra.shape
    reach = pair_mask.shape[1] - 1
    n_chan, n_win, n_freq = (lax.axis_size(a) for a in ("chan", "win", "freq"))
    width = LAGS // (n_win * n_freq)
    n_bins = f_dev * n_freq
    params = pltpu.CompilerParams(vmem_limit_bytes=VMEM_LIMIT)


    def cost(flops, size):
        return pl.CostEstimate(flops=flops, bytes_accessed=size, transcendentals=0)

    below = from_behind(spectra, "chan", -1)
    far_routes = [[(c + away, c) for c in range(1, n_chan - away)] for away in range(2, reach)]
    power, copied = pl.pallas_call(
        power_kernel,
        out_shape=[
            jax.ShapeDtypeStruct((w_dev, ch, 1), jnp.float32),
            jax.ShapeDtypeStruct(spectra.shape, spectra.dtype),
        ],
        in_specs=[VMEM], out_specs=[VMEM] * 2, compiler_params=params, cost_estimate=cost(ch, ch),
    )(spectra)
    twist = phases(F_LO + np.arange(n_bins), np.ones(1)).reshape(2, n_freq, f_dev)
    twist = jnp.asarray(np.moveaxis(twist, 0, 1))

    def swap(power):
        routes = [[(f, (f + turn) % n_freq) for f in range(n_freq)] for turn in range(1, n_freq)]
        return [lax.ppermute(power, "freq", route) for route in routes]

    def half_power(block):
        return pl.pallas_call(
            partial_kernel,
            out_shape=jax.ShapeDtypeStruct(power.shape, jnp.float32),
            in_specs=[VMEM], out_specs=VMEM, compiler_params=params, cost_estimate=cost(ch, ch),
        )(block)

    def whiten(block, others):
        return pl.pallas_call(
            functools.partial(whiten_kernel, n_bins),
            out_shape=jax.ShapeDtypeStruct(block.shape, jnp.bfloat16),
            in_specs=[VMEM] * (1 + len(others)), out_specs=VMEM, compiler_params=params,
        )(block, *others)

    def kept(block):
        return pl.pallas_call(
            keep_kernel,
            out_shape=jax.ShapeDtypeStruct((w_dev, 3) + block.shape[2:], jnp.float32),
            in_specs=[VMEM] * 2, out_specs=VMEM, compiler_params=params,
        )(keep.reshape(1, w_dev), block)

    def pairs(base, partners, by_window):
        n = len(partners)
        return pl.pallas_call(
            functools.partial(pairs_kernel, n, n_win, n_freq, by_window),
            out_shape=[jax.ShapeDtypeStruct((n, n_win, ch * ch, width), jnp.float32)] * n_freq,
            in_specs=[VMEM] * (3 + n), out_specs=[VMEM] * n_freq,
            scratch_shapes=[
                pltpu.VMEM((2, 2 * n * ch * ch, f_dev), jnp.bfloat16),
                pltpu.VMEM((2, n * ch * ch, LAGS // 2), jnp.float32),
            ],
            compiler_params=params,
            cost_estimate=cost(ch, ch),
        )(base, *partners, twist, table)

    def turns(parts, axis, size):
        received = [parts[0]]
        for turn in range(1, size):
            route = [(g, (g + turn) % size) for g in range(size)]
            received.append(lax.ppermute(parts[turn], axis, route))
        return received

    def split_windows(parts, kinds):
        n = parts[0].shape[0]
        return pl.pallas_call(
            functools.partial(add_kernel, n_freq),
            out_shape=[jax.ShapeDtypeStruct((n, ch * ch, width), kind) for kind in kinds],
            in_specs=[VMEM] * n_freq, out_specs=[VMEM] * n_win, compiler_params=params,
        )(*turns(parts, "freq", n_freq))

    white = whiten(copied, swap(power))
    far = [lax.ppermute(white, "chan", route) for route in far_routes]
    above = lax.ppermute(white, "chan", [(c - 1, c) for c in range(1, n_chan - 1)])
    half_lags = 2 * np.arange(LAGS // 2) + 1
    coarse = phases(np.arange(0, n_bins, FINE), half_lags)
    fine = phases(F_LO + np.arange(FINE), half_lags)
    white, ends = lax.optimization_barrier((white, jnp.asarray(np.concatenate([coarse, fine], axis=1))))
    table = pl.pallas_call(
        table_kernel,
        out_shape=jax.ShapeDtypeStruct((4, f_dev, LAGS // 2), jnp.bfloat16),
        in_specs=[VMEM], out_specs=VMEM, compiler_params=params, cost_estimate=cost(ch, ch),
    )(ends)
    own = kept(white)
    below = whiten(below, swap(half_power(below)))
    parts = pairs(own, [white, below], False)
    far, parts = lax.optimization_barrier((far, parts))
    above, far = lax.optimization_barrier((above, far))
    kinds = [jnp.float32] + [jnp.bfloat16] * (n_win - 1)
    near = turns(split_windows(parts, kinds), "win", n_win)
    remote = turns(pairs(kept(above), [below] + far, True), "freq", n_freq)
    shape = (remote[0].shape[0], ch * ch, width)
    n_ships = n_win // n_freq
    shipped = pl.pallas_call(
        functools.partial(group_kernel, n_freq),
        out_shape=[jax.ShapeDtypeStruct((n_freq,) + shape, jnp.bfloat16)] * n_ships,
        in_specs=[VMEM] * n_freq, out_specs=[VMEM] * n_ships, compiler_params=params,
    )(*remote)
    arrived = []
    for ship, block in enumerate(shipped):
        route = [
            ((c * n_win + w) * n_freq + f, ((c - 1) * n_win + (w + ship * n_freq + f) % n_win) * n_freq + f)
            for c in range(1, n_chan - 1) for w in range(n_win) for f in range(n_freq)
        ]
        arrived.append(lax.ppermute(block, ("chan", "win", "freq"), route))
    arrived = pl.pallas_call(
        functools.partial(ungroup_kernel, n_ships),
        out_shape=[jax.ShapeDtypeStruct(shape, jnp.bfloat16 if n_ships == 1 else jnp.float32)] * n_freq,
        in_specs=[VMEM] * n_ships, out_specs=[VMEM] * n_freq, compiler_params=params,
    )(*arrived)
    arrived = turns(arrived, "freq", n_freq)
    scale = 1.0 / math.sqrt(w_dev * n_win * n_bins)
    factors = jnp.repeat(pair_mask.T.astype(jnp.float32) * scale, ch, axis=1)[..., None]
    return pl.pallas_call(
        functools.partial(combine_kernel, n_win, n_freq),
        out_shape=jax.ShapeDtypeStruct((ch, reach + 1, ch, width), jnp.float32),
        in_specs=[VMEM] * (1 + n_win + n_freq), out_specs=VMEM, compiler_params=params,
    )(factors, *near, *arrived)


def solution(mesh):
    in_specs = (
        P("win", None, ("fibre", "chan"), "freq"),
        P(("fibre", "win")),
        P(("fibre", "chan"), None),
    )
    out_specs = P(("fibre", "chan"), None, None, ("win", "freq"))
    return jax.shard_map(local, mesh=mesh, in_specs=in_specs, out_specs=out_specs, check_vma=False)
```

```python
import functools
import math

import jax
import jax.numpy as jnp
import numpy as np
from jax import lax
from jax.experimental import pallas as pl
from jax.experimental.pallas import tpu as pltpu
from jax.sharding import PartitionSpec as P

LAGS = 1024
F_LO = 60
NSAMP = 15000
EPS = 1e-06
LANES = 128
SUBLANES = 8
FINE = 32
BLOCK = 256
VMEM_LIMIT = 16 * 1024 * 1024


def from_behind(block, axis, distance):
    devices = range(lax.axis_size(axis))
    route = [(i - distance, i) for i in devices if i - distance in devices]
    return lax.ppermute(block, axis, route)


def phases(bins, half_lags):
    turns = np.remainder(np.asarray(bins, np.int64)[:, None] * np.asarray(half_lags, np.int64)[None, :], 2 * NSAMP)
    angle = turns * (math.pi / NSAMP)
    return np.stack([np.cos(angle), np.sin(angle)]).astype(np.float32)


def split(value):
    high = value.astype(jnp.bfloat16)
    return high, (value - high.astype(jnp.float32)).astype(jnp.bfloat16)


def bin_power(x):
    x = x.astype(jnp.float32)
    return jnp.sum(x[0] * x[0] + x[1] * x[1], axis=-1, keepdims=True)


def power_kernel(x_ref, power_ref, copy_ref):
    for w in range(x_ref.shape[0]):
        x = x_ref[w]
        power_ref[w] = bin_power(x)
        copy_ref[w] = x


def partial_kernel(x_ref, power_ref):
    for w in range(x_ref.shape[0]):
        power_ref[w] = bin_power(x_ref[w])


def whiten_kernel(n_bins, x_ref, *refs):
    out_ref = refs[-1]
    for w in range(x_ref.shape[0]):
        power = bin_power(x_ref[w])
        for ref in refs[:-1]:
            power = power + ref[w]
        scale = lax.rsqrt(power / n_bins + EPS)
        for part in range(2):
            out_ref[w, part] = (x_ref[w, part].astype(jnp.float32) * scale).astype(jnp.bfloat16)


def keep_kernel(keep_ref, white_ref, out_ref):
    for w in range(white_ref.shape[0]):
        value = white_ref[w].astype(jnp.float32) * keep_ref[:, w:w + 1].astype(jnp.float32)[None]
        out_ref[w, 0] = value[0]
        out_ref[w, 1] = value[1]
        out_ref[w, 2] = value[0] + value[1]


def table_kernel(base_ref, table_ref):
    f_dev, width = table_ref.shape[1:]
    coarse = base_ref.shape[1] - FINE
    start = lax.axis_index("freq") * (f_dev // FINE)
    for block in range(0, width, BLOCK):
        lags = slice(block, block + BLOCK)
        fine_cos = base_ref[0, coarse:, lags]
        fine_sin = base_ref[1, coarse:, lags]

        def body(step, carry):
            first = pl.multiple_of(start + step * SUBLANES, SUBLANES)
            coarse_cos = base_ref[0, pl.ds(first, SUBLANES), lags]
            coarse_sin = base_ref[1, pl.ds(first, SUBLANES), lags]
            for n in range(SUBLANES):
                cos_a, sin_a = coarse_cos[n:n + 1], coarse_sin[n:n + 1]
                rows = pl.ds(pl.multiple_of((step * SUBLANES + n) * FINE, FINE), FINE)
                table_ref[0, rows, lags], table_ref[1, rows, lags] = split(cos_a * fine_cos - sin_a * fine_sin)
                table_ref[2, rows, lags], table_ref[3, rows, lags] = split(cos_a * fine_sin + sin_a * fine_cos)
            return carry

        lax.fori_loop(0, f_dev // (FINE * SUBLANES), body, 0)


def cross_tile(base_ref, partner_ref, lanes):
    w_dev, _, ch, _ = base_ref.shape
    sums = [[None] * ch for _ in range(3)]
    for w in range(w_dev):
        partner_re = partner_ref[w, 0, :, lanes].astype(jnp.float32)
        partner_im = partner_ref[w, 1, :, lanes].astype(jnp.float32)
        factors = (partner_re + partner_im, partner_re - partner_im, partner_re)
        for i in range(ch):
            for n, factor in enumerate(factors):
                product = base_ref[w, n, i:i + 1, lanes] * factor
                sums[n][i] = product if w == 0 else sums[n][i] + product
    real = [both - im for im, both in zip(sums[1], sums[2])]
    imag = [both - re for re, both in zip(sums[0], sums[2])]
    return real, imag


def pairs_kernel(n_partners, n_win, n_freq, by_window, base_ref, *refs):
    partner_refs = refs[:n_partners]
    twist_ref, table_ref = refs[n_partners:n_partners + 2]
    out_refs = refs[-2 - n_freq:-2]
    rows_ref, sums_ref = refs[-2:]
    ch, f_dev = base_ref.shape[2:]
    pairs = ch * ch
    groups = n_win * n_freq
    width = out_refs[0].shape[-1]
    freq, win = lax.axis_index("freq"), lax.axis_index("win")
    dot = functools.partial(jnp.dot, preferred_element_type=jnp.float32)
    count = n_partners * pairs

    def prepare(lanes):
        cos = twist_ref[freq, 0:1, lanes]
        sin = twist_ref[freq, 1:2, lanes]
        for k, partner_ref in enumerate(partner_refs):
            real, imag = cross_tile(base_ref, partner_ref, lanes)
            for i in range(0, ch, 2):
                rows = k * pairs + i * ch
                re = jnp.concatenate(real[i:i + 2], axis=0)
                im = jnp.concatenate(imag[i:i + 2], axis=0)
                for part, value in enumerate((re * cos + im * sin, im * cos - re * sin)):
                    high, low = split(value)
                    rows_ref[part, rows:rows + 2 * ch, lanes] = high
                    rows_ref[part, count + rows:count + rows + 2 * ch, lanes] = low

    def body(tile, carry):
        prepare(pl.ds(pl.multiple_of(tile * LANES, LANES), LANES))
        return carry

    def transform(part, bins):
        both = dot(rows_ref[part, :, bins], table_ref[2 * part, bins])
        return both[:count] + both[count:] + dot(rows_ref[part, :count, bins], table_ref[2 * part + 1, bins])

    tiles = f_dev // LANES
    early = tiles - tiles // 2
    lax.fori_loop(0, early, body, 0)
    for part in range(2):
        sums_ref[part] = transform(part, slice(0, early * LANES))
    for tile in range(early, tiles):
        prepare(slice(tile * LANES, (tile + 1) * LANES))
    for part in range(2):
        sums_ref[part] += transform(part, slice(early * LANES, f_dev))
    for turn_freq, out_ref in enumerate(out_refs):
        core = (freq + turn_freq) % n_freq
        for turn_win in range(n_win):
            if by_window:
                away = turn_win // n_freq * n_freq + core
                owner = (win + away) % n_win * n_freq + (core + turn_win) % n_freq
            else:
                owner = (win + turn_win) % n_win * n_freq + core
            upper = owner >= groups // 2
            block = jnp.where(upper, owner - groups // 2, groups // 2 - 1 - owner)
            sign = jnp.where(upper, -1.0, 1.0)
            lags = pl.ds(pl.multiple_of(block * width, LANES), width)
            for k in range(n_partners):
                rows = slice(k * pairs, (k + 1) * pairs)
                out_ref[k, turn_win] = sums_ref[0, rows, lags] + sign * sums_ref[1, rows, lags]


def add_kernel(n_parts, *refs):
    for turn, out_ref in enumerate(refs[n_parts:]):
        total = refs[0][:, turn]
        for ref in refs[1:n_parts]:
            total = total + ref[:, turn]
        out_ref[...] = total.astype(out_ref.dtype)


def group_kernel(n_parts, *refs):
    out_refs = refs[n_parts:]
    per_ship = refs[0].shape[1] // len(out_refs)
    for ship, out_ref in enumerate(out_refs):
        for turn in range(per_ship):
            total = refs[0][:, ship * per_ship + turn]
            for ref in refs[1:n_parts]:
                total = total + ref[:, ship * per_ship + turn]
            out_ref[turn] = total.astype(out_ref.dtype)


def ungroup_kernel(n_ships, *refs):
    for turn, out_ref in enumerate(refs[n_ships:]):
        total = refs[0][turn].astype(jnp.float32)
        for ref in refs[1:n_ships]:
            total = total + ref[turn].astype(jnp.float32)
        out_ref[...] = total.astype(out_ref.dtype)


def reverse_lanes(value):
    backward = LANES - 1 - lax.broadcasted_iota(jnp.int32, (value.shape[0], LANES), 1)
    pieces = [
        jnp.take_along_axis(value[:, start:start + LANES], backward, axis=1, mode="promise_in_bounds")
        for start in range(0, value.shape[1], LANES)
    ]
    return jnp.concatenate(pieces[::-1], axis=1)


def combine_kernel(n_win, n_freq, factor_ref, *refs):
    out_ref = refs[-1]
    ch = out_ref.shape[0]
    lower = lax.axis_index("win") * n_freq + lax.axis_index("freq") < n_win * n_freq // 2
    k = 0
    for parts in (refs[:n_win], refs[n_win:-1]):
        for n in range(parts[0].shape[0]):
            total = parts[0][n].astype(jnp.float32)
            for ref in parts[1:]:
                total = total + ref[n].astype(jnp.float32)
            total = jnp.where(lower, reverse_lanes(total), total) * factor_ref[k]
            for i in range(ch):
                out_ref[i, k] = total[i * ch:(i + 1) * ch]
            k += 1


VMEM = pl.BlockSpec(memory_space=pltpu.VMEM)


def local(spectra, keep, pair_mask):
    w_dev, _, ch, f_dev = spectra.shape
    reach = pair_mask.shape[1] - 1
    n_chan, n_win, n_freq = (lax.axis_size(a) for a in ("chan", "win", "freq"))
    width = LAGS // (n_win * n_freq)
    n_bins = f_dev * n_freq
    params = pltpu.CompilerParams(vmem_limit_bytes=VMEM_LIMIT)


    def cost(flops, size):
        return pl.CostEstimate(flops=flops, bytes_accessed=size, transcendentals=0)

    below = from_behind(spectra, "chan", -1)
    far_routes = [[(c + away, c) for c in range(1, n_chan - away)] for away in range(2, reach)]
    power, copied = pl.pallas_call(
        power_kernel,
        out_shape=[
            jax.ShapeDtypeStruct((w_dev, ch, 1), jnp.float32),
            jax.ShapeDtypeStruct(spectra.shape, spectra.dtype),
        ],
        in_specs=[VMEM], out_specs=[VMEM] * 2, compiler_params=params, cost_estimate=cost(ch, ch),
    )(spectra)
    twist = phases(F_LO + np.arange(n_bins), np.ones(1)).reshape(2, n_freq, f_dev)
    twist = jnp.asarray(np.moveaxis(twist, 0, 1))

    def swap(power):
        routes = [[(f, (f + turn) % n_freq) for f in range(n_freq)] for turn in range(1, n_freq)]
        return [lax.ppermute(power, "freq", route) for route in routes]

    def half_power(block):
        return pl.pallas_call(
            partial_kernel,
            out_shape=jax.ShapeDtypeStruct(power.shape, jnp.float32),
            in_specs=[VMEM], out_specs=VMEM, compiler_params=params, cost_estimate=cost(ch, ch),
        )(block)

    def whiten(block, others):
        return pl.pallas_call(
            functools.partial(whiten_kernel, n_bins),
            out_shape=jax.ShapeDtypeStruct(block.shape, jnp.bfloat16),
            in_specs=[VMEM] * (1 + len(others)), out_specs=VMEM, compiler_params=params,
        )(block, *others)

    def kept(block):
        return pl.pallas_call(
            keep_kernel,
            out_shape=jax.ShapeDtypeStruct((w_dev, 3) + block.shape[2:], jnp.float32),
            in_specs=[VMEM] * 2, out_specs=VMEM, compiler_params=params,
        )(keep.reshape(1, w_dev), block)

    def pairs(base, partners, by_window):
        n = len(partners)
        return pl.pallas_call(
            functools.partial(pairs_kernel, n, n_win, n_freq, by_window),
            out_shape=[jax.ShapeDtypeStruct((n, n_win, ch * ch, width), jnp.float32)] * n_freq,
            in_specs=[VMEM] * (3 + n), out_specs=[VMEM] * n_freq,
            scratch_shapes=[
                pltpu.VMEM((2, 2 * n * ch * ch, f_dev), jnp.bfloat16),
                pltpu.VMEM((2, n * ch * ch, LAGS // 2), jnp.float32),
            ],
            compiler_params=params,
            cost_estimate=cost(ch, ch),
        )(base, *partners, twist, table)

    def turns(parts, axis, size):
        received = [parts[0]]
        for turn in range(1, size):
            route = [(g, (g + turn) % size) for g in range(size)]
            received.append(lax.ppermute(parts[turn], axis, route))
        return received

    def split_windows(parts, kinds):
        n = parts[0].shape[0]
        return pl.pallas_call(
            functools.partial(add_kernel, n_freq),
            out_shape=[jax.ShapeDtypeStruct((n, ch * ch, width), kind) for kind in kinds],
            in_specs=[VMEM] * n_freq, out_specs=[VMEM] * n_win, compiler_params=params,
        )(*turns(parts, "freq", n_freq))

    white = whiten(copied, swap(power))
    far = [lax.ppermute(white, "chan", route) for route in far_routes]
    above = lax.ppermute(white, "chan", [(c - 1, c) for c in range(1, n_chan - 1)])
    half_lags = 2 * np.arange(LAGS // 2) + 1
    coarse = phases(np.arange(0, n_bins, FINE), half_lags)
    fine = phases(F_LO + np.arange(FINE), half_lags)
    white, ends = lax.optimization_barrier((white, jnp.asarray(np.concatenate([coarse, fine], axis=1))))
    table = pl.pallas_call(
        table_kernel,
        out_shape=jax.ShapeDtypeStruct((4, f_dev, LAGS // 2), jnp.bfloat16),
        in_specs=[VMEM], out_specs=VMEM, compiler_params=params, cost_estimate=cost(ch, ch),
    )(ends)
    own = kept(white)
    below = whiten(below, swap(half_power(below)))
    parts = pairs(own, [white, below], False)
    far, parts = lax.optimization_barrier((far, parts))
    above, far = lax.optimization_barrier((above, far))
    kinds = [jnp.float32] + [jnp.bfloat16] * (n_win - 1)
    near = turns(split_windows(parts, kinds), "win", n_win)
    remote = turns(pairs(kept(above), [below] + far, True), "freq", n_freq)
    shape = (remote[0].shape[0], ch * ch, width)
    n_ships = n_win // n_freq
    shipped = pl.pallas_call(
        functools.partial(group_kernel, n_freq),
        out_shape=[jax.ShapeDtypeStruct((n_freq,) + shape, jnp.bfloat16)] * n_ships,
        in_specs=[VMEM] * n_freq, out_specs=[VMEM] * n_ships, compiler_params=params,
    )(*remote)
    arrived = []
    for ship, block in enumerate(shipped):
        route = [
            ((c * n_win + w) * n_freq + f, ((c - 1) * n_win + (w + ship * n_freq + f) % n_win) * n_freq + f)
            for c in range(1, n_chan - 1) for w in range(n_win) for f in range(n_freq)
        ]
        arrived.append(lax.ppermute(block, ("chan", "win", "freq"), route))
    arrived = pl.pallas_call(
        functools.partial(ungroup_kernel, n_ships),
        out_shape=[jax.ShapeDtypeStruct(shape, jnp.bfloat16 if n_ships == 1 else jnp.float32)] * n_freq,
        in_specs=[VMEM] * n_ships, out_specs=[VMEM] * n_freq, compiler_params=params,
    )(*arrived)
    arrived = turns(arrived, "freq", n_freq)
    scale = 1.0 / math.sqrt(w_dev * n_win * n_bins)
    factors = jnp.repeat(pair_mask.T.astype(jnp.float32) * scale, ch, axis=1)[..., None]
    return pl.pallas_call(
        functools.partial(combine_kernel, n_win, n_freq),
        out_shape=jax.ShapeDtypeStruct((ch, reach + 1, ch, width), jnp.float32),
        in_specs=[VMEM] * (1 + n_win + n_freq), out_specs=VMEM, compiler_params=params,
    )(factors, *near, *arrived)


def solution(mesh):
    in_specs = (
        P("win", None, ("fibre", "chan"), "freq"),
        P(("fibre", "win")),
        P(("fibre", "chan"), None),
    )
    out_specs = P(("fibre", "chan"), None, None, ("win", "freq"))
    return jax.shard_map(local, mesh=mesh, in_specs=in_specs, out_specs=out_specs, check_vma=False)
```

```python
import functools
import math

import jax
import jax.numpy as jnp
import numpy as np
from jax import lax
from jax.experimental import pallas as pl
from jax.experimental.pallas import tpu as pltpu
from jax.sharding import PartitionSpec as P

LAGS = 1024
F_LO = 60
NSAMP = 15000
EPS = 1e-06
LANES = 128
SUBLANES = 8
FINE = 32
BLOCK = 256
STEPS = 4
VMEM_LIMIT = 16 * 1024 * 1024


def from_behind(block, axis, distance):
    devices = range(lax.axis_size(axis))
    route = [(i - distance, i) for i in devices if i - distance in devices]
    return lax.ppermute(block, axis, route)


def phases(bins, half_lags):
    turns = np.remainder(np.asarray(bins, np.int64)[:, None] * np.asarray(half_lags, np.int64)[None, :], 2 * NSAMP)
    angle = turns * (math.pi / NSAMP)
    return np.stack([np.cos(angle), np.sin(angle)]).astype(np.float32)


def split(value):
    high = value.astype(jnp.bfloat16)
    return high, (value - high.astype(jnp.float32)).astype(jnp.bfloat16)


def bin_power(x):
    x = x.astype(jnp.float32)
    return jnp.sum(x[0] * x[0] + x[1] * x[1], axis=-1, keepdims=True)


def power_kernel(x_ref, power_ref, copy_ref):
    for w in range(x_ref.shape[0]):
        x = x_ref[w]
        power_ref[w] = bin_power(x)
        copy_ref[w] = x


def partial_kernel(x_ref, power_ref):
    for w in range(x_ref.shape[0]):
        power_ref[w] = bin_power(x_ref[w])


def whiten_kernel(n_bins, x_ref, *refs):
    out_ref = refs[-1]
    for w in range(x_ref.shape[0]):
        power = bin_power(x_ref[w])
        for ref in refs[:-1]:
            power = power + ref[w]
        scale = lax.rsqrt(power / n_bins + EPS)
        for part in range(2):
            out_ref[w, part] = (x_ref[w, part].astype(jnp.float32) * scale).astype(jnp.bfloat16)


def keep_kernel(keep_ref, white_ref, out_ref):
    for w in range(white_ref.shape[0]):
        value = white_ref[w].astype(jnp.float32) * keep_ref[:, w:w + 1].astype(jnp.float32)[None]
        out_ref[w, 0] = value[0]
        out_ref[w, 1] = value[1]
        out_ref[w, 2] = value[0] + value[1]


def table_kernel(base_ref, table_ref):
    f_dev, width = table_ref.shape[1:]
    coarse = base_ref.shape[1] - FINE
    start = lax.axis_index("freq") * (f_dev // FINE)
    for block in range(0, width, BLOCK):
        lags = slice(block, block + BLOCK)
        fine_cos = base_ref[0, coarse:, lags]
        fine_sin = base_ref[1, coarse:, lags]

        def body(step, carry):
            first = pl.multiple_of(start + step * SUBLANES, SUBLANES)
            coarse_cos = base_ref[0, pl.ds(first, SUBLANES), lags]
            coarse_sin = base_ref[1, pl.ds(first, SUBLANES), lags]
            for n in range(SUBLANES):
                cos_a, sin_a = coarse_cos[n:n + 1], coarse_sin[n:n + 1]
                rows = pl.ds(pl.multiple_of((step * SUBLANES + n) * FINE, FINE), FINE)
                table_ref[0, rows, lags], table_ref[1, rows, lags] = split(cos_a * fine_cos - sin_a * fine_sin)
                table_ref[2, rows, lags], table_ref[3, rows, lags] = split(cos_a * fine_sin + sin_a * fine_cos)
            return carry

        lax.fori_loop(0, f_dev // (FINE * SUBLANES), body, 0)


def cross_tile(base_ref, partner_ref, lanes):
    w_dev, _, ch, _ = base_ref.shape
    sums = [[None] * ch for _ in range(3)]
    for w in range(w_dev):
        partner_re = partner_ref[w, 0, :, lanes].astype(jnp.float32)
        partner_im = partner_ref[w, 1, :, lanes].astype(jnp.float32)
        factors = (partner_re + partner_im, partner_re - partner_im, partner_re)
        for i in range(ch):
            for n, factor in enumerate(factors):
                product = base_ref[w, n, i:i + 1, lanes] * factor
                sums[n][i] = product if w == 0 else sums[n][i] + product
    real = [both - im for im, both in zip(sums[1], sums[2])]
    imag = [both - re for re, both in zip(sums[0], sums[2])]
    return real, imag


def pairs_kernel(n_partners, n_win, n_freq, by_window, base_ref, *refs):
    partner_refs = refs[:n_partners]
    twist_ref, table_ref = refs[n_partners:n_partners + 2]
    out_refs = refs[-2 - n_freq:-2]
    rows_ref, sums_ref = refs[-2:]
    ch, f_dev = base_ref.shape[2:]
    pairs = ch * ch
    groups = n_win * n_freq
    width = out_refs[0].shape[-1]
    freq, win = lax.axis_index("freq"), lax.axis_index("win")
    dot = functools.partial(jnp.dot, preferred_element_type=jnp.float32)
    count = n_partners * pairs

    def prepare(lanes):
        cos = twist_ref[freq, 0:1, lanes]
        sin = twist_ref[freq, 1:2, lanes]
        for k, partner_ref in enumerate(partner_refs):
            real, imag = cross_tile(base_ref, partner_ref, lanes)
            for i in range(0, ch, 2):
                rows = k * pairs + i * ch
                re = jnp.concatenate(real[i:i + 2], axis=0)
                im = jnp.concatenate(imag[i:i + 2], axis=0)
                for part, value in enumerate((re * cos + im * sin, im * cos - re * sin)):
                    high, low = split(value)
                    rows_ref[part, rows:rows + 2 * ch, lanes] = high
                    rows_ref[part, count + rows:count + rows + 2 * ch, lanes] = low

    def body(tile, carry):
        prepare(pl.ds(pl.multiple_of(tile * LANES, LANES), LANES))
        return carry

    def transform(part, bins):
        both = dot(rows_ref[part, :, bins], table_ref[2 * part, bins])
        return both[:count] + both[count:] + dot(rows_ref[part, :count, bins], table_ref[2 * part + 1, bins])

    tiles = f_dev // LANES
    per_step = max(1, tiles // STEPS)
    lax.fori_loop(0, per_step, body, 0)
    for first in range(0, tiles, per_step):
        for part in range(2):
            value = transform(part, slice(first * LANES, (first + per_step) * LANES))
            sums_ref[part] = value if first == 0 else sums_ref[part] + value
        for tile in range(first + per_step, min(first + 2 * per_step, tiles)):
            prepare(slice(tile * LANES, (tile + 1) * LANES))
    for turn_freq, out_ref in enumerate(out_refs):
        core = (freq + turn_freq) % n_freq
        for turn_win in range(n_win):
            if by_window:
                away = turn_win // n_freq * n_freq + core
                owner = (win + away) % n_win * n_freq + (core + turn_win) % n_freq
            else:
                owner = (win + turn_win) % n_win * n_freq + core
            upper = owner >= groups // 2
            block = jnp.where(upper, owner - groups // 2, groups // 2 - 1 - owner)
            sign = jnp.where(upper, -1.0, 1.0)
            lags = pl.ds(pl.multiple_of(block * width, LANES), width)
            for k in range(n_partners):
                rows = slice(k * pairs, (k + 1) * pairs)
                out_ref[k, turn_win] = sums_ref[0, rows, lags] + sign * sums_ref[1, rows, lags]


def add_kernel(n_parts, *refs):
    for turn, out_ref in enumerate(refs[n_parts:]):
        total = refs[0][:, turn]
        for ref in refs[1:n_parts]:
            total = total + ref[:, turn]
        out_ref[...] = total.astype(out_ref.dtype)


def group_kernel(n_parts, *refs):
    out_refs = refs[n_parts:]
    per_ship = refs[0].shape[1] // len(out_refs)
    for ship, out_ref in enumerate(out_refs):
        for turn in range(per_ship):
            total = refs[0][:, ship * per_ship + turn]
            for ref in refs[1:n_parts]:
                total = total + ref[:, ship * per_ship + turn]
            out_ref[turn] = total.astype(out_ref.dtype)


def ungroup_kernel(n_ships, *refs):
    for turn, out_ref in enumerate(refs[n_ships:]):
        total = refs[0][turn].astype(jnp.float32)
        for ref in refs[1:n_ships]:
            total = total + ref[turn].astype(jnp.float32)
        out_ref[...] = total.astype(out_ref.dtype)


def reverse_lanes(value):
    backward = LANES - 1 - lax.broadcasted_iota(jnp.int32, (value.shape[0], LANES), 1)
    pieces = [
        jnp.take_along_axis(value[:, start:start + LANES], backward, axis=1, mode="promise_in_bounds")
        for start in range(0, value.shape[1], LANES)
    ]
    return jnp.concatenate(pieces[::-1], axis=1)


def combine_kernel(n_win, n_freq, factor_ref, *refs):
    out_ref = refs[-1]
    ch = out_ref.shape[0]
    lower = lax.axis_index("win") * n_freq + lax.axis_index("freq") < n_win * n_freq // 2
    k = 0
    for parts in (refs[:n_win], refs[n_win:-1]):
        for n in range(parts[0].shape[0]):
            total = parts[0][n].astype(jnp.float32)
            for ref in parts[1:]:
                total = total + ref[n].astype(jnp.float32)
            total = jnp.where(lower, reverse_lanes(total), total) * factor_ref[k]
            for i in range(ch):
                out_ref[i, k] = total[i * ch:(i + 1) * ch]
            k += 1


VMEM = pl.BlockSpec(memory_space=pltpu.VMEM)


def local(spectra, keep, pair_mask):
    w_dev, _, ch, f_dev = spectra.shape
    reach = pair_mask.shape[1] - 1
    n_chan, n_win, n_freq = (lax.axis_size(a) for a in ("chan", "win", "freq"))
    width = LAGS // (n_win * n_freq)
    n_bins = f_dev * n_freq
    params = pltpu.CompilerParams(vmem_limit_bytes=VMEM_LIMIT)


    def cost(flops, size):
        return pl.CostEstimate(flops=flops, bytes_accessed=size, transcendentals=0)

    below = from_behind(spectra, "chan", -1)
    far_routes = [[(c + away, c) for c in range(1, n_chan - away)] for away in range(2, reach)]
    power, copied = pl.pallas_call(
        power_kernel,
        out_shape=[
            jax.ShapeDtypeStruct((w_dev, ch, 1), jnp.float32),
            jax.ShapeDtypeStruct(spectra.shape, spectra.dtype),
        ],
        in_specs=[VMEM], out_specs=[VMEM] * 2, compiler_params=params, cost_estimate=cost(ch, ch),
    )(spectra)
    twist = phases(F_LO + np.arange(n_bins), np.ones(1)).reshape(2, n_freq, f_dev)
    twist = jnp.asarray(np.moveaxis(twist, 0, 1))

    def swap(power):
        routes = [[(f, (f + turn) % n_freq) for f in range(n_freq)] for turn in range(1, n_freq)]
        return [lax.ppermute(power, "freq", route) for route in routes]

    def half_power(block):
        return pl.pallas_call(
            partial_kernel,
            out_shape=jax.ShapeDtypeStruct(power.shape, jnp.float32),
            in_specs=[VMEM], out_specs=VMEM, compiler_params=params, cost_estimate=cost(ch, ch),
        )(block)

    def whiten(block, others):
        return pl.pallas_call(
            functools.partial(whiten_kernel, n_bins),
            out_shape=jax.ShapeDtypeStruct(block.shape, jnp.bfloat16),
            in_specs=[VMEM] * (1 + len(others)), out_specs=VMEM, compiler_params=params,
        )(block, *others)

    def kept(block):
        return pl.pallas_call(
            keep_kernel,
            out_shape=jax.ShapeDtypeStruct((w_dev, 3) + block.shape[2:], jnp.float32),
            in_specs=[VMEM] * 2, out_specs=VMEM, compiler_params=params,
        )(keep.reshape(1, w_dev), block)

    def pairs(base, partners, by_window):
        n = len(partners)
        return pl.pallas_call(
            functools.partial(pairs_kernel, n, n_win, n_freq, by_window),
            out_shape=[jax.ShapeDtypeStruct((n, n_win, ch * ch, width), jnp.float32)] * n_freq,
            in_specs=[VMEM] * (3 + n), out_specs=[VMEM] * n_freq,
            scratch_shapes=[
                pltpu.VMEM((2, 2 * n * ch * ch, f_dev), jnp.bfloat16),
                pltpu.VMEM((2, n * ch * ch, LAGS // 2), jnp.float32),
            ],
            compiler_params=params,
            cost_estimate=cost(ch, ch),
        )(base, *partners, twist, table)

    def turns(parts, axis, size):
        received = [parts[0]]
        for turn in range(1, size):
            route = [(g, (g + turn) % size) for g in range(size)]
            received.append(lax.ppermute(parts[turn], axis, route))
        return received

    def split_windows(parts, kinds):
        n = parts[0].shape[0]
        return pl.pallas_call(
            functools.partial(add_kernel, n_freq),
            out_shape=[jax.ShapeDtypeStruct((n, ch * ch, width), kind) for kind in kinds],
            in_specs=[VMEM] * n_freq, out_specs=[VMEM] * n_win, compiler_params=params,
        )(*turns(parts, "freq", n_freq))

    white = whiten(copied, swap(power))
    far = [lax.ppermute(white, "chan", route) for route in far_routes]
    above = lax.ppermute(white, "chan", [(c - 1, c) for c in range(1, n_chan - 1)])
    half_lags = 2 * np.arange(LAGS // 2) + 1
    coarse = phases(np.arange(0, n_bins, FINE), half_lags)
    fine = phases(F_LO + np.arange(FINE), half_lags)
    white, ends = lax.optimization_barrier((white, jnp.asarray(np.concatenate([coarse, fine], axis=1))))
    table = pl.pallas_call(
        table_kernel,
        out_shape=jax.ShapeDtypeStruct((4, f_dev, LAGS // 2), jnp.bfloat16),
        in_specs=[VMEM], out_specs=VMEM, compiler_params=params, cost_estimate=cost(ch, ch),
    )(ends)
    own = kept(white)
    below = whiten(below, swap(half_power(below)))
    parts = pairs(own, [white, below], False)
    far, parts = lax.optimization_barrier((far, parts))
    above, far = lax.optimization_barrier((above, far))
    kinds = [jnp.float32] + [jnp.bfloat16] * (n_win - 1)
    near = turns(split_windows(parts, kinds), "win", n_win)
    remote = turns(pairs(kept(above), [below] + far, True), "freq", n_freq)
    shape = (remote[0].shape[0], ch * ch, width)
    n_ships = n_win // n_freq
    shipped = pl.pallas_call(
        functools.partial(group_kernel, n_freq),
        out_shape=[jax.ShapeDtypeStruct((n_freq,) + shape, jnp.bfloat16)] * n_ships,
        in_specs=[VMEM] * n_freq, out_specs=[VMEM] * n_ships, compiler_params=params,
    )(*remote)
    arrived = []
    for ship, block in enumerate(shipped):
        route = [
            ((c * n_win + w) * n_freq + f, ((c - 1) * n_win + (w + ship * n_freq + f) % n_win) * n_freq + f)
            for c in range(1, n_chan - 1) for w in range(n_win) for f in range(n_freq)
        ]
        arrived.append(lax.ppermute(block, ("chan", "win", "freq"), route))
    arrived = pl.pallas_call(
        functools.partial(ungroup_kernel, n_ships),
        out_shape=[jax.ShapeDtypeStruct(shape, jnp.bfloat16 if n_ships == 1 else jnp.float32)] * n_freq,
        in_specs=[VMEM] * n_ships, out_specs=[VMEM] * n_freq, compiler_params=params,
    )(*arrived)
    arrived = turns(arrived, "freq", n_freq)
    scale = 1.0 / math.sqrt(w_dev * n_win * n_bins)
    factors = jnp.repeat(pair_mask.T.astype(jnp.float32) * scale, ch, axis=1)[..., None]
    return pl.pallas_call(
        functools.partial(combine_kernel, n_win, n_freq),
        out_shape=jax.ShapeDtypeStruct((ch, reach + 1, ch, width), jnp.float32),
        in_specs=[VMEM] * (1 + n_win + n_freq), out_specs=VMEM, compiler_params=params,
    )(factors, *near, *arrived)


def solution(mesh):
    in_specs = (
        P("win", None, ("fibre", "chan"), "freq"),
        P(("fibre", "win")),
        P(("fibre", "chan"), None),
    )
    out_specs = P(("fibre", "chan"), None, None, ("win", "freq"))
    return jax.shard_map(local, mesh=mesh, in_specs=in_specs, out_specs=out_specs, check_vma=False)
```

```python
import functools
import math

import jax
import jax.numpy as jnp
import numpy as np
from jax import lax
from jax.experimental import pallas as pl
from jax.experimental.pallas import tpu as pltpu
from jax.sharding import PartitionSpec as P

LAGS = 1024
F_LO = 60
NSAMP = 15000
EPS = 1e-06
LANES = 128
SUBLANES = 8
FINE = 32
BLOCK = 256
STEPS = 4
VMEM_LIMIT = 16 * 1024 * 1024


def from_behind(block, axis, distance):
    devices = range(lax.axis_size(axis))
    route = [(i - distance, i) for i in devices if i - distance in devices]
    return lax.ppermute(block, axis, route)


def phases(bins, half_lags):
    turns = np.remainder(np.asarray(bins, np.int64)[:, None] * np.asarray(half_lags, np.int64)[None, :], 2 * NSAMP)
    angle = turns * (math.pi / NSAMP)
    return np.stack([np.cos(angle), np.sin(angle)]).astype(np.float32)


def split(value):
    high = value.astype(jnp.bfloat16)
    return high, (value - high.astype(jnp.float32)).astype(jnp.bfloat16)


def bin_power(x):
    x = x.astype(jnp.float32)
    return jnp.sum(x[0] * x[0] + x[1] * x[1], axis=-1, keepdims=True)


def power_kernel(x_ref, power_ref, copy_ref):
    for w in range(x_ref.shape[0]):
        x = x_ref[w]
        power_ref[w] = bin_power(x)
        copy_ref[w] = x


def partial_kernel(x_ref, power_ref):
    for w in range(x_ref.shape[0]):
        power_ref[w] = bin_power(x_ref[w])


def whiten_kernel(n_bins, x_ref, *refs):
    out_ref = refs[-1]
    for w in range(x_ref.shape[0]):
        power = bin_power(x_ref[w])
        for ref in refs[:-1]:
            power = power + ref[w]
        scale = lax.rsqrt(power / n_bins + EPS)
        for part in range(2):
            out_ref[w, part] = (x_ref[w, part].astype(jnp.float32) * scale).astype(jnp.bfloat16)


def keep_kernel(keep_ref, white_ref, out_ref):
    for w in range(white_ref.shape[0]):
        value = white_ref[w].astype(jnp.float32) * keep_ref[:, w:w + 1].astype(jnp.float32)[None]
        out_ref[w, 0] = value[0]
        out_ref[w, 1] = value[1]
        out_ref[w, 2] = value[0] + value[1]


def table_kernel(base_ref, table_ref):
    f_dev, width = table_ref.shape[1:]
    coarse = base_ref.shape[1] - FINE
    start = lax.axis_index("freq") * (f_dev // FINE)
    for block in range(0, width, BLOCK):
        lags = slice(block, block + BLOCK)
        fine_cos = base_ref[0, coarse:, lags]
        fine_sin = base_ref[1, coarse:, lags]

        def body(step, carry):
            first = pl.multiple_of(start + step * SUBLANES, SUBLANES)
            coarse_cos = base_ref[0, pl.ds(first, SUBLANES), lags]
            coarse_sin = base_ref[1, pl.ds(first, SUBLANES), lags]
            for n in range(SUBLANES):
                cos_a, sin_a = coarse_cos[n:n + 1], coarse_sin[n:n + 1]
                rows = pl.ds(pl.multiple_of((step * SUBLANES + n) * FINE, FINE), FINE)
                table_ref[0, rows, lags], table_ref[1, rows, lags] = split(cos_a * fine_cos - sin_a * fine_sin)
                table_ref[2, rows, lags], table_ref[3, rows, lags] = split(cos_a * fine_sin + sin_a * fine_cos)
            return carry

        lax.fori_loop(0, f_dev // (FINE * SUBLANES), body, 0)


def cross_tile(base_ref, partner_ref, lanes):
    w_dev, _, ch, _ = base_ref.shape
    sums = [[None] * ch for _ in range(3)]
    for w in range(w_dev):
        partner_re = partner_ref[w, 0, :, lanes].astype(jnp.float32)
        partner_im = partner_ref[w, 1, :, lanes].astype(jnp.float32)
        factors = (partner_re + partner_im, partner_re - partner_im, partner_re)
        for i in range(ch):
            for n, factor in enumerate(factors):
                product = base_ref[w, n, i:i + 1, lanes] * factor
                sums[n][i] = product if w == 0 else sums[n][i] + product
    real = [both - im for im, both in zip(sums[1], sums[2])]
    imag = [both - re for re, both in zip(sums[0], sums[2])]
    return real, imag


def pairs_kernel(n_partners, n_win, n_freq, by_window, base_ref, *refs):
    partner_refs = refs[:n_partners]
    twist_ref, table_ref = refs[n_partners:n_partners + 2]
    out_refs = refs[-2 - n_freq:-2]
    rows_ref, sums_ref = refs[-2:]
    ch, f_dev = base_ref.shape[2:]
    pairs = ch * ch
    groups = n_win * n_freq
    width = out_refs[0].shape[-1]
    freq, win = lax.axis_index("freq"), lax.axis_index("win")
    dot = functools.partial(jnp.dot, preferred_element_type=jnp.float32)
    count = n_partners * pairs

    def prepare(lanes):
        cos = twist_ref[freq, 0:1, lanes]
        sin = twist_ref[freq, 1:2, lanes]
        for k, partner_ref in enumerate(partner_refs):
            real, imag = cross_tile(base_ref, partner_ref, lanes)
            for i in range(0, ch, 2):
                rows = k * pairs + i * ch
                re = jnp.concatenate(real[i:i + 2], axis=0)
                im = jnp.concatenate(imag[i:i + 2], axis=0)
                for part, value in enumerate((re * cos + im * sin, im * cos - re * sin)):
                    high, low = split(value)
                    rows_ref[part, rows:rows + 2 * ch, lanes] = high
                    rows_ref[part, count + rows:count + rows + 2 * ch, lanes] = low

    def body(tile, carry):
        prepare(pl.ds(pl.multiple_of(tile * LANES, LANES), LANES))
        return carry

    def transform(part, bins):
        both = dot(rows_ref[part, :, bins], table_ref[2 * part, bins])
        return both[:count] + both[count:] + dot(rows_ref[part, :count, bins], table_ref[2 * part + 1, bins])

    tiles = f_dev // LANES
    per_step = max(1, tiles // STEPS)
    lax.fori_loop(0, per_step, body, 0)
    for first in range(0, tiles, per_step):
        for part in range(2):
            value = transform(part, slice(first * LANES, (first + per_step) * LANES))
            sums_ref[part] = value if first == 0 else sums_ref[part] + value
        for tile in range(first + per_step, min(first + 2 * per_step, tiles)):
            prepare(slice(tile * LANES, (tile + 1) * LANES))
    for turn_freq, out_ref in enumerate(out_refs):
        core = (freq + turn_freq) % n_freq
        for turn_win in range(n_win):
            if by_window:
                away = turn_win // n_freq * n_freq + core
                owner = (win + away) % n_win * n_freq + (core + turn_win) % n_freq
            else:
                owner = (win + turn_win) % n_win * n_freq + core
            upper = owner >= groups // 2
            block = jnp.where(upper, owner - groups // 2, groups // 2 - 1 - owner)
            sign = jnp.where(upper, -1.0, 1.0)
            lags = pl.ds(pl.multiple_of(block * width, LANES), width)
            for k in range(n_partners):
                rows = slice(k * pairs, (k + 1) * pairs)
                out_ref[k, turn_win] = sums_ref[0, rows, lags] + sign * sums_ref[1, rows, lags]


def add_kernel(n_parts, *refs):
    for turn, out_ref in enumerate(refs[n_parts:]):
        total = refs[0][:, turn]
        for ref in refs[1:n_parts]:
            total = total + ref[:, turn]
        out_ref[...] = total.astype(out_ref.dtype)


def group_kernel(n_parts, *refs):
    out_refs = refs[n_parts:]
    per_ship = refs[0].shape[1] // len(out_refs)
    for ship, out_ref in enumerate(out_refs):
        for turn in range(per_ship):
            total = refs[0][:, ship * per_ship + turn]
            for ref in refs[1:n_parts]:
                total = total + ref[:, ship * per_ship + turn]
            out_ref[turn] = total.astype(out_ref.dtype)


def ungroup_kernel(n_ships, *refs):
    for turn, out_ref in enumerate(refs[n_ships:]):
        total = refs[0][turn].astype(jnp.float32)
        for ref in refs[1:n_ships]:
            total = total + ref[turn].astype(jnp.float32)
        out_ref[...] = total.astype(out_ref.dtype)


def reverse_lanes(value):
    backward = LANES - 1 - lax.broadcasted_iota(jnp.int32, (value.shape[0], LANES), 1)
    pieces = [
        jnp.take_along_axis(value[:, start:start + LANES], backward, axis=1, mode="promise_in_bounds")
        for start in range(0, value.shape[1], LANES)
    ]
    return jnp.concatenate(pieces[::-1], axis=1)


def combine_kernel(n_win, n_freq, factor_ref, *refs):
    out_ref = refs[-1]
    ch = out_ref.shape[0]
    lower = lax.axis_index("win") * n_freq + lax.axis_index("freq") < n_win * n_freq // 2
    k = 0
    for parts in (refs[:n_win], refs[n_win:-1]):
        for n in range(parts[0].shape[0]):
            total = parts[0][n].astype(jnp.float32)
            for ref in parts[1:]:
                total = total + ref[n].astype(jnp.float32)
            total = jnp.where(lower, reverse_lanes(total), total) * factor_ref[k]
            for i in range(ch):
                out_ref[i, k] = total[i * ch:(i + 1) * ch]
            k += 1


VMEM = pl.BlockSpec(memory_space=pltpu.VMEM)


def local(spectra, keep, pair_mask):
    w_dev, _, ch, f_dev = spectra.shape
    reach = pair_mask.shape[1] - 1
    n_chan, n_win, n_freq = (lax.axis_size(a) for a in ("chan", "win", "freq"))
    width = LAGS // (n_win * n_freq)
    n_bins = f_dev * n_freq
    params = pltpu.CompilerParams(vmem_limit_bytes=VMEM_LIMIT)


    def cost(flops, size):
        return pl.CostEstimate(flops=flops, bytes_accessed=size, transcendentals=0)

    below = from_behind(spectra, "chan", -1)
    far_routes = [[(c + away, c) for c in range(1, n_chan - away)] for away in range(2, reach)]
    power, copied = pl.pallas_call(
        power_kernel,
        out_shape=[
            jax.ShapeDtypeStruct((w_dev, ch, 1), jnp.float32),
            jax.ShapeDtypeStruct(spectra.shape, spectra.dtype),
        ],
        in_specs=[VMEM], out_specs=[VMEM] * 2, compiler_params=params, cost_estimate=cost(ch, ch),
    )(spectra)
    twist = phases(F_LO + np.arange(n_bins), np.ones(1)).reshape(2, n_freq, f_dev)
    twist = jnp.asarray(np.moveaxis(twist, 0, 1))

    def swap(power):
        routes = [[(f, (f + turn) % n_freq) for f in range(n_freq)] for turn in range(1, n_freq)]
        return [lax.ppermute(power, "freq", route) for route in routes]

    def half_power(block):
        return pl.pallas_call(
            partial_kernel,
            out_shape=jax.ShapeDtypeStruct(power.shape, jnp.float32),
            in_specs=[VMEM], out_specs=VMEM, compiler_params=params, cost_estimate=cost(ch, ch),
        )(block)

    def whiten(block, others):
        return pl.pallas_call(
            functools.partial(whiten_kernel, n_bins),
            out_shape=jax.ShapeDtypeStruct(block.shape, jnp.bfloat16),
            in_specs=[VMEM] * (1 + len(others)), out_specs=VMEM, compiler_params=params,
        )(block, *others)

    def kept(block):
        return pl.pallas_call(
            keep_kernel,
            out_shape=jax.ShapeDtypeStruct((w_dev, 3) + block.shape[2:], jnp.float32),
            in_specs=[VMEM] * 2, out_specs=VMEM, compiler_params=params,
        )(keep.reshape(1, w_dev), block)

    def pairs(base, partners, by_window):
        n = len(partners)
        return pl.pallas_call(
            functools.partial(pairs_kernel, n, n_win, n_freq, by_window),
            out_shape=[jax.ShapeDtypeStruct((n, n_win, ch * ch, width), jnp.float32)] * n_freq,
            in_specs=[VMEM] * (3 + n), out_specs=[VMEM] * n_freq,
            scratch_shapes=[
                pltpu.VMEM((2, 2 * n * ch * ch, f_dev), jnp.bfloat16),
                pltpu.VMEM((2, n * ch * ch, LAGS // 2), jnp.float32),
            ],
            compiler_params=params,
            cost_estimate=cost(ch, ch),
        )(base, *partners, twist, table)

    def turns(parts, axis, size):
        received = [parts[0]]
        for turn in range(1, size):
            route = [(g, (g + turn) % size) for g in range(size)]
            received.append(lax.ppermute(parts[turn], axis, route))
        return received

    def split_windows(parts, kinds):
        n = parts[0].shape[0]
        return pl.pallas_call(
            functools.partial(add_kernel, n_freq),
            out_shape=[jax.ShapeDtypeStruct((n, ch * ch, width), kind) for kind in kinds],
            in_specs=[VMEM] * n_freq, out_specs=[VMEM] * n_win, compiler_params=params,
        )(*turns(parts, "freq", n_freq))

    white = whiten(copied, swap(power))
    far = [lax.ppermute(white, "chan", route) for route in far_routes]
    above = lax.ppermute(white, "chan", [(c - 1, c) for c in range(1, n_chan - 1)])
    half_lags = 2 * np.arange(LAGS // 2) + 1
    coarse = phases(np.arange(0, n_bins, FINE), half_lags)
    fine = phases(F_LO + np.arange(FINE), half_lags)
    white, ends = lax.optimization_barrier((white, jnp.asarray(np.concatenate([coarse, fine], axis=1))))
    table = pl.pallas_call(
        table_kernel,
        out_shape=jax.ShapeDtypeStruct((4, f_dev, LAGS // 2), jnp.bfloat16),
        in_specs=[VMEM], out_specs=VMEM, compiler_params=params, cost_estimate=cost(ch, ch),
    )(ends)
    own = kept(white)
    below = whiten(below, swap(half_power(below)))
    parts = pairs(own, [white, below], False)
    far, parts = lax.optimization_barrier((far, parts))
    above, far = lax.optimization_barrier((above, far))
    kinds = [jnp.float32] + [jnp.bfloat16] * (n_win - 1)
    remote = turns(pairs(kept(above), [below] + far, True), "freq", n_freq)
    remote, parts = lax.optimization_barrier((remote, parts))
    near = turns(split_windows(parts, kinds), "win", n_win)
    shape = (remote[0].shape[0], ch * ch, width)
    n_ships = n_win // n_freq
    shipped = pl.pallas_call(
        functools.partial(group_kernel, n_freq),
        out_shape=[jax.ShapeDtypeStruct((n_freq,) + shape, jnp.bfloat16)] * n_ships,
        in_specs=[VMEM] * n_freq, out_specs=[VMEM] * n_ships, compiler_params=params,
    )(*remote)
    arrived = []
    for ship, block in enumerate(shipped):
        route = [
            ((c * n_win + w) * n_freq + f, ((c - 1) * n_win + (w + ship * n_freq + f) % n_win) * n_freq + f)
            for c in range(1, n_chan - 1) for w in range(n_win) for f in range(n_freq)
        ]
        arrived.append(lax.ppermute(block, ("chan", "win", "freq"), route))
    arrived = pl.pallas_call(
        functools.partial(ungroup_kernel, n_ships),
        out_shape=[jax.ShapeDtypeStruct(shape, jnp.bfloat16 if n_ships == 1 else jnp.float32)] * n_freq,
        in_specs=[VMEM] * n_ships, out_specs=[VMEM] * n_freq, compiler_params=params,
    )(*arrived)
    arrived = turns(arrived, "freq", n_freq)
    scale = 1.0 / math.sqrt(w_dev * n_win * n_bins)
    factors = jnp.repeat(pair_mask.T.astype(jnp.float32) * scale, ch, axis=1)[..., None]
    return pl.pallas_call(
        functools.partial(combine_kernel, n_win, n_freq),
        out_shape=jax.ShapeDtypeStruct((ch, reach + 1, ch, width), jnp.float32),
        in_specs=[VMEM] * (1 + n_win + n_freq), out_specs=VMEM, compiler_params=params,
    )(factors, *near, *arrived)


def solution(mesh):
    in_specs = (
        P("win", None, ("fibre", "chan"), "freq"),
        P(("fibre", "win")),
        P(("fibre", "chan"), None),
    )
    out_specs = P(("fibre", "chan"), None, None, ("win", "freq"))
    return jax.shard_map(local, mesh=mesh, in_specs=in_specs, out_specs=out_specs, check_vma=False)
```
